512 devices in a mesh: face: 8 (over x_hi, y), tile: 64 (over x_lo, z, core).
Axes of the slice: x: 4 (x_hi: 2, x_lo: 2; x = x_hi * 2 + x_lo), y: 4, z: 16, core: 2. Of those that a mesh axis runs over, the one named last changes fastest.
Arguments:
- saved_input: bfloat16 [1, 32, 64, 64, 256], P(None, 'face', 'tile'), may hold values from -16 to 16
- saved_pre: bfloat16 [1, 32, 64, 64, 256], P(None, 'face', 'tile'), may hold values from -8 to 8
- cotangent: bfloat16 [1, 32, 64, 64, 256], P(None, 'face', 'tile'), may hold values from -16 to 16
- first_weight: bfloat16 [3, 3, 256, 256], replicated, may hold values from -0.125 to 0.125
- second_weight: bfloat16 [3, 3, 256, 256], replicated, may hold values from -0.125 to 0.125
- seams: int32 [32, 4], P('face'), may hold values from 0 to 31, as said below
- corners: int32 [32, 4], P('face'), may hold values from 0 to 31, as said below
Outputs:
- grad_input: bfloat16 [1, 32, 64, 64, 256], P(None, 'face', 'tile')
- grad_first: float32 [3, 3, 256, 256], P(None, None, 'tile', 'face')
The draws below stay inside these ranges and needn't reach their ends.
Inputs may be any that keep to these rules, and one draw needn't show every extreme that they name: seams[f, s] names the face glued to side s of face f (0 top, 1 right, 2 bottom, 3 left). A top side meets the bottom side of the face named there and a right side the left side, pixel for pixel in the same order along the side; the gluing holds both ways (seams[seams[f, 1], 3] = f and seams[seams[f, 0], 2] = f), and crossing a side seam then a top or bottom seam reaches the same face as the other order. corners[f, c] names the face reached from f by crossing the two seams that meet at corner c (0 top left, 1 top right, 2 bottom left, 3 bottom right).
All inputs are finite; a program needn't handle non-finite values.
Results may differ from the reference program's by a relative error of at most 0.0033.
Values may be sent and summed in bfloat16 or wider, within the bound.
No kernel may reach another device: no remote copies, remote signals or barrier semaphores. Data moves between devices by JAX's collectives and lax.ppermute only.
A program may use at most 64 MiB of HBM per device.

```python
import math
import jax
import jax.numpy as jnp
from jax import lax

C = 256
B = 1
FACES = 32
NS = 64
PIXELS = 131072


def face_grid(key):
    face_count = FACES
    grid_height = 2 if face_count % 2 == 0 and face_count >= 4 else 1
    grid_width = face_count // grid_height
    labels = jax.random.permutation(jax.random.fold_in(key, 7), face_count).astype(jnp.int32)
    position = jnp.zeros((face_count,), jnp.int32).at[labels].set(jnp.arange(face_count, dtype=jnp.int32))
    return (labels, position, grid_height, grid_width)


def neighbour(grid, step_row, step_col):
    labels, position, grid_height, grid_width = grid
    grid_row = position // grid_width
    grid_col = position % grid_width
    target = (grid_row + step_row) % grid_height * grid_width + (grid_col + step_col) % grid_width
    return labels[target]


def draw_seams(key, part):
    grid = face_grid(key)
    return jnp.stack([neighbour(grid, -1, 0), neighbour(grid, 0, 1), neighbour(grid, 1, 0), neighbour(grid, 0, -1)], axis=1).astype(jnp.int32)


def draw_corners(key, part):
    grid = face_grid(key)
    return jnp.stack([neighbour(grid, -1, -1), neighbour(grid, -1, 1), neighbour(grid, 1, -1), neighbour(grid, 1, 1)], axis=1).astype(jnp.int32)


def raised(result, stream_key, source, target, shards_of, factor):
    def block_of(axis_at):
        return (jnp.arange(result.shape[axis_at]) // (result.shape[axis_at] // shards_of)).reshape((-1,) + (1,) * (result.ndim - 1 - axis_at))

    one_side = jax.random.permutation(stream_key, shards_of)[block_of(target)]
    far = (block_of(target) + shards_of // 2) % shards_of
    return jnp.where((block_of(source) == one_side) | (block_of(source) == far), factor * result, result)


def block_levels(own_key, shape, pieces, smallest, largest):
    factor_of = 1.0
    for dim, parts in pieces:
        heights = jax.random.uniform(jax.random.fold_in(jax.random.fold_in(own_key, 6), dim), (parts,), jnp.float32, smallest / len(pieces), largest / len(pieces))
        factor_of = factor_of * jnp.repeat(jnp.exp(heights), shape[dim] // parts).reshape((-1,) + (1,) * (len(shape) - 1 - dim))
    return factor_of


def noise(own_key, dims, width, reach, cuts=(), kind=jnp.bfloat16):
    gain = block_levels(own_key, dims, cuts, -0.22, 0.18) if cuts else 1.0
    values = jax.random.normal(own_key, dims, jnp.float32) * width * gain
    return jnp.minimum(jnp.maximum(values, -reach), reach).astype(kind)


def heavy_noise(own_key, extent, width, reach, cuts, heavy, kind=jnp.bfloat16):
    entries = width * jax.random.normal(own_key, extent, jnp.float32)
    if cuts:
        entries = entries * block_levels(own_key, extent, cuts, -0.22, 0.18)
    return jnp.clip(raised(entries, jax.random.fold_in(own_key, 3), *heavy), -reach, reach).astype(kind)


def setup_inputs(seed: int = 0) -> dict:
    seeds = jax.random.split(jax.random.key(seed), 8)
    return {
        "saved_input": heavy_noise(seeds[0], (B, FACES, NS, NS, C), 1.0, 16.0, ((1, 8), (2, 64)), (2, 4, 64, 4.0)),
        "saved_pre": noise(seeds[1], (B, FACES, NS, NS, C), 1.5, 8.0, ((1, 8), (2, 64))),
        "cotangent": heavy_noise(seeds[2], (B, FACES, NS, NS, C), 1.0, 16.0, ((1, 8), (2, 64)), (2, 4, 64, 4.0)),
        "first_weight": noise(seeds[3], (3, 3, C, C), (9 * C) ** -0.5, 0.125),
        "second_weight": noise(seeds[4], (3, 3, C, C), (9 * C) ** -0.5, 0.125),
        "seams": draw_seams(jax.random.fold_in(seeds[7], 71), 0),
        "corners": draw_corners(jax.random.fold_in(seeds[7], 71), 0),
    }


exact_precision = lax.Precision.HIGHEST

def pad_face(values, seams, corners, batch, face_index):
    side_cells = values.shape[2]
    centre = values[batch, face_index]
    above_row = values[batch, seams[face_index, 0]][side_cells - 1]
    below_row = values[batch, seams[face_index, 2]][0]
    left_column = values[batch, seams[face_index, 3]][:, side_cells - 1]
    right_column = values[batch, seams[face_index, 1]][:, 0]
    top_left = values[batch, corners[face_index, 0]][side_cells - 1, side_cells - 1]
    top_right = values[batch, corners[face_index, 1]][side_cells - 1, 0]
    low_left = values[batch, corners[face_index, 2]][0, side_cells - 1]
    low_right = values[batch, corners[face_index, 3]][0, 0]
    top_line = jnp.concatenate([top_left[None], above_row, top_right[None]], 0)
    low_line = jnp.concatenate([low_left[None], below_row, low_right[None]], 0)
    middle = jnp.concatenate([left_column[:, None], centre, right_column[:, None]], 1)
    return jnp.concatenate([top_line[None], middle, low_line[None]], 0)

def correlate(padded, kernel):
    return lax.conv_general_dilated(padded[None].astype(jnp.float32), kernel.astype(jnp.float32), (1, 1), 'VALID', dimension_numbers=('NHWC', 'HWIO', 'NHWC'), precision=exact_precision)[0]

def flipped(weight):
    return jnp.transpose(weight[::-1, ::-1], (0, 1, 3, 2))

def silu_slope(pre_act):
    logistic = jax.nn.sigmoid(pre_act)
    return logistic * (1.0 + pre_act * (1.0 - logistic))

def reference(saved_input, saved_pre, cotangent, first_weight, second_weight, seams, corners):
    face_count = saved_input.shape[1]
    side_cells = saved_input.shape[2]
    channels = saved_input.shape[4]
    pair_count = saved_input.shape[0] * face_count
    back_one = flipped(first_weight)
    back_two = flipped(second_weight)

    def first_pass(pair_index):
        batch = pair_index // face_count
        face_index = pair_index % face_count
        padded = pad_face(cotangent, seams, corners, batch, face_index)
        grad_hidden = correlate(padded, back_two)
        pre_act = saved_pre[batch, face_index].astype(jnp.float32)
        return (grad_hidden * silu_slope(pre_act)).astype(jnp.bfloat16)
    grad_pre = lax.map(first_pass, jnp.arange(pair_count, dtype=jnp.int32)).reshape(saved_input.shape)

    def second_pass(totals, pair_index):
        batch = pair_index // face_count
        face_index = pair_index % face_count
        padded_grad = pad_face(grad_pre, seams, corners, batch, face_index)
        grad_face = (cotangent[batch, face_index].astype(jnp.float32) + correlate(padded_grad, back_one)).astype(jnp.bfloat16)
        padded_input = pad_face(saved_input, seams, corners, batch, face_index).astype(jnp.float32)
        own_grad = grad_pre[batch, face_index].astype(jnp.float32).reshape(-1, channels)
        first_terms = []
        for tap_row in range(3):
            for tap_col in range(3):
                window_in = padded_input[tap_row:tap_row + side_cells, tap_col:tap_col + side_cells].reshape(-1, channels)
                first_terms.append(jnp.dot(window_in.T, own_grad, precision=exact_precision))
        first_total = totals + jnp.stack(first_terms, 0).reshape(3, 3, channels, channels)
        return (first_total, grad_face)
    zeros = jnp.zeros((3, 3, channels, channels), jnp.float32)
    totals, grad_faces = lax.scan(second_pass, zeros, jnp.arange(pair_count, dtype=jnp.int32))
    grad_input = grad_faces.reshape(saved_input.shape)
    scale_factor = 1.0 / math.sqrt(PIXELS)
    return (grad_input, totals * scale_factor)
```

```python
import functools
import math

import jax
import jax.numpy as jnp
import numpy as np
from jax import lax
from jax.experimental import pallas as pl
from jax.experimental.pallas import tpu as pltpu
from jax.sharding import Mesh
from jax.sharding import PartitionSpec as P

FACE = ("xh", "y")
TILE = ("xl", "z", "c")
CHIP = ("xl", "z")
GAP = 16
SIDE = 32
SEAM_AT = 26
VMEM = 40 * 2**20


def params():
    return pltpu.CompilerParams(vmem_limit_bytes=VMEM)


def whole(n):
    return [pl.BlockSpec(memory_space=pltpu.VMEM)] * n


SMEM = pl.BlockSpec(memory_space=pltpu.SMEM)


def pick_kernel(faces, want_ref, table_ref, out_ref):
    for i in range(faces):
        out_ref[i] = table_ref[want_ref[i]]


def one_hot(index, width):
    rows = index.shape[0]
    return jnp.where(lax.broadcasted_iota(jnp.int32, (rows, width), 1) == index, 1.0, 0.0).astype(jnp.bfloat16)


def grad_pre_kernel(
    local, side, blocks, flags_ref, index_ref, place_ref, table_ref, gfar_ref, near_ref, own_ref, part_ref,
    gb_ref, wrap_ref, weight_ref, out_ref, g_pad, p_pad, tails,
):
    pitch = side + 2 * GAP
    row = local * pitch
    px_blocks, ch_blocks = blocks
    px, ch = side // px_blocks, out_ref.shape[-1] // ch_blocks
    core, wrap_a, wrap_b = flags_ref[0], flags_ref[1], flags_ref[2]
    cells = jnp.dot(one_hot(index_ref[...], table_ref.shape[0]), table_ref[...], preferred_element_type=jnp.float32)
    cells = cells.astype(jnp.bfloat16)
    tails[...] = jnp.dot(
        one_hot(place_ref[...], cells.shape[0]), cells, preferred_element_type=jnp.float32
    ).astype(jnp.bfloat16)

    def put(pad, slot, source, face, tail_at):
        at = pl.multiple_of(slot * row + face * pitch, 16)
        pad[pl.ds(at + GAP, side), :] = source[face]
        tail = pl.multiple_of((tail_at + slot * local + face) * 2 * GAP, 16)
        pad[pl.ds(at, GAP), :] = tails[pl.ds(tail, GAP), :]
        pad[pl.ds(at + GAP + side, GAP), :] = tails[pl.ds(tail + GAP, GAP), :]

    def put_wrap(pad, slot, which, face):
        at = pl.multiple_of(slot * row + face * pitch + GAP, 16)
        for b in range(px_blocks * ch_blocks):
            i, j = divmod(b, ch_blocks)
            pad[pl.ds(at + i * px, px), j * ch : (j + 1) * ch] = wrap_ref[b, face, which]

    g_sources = (gfar_ref, near_ref.at[0], own_ref.at[0], part_ref.at[0], gb_ref)
    p_sources = (near_ref.at[1], own_ref.at[1], part_ref.at[1])
    slot_of = lambda role, last: jnp.where(core == 0, role, last - role)
    for face in range(local):
        for role, source in enumerate(g_sources):
            put(g_pad, slot_of(role, 4), source, face, 0)
        for role, source in enumerate(p_sources):
            put(p_pad, slot_of(role, 2), source, face, 5 * local)

    @pl.when(wrap_a == 1)
    def _():
        for face in range(local):
            put_wrap(g_pad, slot_of(0, 4), 0, face)
            put_wrap(g_pad, slot_of(1, 4), 1, face)
            put_wrap(p_pad, slot_of(0, 2), 2, face)

    @pl.when(wrap_b == 1)
    def _():
        for face in range(local):
            put_wrap(g_pad, slot_of(4, 4), 0, face)

    for slot in range(3):
        grad = conv_rows(g_pad, slot * row, row, weight_ref)
        pre = p_pad[slot * row : (slot + 1) * row, :].astype(jnp.float32)
        logistic = jax.nn.sigmoid(pre)
        slope = logistic * (1.0 + pre * (1.0 - logistic))
        out_ref[slot * row : (slot + 1) * row, :] = (grad * slope).astype(jnp.bfloat16)


def conv_rows(pad, start, row, weight_ref):
    sums = []
    for c in range(3):
        total = None
        for r in range(3):
            rows = pad[start + (2 - r) * row : start + (3 - r) * row, :]
            term = lax.dot_general(
                rows, weight_ref[r, c], (((1,), (1,)), ((), ())), preferred_element_type=jnp.float32
            )
            total = term if total is None else total + term
        sums.append(total)
    return pltpu.roll(sums[2], 1, 0) + sums[1] + pltpu.roll(sums[0], row - 1, 0)


def grad_input_kernel(local, side, pre_ref, own_ref, weight_ref, out_ref):
    pitch = side + 2 * GAP
    grad = conv_rows(pre_ref, 0, local * pitch, weight_ref)
    for face in range(local):
        at = face * pitch + GAP
        own = own_ref[face].astype(jnp.float32)
        out_ref[face] = (own + grad[at : at + side, :]).astype(jnp.bfloat16)


def grad_first_kernel(row, flags_ref, x_ref, pre_ref, swapped_ref, out_ref, rows4):
    core = flags_ref[0]
    rows4[pl.ds(pl.multiple_of(core * row, 16), 3 * row), :] = pre_ref[...]
    rows4[pl.ds(pl.multiple_of((1 - core) * 3 * row, 16), row), :] = swapped_ref[...]
    dests, _, width, half = out_ref.shape
    for r in range(3):
        lines = rows4[(2 - r) * row : (4 - r) * row, :]
        terms = jnp.dot(x_ref[...], lines, preferred_element_type=jnp.float32)
        for c in range(3):
            turned = terms[c * half : (c + 1) * half, :].T.astype(jnp.bfloat16)
            for d in range(dests):
                out_ref[d, 3 * r + c] = turned[d * width : (d + 1) * width, :]


def on_device(sizes, saved_input, saved_pre, cotangent, first_weight, second_weight, seams, corners):
    nxh, ny, nxl, nz, nc = sizes
    nface, ntile, nchip = nxh * ny, nxl * nz * nc, nxl * nz
    x, p, g = saved_input[0, :, 0], saved_pre[0, :, 0], cotangent[0, :, 0]
    local, side, channels = x.shape
    faces = nface * local
    pitch = side + 2 * GAP
    row = local * pitch
    bf = jnp.bfloat16
    core = lax.axis_index("c")
    chip = lax.axis_index(CHIP)

    t_all = range(ntile)
    out = lambda t: t + 1 if t % 2 else t - 1
    far = lambda t: t + 2 if t % 2 else t - 2
    back = lambda t: t - 2 if t % 2 else t + 2
    pairs = lambda source: [(source(t) % ntile, t) for t in t_all]
    gp = jnp.stack([g, p], 0)
    part = lax.ppermute(jnp.stack([g, p, x], 0), "c", [(0, 1), (1, 0)])
    near = lax.ppermute(gp, TILE, pairs(out))
    gfar = lax.ppermute(g, TILE, pairs(far))
    gb = lax.ppermute(g, TILE, pairs(back))

    top = chip < nchip // 2
    wrap_a = jnp.where(core == 0, chip == 0, chip == nchip - 1)
    wrap_b = jnp.where(core == 0, chip == nchip - 1, chip == 0)
    flags = jnp.stack([core, wrap_a.astype(jnp.int32), wrap_b.astype(jnp.int32)])

    ends = lambda a: [a[:, 0:2], a[:, side - 2 : side]]
    tips = lambda a: [a[:, 0:1], a[:, side - 1 : side]]
    seam_cell = jnp.pad(seams.astype(bf)[:, None, :], ((0, 0), (0, SIDE - SEAM_AT - 1), (0, channels - 4)))
    cells = jnp.concatenate(
        [*ends(gfar), *ends(near[0]), *ends(g), *ends(part[0]), *ends(gb), *tips(near[1]), *tips(p), *tips(part[1]), seam_cell],
        1,
    )
    px_blocks = 4
    ch_blocks = nface // px_blocks
    px, ch = side // px_blocks, channels // ch_blocks
    holds_a = (core == 0) == top
    rows3 = jnp.where(holds_a, jnp.stack([gfar, near[0], near[1]], 0), gb[None])
    pieces = jnp.transpose(
        rows3.reshape(3, local, px_blocks, px, ch_blocks, ch), (2, 4, 1, 0, 3, 5)
    )
    halves = pieces.reshape(nface, local, ch_blocks, 3 * px // ch_blocks, ch)
    pieces = jnp.concatenate([halves[:, :, i] for i in range(ch_blocks)], -1)
    sent = jnp.concatenate([jnp.broadcast_to(cells[None], (nface,) + cells.shape), pieces], 2)
    table = lax.all_to_all(sent, FACE, 0, 0, tiled=True).reshape(faces, -1, channels)

    all_seams = table[:, SEAM_AT, :4].astype(jnp.int32)
    want = jnp.where(top, all_seams[:, 0], all_seams[:, 2])
    count = table.shape[1] - SIDE
    picked = pl.pallas_call(
        functools.partial(pick_kernel, faces),
        out_shape=jax.ShapeDtypeStruct((faces, count, channels), bf),
        in_specs=[SMEM, *whole(1)],
        out_specs=whole(1)[0],
        compiler_params=params(),
        name="pick",
    )(want, table[:, SIDE:])
    wrapped = lax.all_to_all(picked.reshape(nface, local, count, channels), FACE, 0, 0, tiled=True)
    wrapped = jnp.concatenate(
        [wrapped[..., i * ch : (i + 1) * ch] for i in range(ch_blocks)], 2
    ).reshape(nface, local, 3, px, ch)

    first = jnp.where(top, 0, 2)
    turn = lambda n: jnp.where(core == 0, np.arange(n), n - 1 - np.arange(n))
    inner = jnp.stack([seams[:, 3], seams[:, 1]], 1)
    outer = lax.dynamic_slice_in_dim(corners, first, 2, 1)
    beyond = lambda flag: jnp.where(flag, outer, inner)
    by_role = jnp.stack([beyond(wrap_a), beyond(wrap_a), inner, inner, beyond(wrap_b)], 0)
    g_role, p_role = turn(5), turn(3)
    g_face = jnp.where(core == 0, by_role, by_role[::-1])
    p_by_role = by_role[1:4]
    p_face = jnp.where(core == 0, p_by_role, p_by_role[::-1])
    g_index = (
        g_face[..., None] * SIDE + g_role[:, None, None, None] * 4 + np.array([[2, 3], [0, 1]], np.int32)
    ).reshape(-1)
    p_index = (
        p_face * SIDE + 20 + p_role[:, None, None] * 2 + np.array([1, 0], np.int32)
    ).reshape(-1)
    cells_held = 128
    index = jnp.concatenate([g_index, p_index])
    index = jnp.pad(index, (0, cells_held - index.shape[0]))[:, None].astype(jnp.int32)
    place = np.full((8 * local, 2, GAP), -1, np.int32)
    for i in range(5 * local):
        place[i, 0, GAP - 2 :] = (4 * i, 4 * i + 1)
        place[i, 1, :2] = (4 * i + 2, 4 * i + 3)
    for i in range(3 * local):
        at = 20 * local + 2 * i
        place[5 * local + i, 0, GAP - 1] = at
        place[5 * local + i, 1, 0] = at + 1
    place = jnp.asarray(place.reshape(-1, 1))

    grad_pre = pl.pallas_call(
        functools.partial(grad_pre_kernel, local, side, (px_blocks, ch_blocks)),
        out_shape=jax.ShapeDtypeStruct((3 * row, channels), bf),
        in_specs=[SMEM, *whole(10)],
        out_specs=whole(1)[0],
        scratch_shapes=[
            pltpu.VMEM((5 * row, channels), bf),
            pltpu.VMEM((3 * row, channels), bf),
            pltpu.VMEM((8 * local * 2 * GAP, channels), bf),
        ],
        compiler_params=params(),
        cost_estimate=pl.CostEstimate(flops=2 * 27 * row * channels**2, bytes_accessed=4 * 2**20, transcendentals=3 * row * channels),
        name="grad_pre",
    )(flags, index, place, table[:, :SIDE].reshape(faces * SIDE, channels), gfar, near, gp, part, gb, wrapped, second_weight)

    lacking = jnp.where(core == 0, grad_pre[:row], grad_pre[2 * row :])
    swapped = lax.ppermute(lacking, "c", [(0, 1), (1, 0)])

    grad_input = pl.pallas_call(
        functools.partial(grad_input_kernel, local, side),
        out_shape=jax.ShapeDtypeStruct((local, side, channels), bf),
        in_specs=whole(3),
        out_specs=whole(1)[0],
        compiler_params=params(),
        cost_estimate=pl.CostEstimate(flops=2 * 9 * row * channels**2, bytes_accessed=2 * 2**20, transcendentals=0),
        name="grad_input",
    )(grad_pre, g, first_weight)

    half = channels // nc
    per_tile = channels // ntile
    both = jnp.where(core == 0, jnp.stack([x, part[2]], 0), jnp.stack([part[2], x], 0))
    shifted = jnp.stack(
        [jnp.pad(both, ((0, 0), (0, 0), (GAP + 1 - c, GAP - 1 + c), (0, 0))) for c in range(3)], 0
    ).reshape(3, 2 * row, channels)
    kept = np.arange(half)
    chosen = (kept // per_tile) * (nc * per_tile) + kept % per_tile
    choose = (chosen[:, None] + core * per_tile == np.arange(channels)[None, :]).astype(bf)
    x_turned = lax.dot_general(
        choose, shifted, (((1,), (2,)), ((), ())), preferred_element_type=jnp.float32
    ).astype(bf)
    x_turned = jnp.transpose(x_turned, (1, 0, 2)).reshape(3 * half, 2 * row)

    width = channels // nface
    parts = pl.pallas_call(
        functools.partial(grad_first_kernel, row),
        out_shape=jax.ShapeDtypeStruct((nface, 9, width, half), bf),
        in_specs=[SMEM, *whole(3)],
        out_specs=whole(1)[0],
        scratch_shapes=[pltpu.VMEM((4 * row, channels), bf)],
        compiler_params=params(),
        cost_estimate=pl.CostEstimate(flops=2 * 9 * half * 2 * row * channels, bytes_accessed=2**20, transcendentals=0),
        name="grad_first",
    )(flags, x_turned, grad_pre, swapped)
    scale_factor = 1.0 / math.sqrt(faces * ntile * side)
    got = lax.all_to_all(parts, FACE, 0, 0, tiled=True)
    total = jnp.sum(got.astype(jnp.float32), 0) * scale_factor
    total = jnp.transpose(total.reshape(9 * width, half)).reshape(nchip, per_tile, 9 * width)
    got = lax.all_to_all(total, CHIP, 0, 0, tiled=True)
    total = jnp.sum(got, 0).reshape(per_tile, 9, width)
    first_out = jnp.transpose(total, (1, 0, 2)).reshape(3, 3, per_tile, width)
    return grad_input.reshape(saved_input.shape), first_out


def solution(mesh, sizes=(2, 4, 2, 16, 2)):
    fine = Mesh(mesh.devices.reshape(sizes), FACE + TILE)
    field = P(None, FACE, TILE, None, None)
    return jax.shard_map(
        functools.partial(on_device, sizes),
        mesh=fine,
        in_specs=(field, field, field, P(), P(), P(FACE, None), P(FACE, None)),
        out_specs=(field, P(None, None, TILE, FACE)),
        check_vma=False,
    )
```

```python
import functools
import math

import jax
import jax.numpy as jnp
import numpy as np
from jax import lax
from jax.experimental import pallas as pl
from jax.experimental.pallas import tpu as pltpu
from jax.sharding import Mesh
from jax.sharding import PartitionSpec as P

FACE = ("xh", "y")
TILE = ("xl", "z", "c")
CHIP = ("xl", "z")
GAP = 16
CELLS = 8
SEAM_AT = 6
VMEM = 40 * 2**20


def whole(n):
    return [pl.BlockSpec(memory_space=pltpu.VMEM)] * n


def pick_kernel(faces, count, want_ref, table_ref, out_ref):
    for i in range(faces):
        out_ref[i] = table_ref[want_ref[i], :count]


def border_kernel(local, side, index_ref, cells_ref, g_ref, p_ref, own_ref, wrap_ref):
    rows, width = index_ref.shape[0], cells_ref.shape[0]
    where = lax.broadcasted_iota(jnp.int32, (rows, width), 1) == index_ref[...]
    tails = jnp.dot(
        jnp.where(where, 1.0, 0.0).astype(jnp.bfloat16), cells_ref[...], preferred_element_type=jnp.float32
    ).astype(jnp.bfloat16)
    for which, source in enumerate((g_ref, p_ref)):
        for face in range(local):
            at = (which * local + face) * GAP
            own_ref[which, face, :side] = source[face]
            own_ref[which, face, side:] = tails[at : at + GAP]
            at += 2 * local * GAP
            wrap_ref[which, face] = tails[at : at + GAP]


def send_kernel(local, side, blocks, flags_ref, own_ref, tails_ref, pieces_ref, near_ref, far_ref):
    px_blocks, ch_blocks = blocks
    px = side // px_blocks
    channels = own_ref.shape[-1]
    ch = channels // ch_blocks
    near, far = flags_ref[1], flags_ref[2]

    def put_wrap(out, which, face):
        for b in range(px_blocks * ch_blocks):
            i, j = divmod(b, ch_blocks)
            piece = pieces_ref[b, face]
            if ch_blocks == 1:
                part = piece[which * px : (which + 1) * px]
            else:
                part = piece[:, which * ch : (which + 1) * ch]
            out[i * px : (i + 1) * px, j * ch : (j + 1) * ch] = part
        out[side:, :] = tails_ref[which, face]

    @pl.when(near == 1)
    def _():
        for face in range(local):
            put_wrap(near_ref.at[0, face], 0, face)
            put_wrap(near_ref.at[1, face], 1, face)

    @pl.when(near == 0)
    def _():
        near_ref[...] = own_ref[...]

    @pl.when(far == 1)
    def _():
        for face in range(local):
            put_wrap(far_ref.at[face], 0, face)

    @pl.when(far == 0)
    def _():
        far_ref[...] = own_ref[0]


def grad_pre_kernel(local, side, flags_ref, own_ref, part_ref, near_ref, far_ref, weight_ref, out_ref, g_pad, p_pad):
    pitch = side + 2 * GAP
    row = local * pitch
    core = flags_ref[0]

    def put(pad, slot, source, face):
        at = pl.multiple_of(slot * row + face * pitch, 16)
        border = source[face, side:]
        pad[pl.ds(at, GAP), :] = border
        pad[pl.ds(at + GAP, side), :] = source[face, :side]
        pad[pl.ds(at + GAP + side, GAP), :] = border

    for face in range(local):
        for role, source in enumerate((far_ref, near_ref.at[0], own_ref.at[0], part_ref)):
            put(g_pad, jnp.where(core == 0, role, 3 - role), source, face)
        for role, source in enumerate((near_ref.at[1], own_ref.at[1])):
            put(p_pad, jnp.where(core == 0, role, 1 - role), source, face)
    for slot in range(2):
        grad = conv_rows(g_pad, slot * row, row, weight_ref)
        pre = p_pad[slot * row : (slot + 1) * row, :].astype(jnp.float32)
        logistic = jax.nn.sigmoid(pre)
        slope = logistic * (1.0 + pre * (1.0 - logistic))
        out_ref[slot * row : (slot + 1) * row, :] = (grad * slope).astype(jnp.bfloat16)


def conv_rows(pad, start, row, weight_ref):
    sums = []
    for c in range(3):
        total = None
        for r in range(3):
            at = start + (2 - r) * row
            rows = pad[pl.ds(at if isinstance(at, int) else pl.multiple_of(at, 16), row), :]
            term = lax.dot_general(
                rows, weight_ref[r, c], (((1,), (1,)), ((), ())), preferred_element_type=jnp.float32
            )
            total = term if total is None else total + term
        sums.append(total)
    return pltpu.roll(sums[2], 1, 0) + sums[1] + pltpu.roll(sums[0], row - 1, 0)


def four_rows(rows4, core, row, pre_ref, swapped_ref):
    rows4[pl.ds(pl.multiple_of(core * 2 * row, 16), 2 * row), :] = pre_ref[...]
    rows4[pl.ds(pl.multiple_of((1 - core) * 2 * row, 16), 2 * row), :] = swapped_ref[...]


def grad_input_kernel(local, side, flags_ref, pre_ref, swapped_ref, own_ref, weight_ref, out_ref, rows4):
    pitch = side + 2 * GAP
    row = local * pitch
    core = flags_ref[0]
    four_rows(rows4, core, row, pre_ref, swapped_ref)
    grad = conv_rows(rows4, core * row, row, weight_ref)
    for face in range(local):
        at = face * pitch + GAP
        own = own_ref[face].astype(jnp.float32)
        out_ref[face] = (own + grad[at : at + side, :]).astype(jnp.bfloat16)


def grad_first_kernel(row, nxl, flags_ref, x_ref, pre_ref, swapped_ref, out_ref, rows4):
    four_rows(rows4, flags_ref[0], row, pre_ref, swapped_ref)
    dests, _, lines, half = out_ref.shape
    for r in range(3):
        terms = jnp.dot(x_ref[...], rows4[(2 - r) * row : (4 - r) * row, :], preferred_element_type=jnp.float32)
        for c in range(3):
            turned = terms[c * half : (c + 1) * half, :].T
            if nxl == 1:
                for d in range(dests):
                    out_ref[d, 3 * r + c] = turned[d * lines : (d + 1) * lines, :].astype(jnp.bfloat16)
                continue
            split = turned.reshape(dests // 2, 2, lines, half)
            left = split[:, 0].reshape(-1, half)
            right = split[:, 1].reshape(-1, half)
            low = lax.broadcasted_iota(jnp.int32, left.shape, 1) < half // 2
            ones = (
                jnp.where(low, left, pltpu.roll(right, half // 2, 1)),
                jnp.where(low, pltpu.roll(left, half // 2, 1), right),
            )
            for xl, one in enumerate(ones):
                for d in range(dests // 2):
                    out_ref[2 * d + xl, 3 * r + c] = one[d * lines : (d + 1) * lines, :].astype(jnp.bfloat16)


def kernel(body, out_shape, inputs, smem=0, scratch=(), name=None, flops=0, nbytes=2**20, exps=0):
    many = isinstance(out_shape, tuple)
    return pl.pallas_call(
        body,
        out_shape=out_shape,
        in_specs=[pl.BlockSpec(memory_space=pltpu.SMEM)] * smem + whole(len(inputs) - smem),
        out_specs=tuple(whole(len(out_shape))) if many else whole(1)[0],
        scratch_shapes=scratch,
        compiler_params=pltpu.CompilerParams(vmem_limit_bytes=VMEM),
        cost_estimate=pl.CostEstimate(flops=flops, bytes_accessed=nbytes, transcendentals=exps),
        name=name,
    )(*inputs)


def on_device(sizes, saved_input, saved_pre, cotangent, first_weight, second_weight, seams, corners):
    nxh, ny, nxl, nz, nc = sizes
    nface, ntile, nchip = nxh * ny, nxl * nz * nc, nxl * nz
    x, p, g = saved_input[0, :, 0], saved_pre[0, :, 0], cotangent[0, :, 0]
    local, side, channels = x.shape
    faces = nface * local
    row = local * (side + 2 * GAP)
    bf = jnp.bfloat16
    shape = jax.ShapeDtypeStruct
    core = lax.axis_index("c")
    tile = lax.axis_index(TILE)
    top = tile >= ntile // 2
    near_wraps = (tile == 0) | (tile == ntile - 1)
    far_wraps = (tile == 1) | (tile == ntile - 2)
    flags = jnp.stack([core, near_wraps.astype(jnp.int32), far_wraps.astype(jnp.int32)])

    px_blocks = 4
    ch_blocks = nface // px_blocks
    px, ch = side // px_blocks, channels // ch_blocks
    cut = lambda a: jnp.transpose(a.reshape(local, px_blocks, px, ch_blocks, ch), (1, 3, 0, 2, 4)).reshape(
        nface, local, px, ch
    )
    pieces = jnp.concatenate([cut(g), cut(p)], 3 if ch_blocks > 1 else 2)
    count = pieces.shape[2]
    seam_cell = jnp.pad(seams.astype(bf)[:, None, :], ((0, 0), (0, 1), (0, channels - 4)))
    cells = jnp.concatenate([g[:, :2], g[:, side - 2 :], p[:, :1], p[:, side - 1 :], seam_cell], 1)
    sent = jnp.concatenate([pieces, jnp.broadcast_to(cells[None], (nface,) + cells.shape)], 2)
    table = lax.all_to_all(sent, FACE, 0, 0, tiled=True).reshape(faces, count + CELLS, channels)

    cells = table[:, count:]
    all_seams = cells[:, SEAM_AT, :4].astype(jnp.int32)
    want = jnp.where(top, all_seams[:, 0], all_seams[:, 2])
    picked = kernel(
        functools.partial(pick_kernel, faces, count), shape((faces, count, channels), bf), (want, table), 1, name="pick"
    )
    wrapped = lax.all_to_all(picked.reshape(nface, local, count, channels), FACE, 0, 0, tiled=True)

    outer = jnp.where(top, corners[:, 0:2], corners[:, 2:4])
    sides = jnp.stack([jnp.stack([seams[:, 3], seams[:, 1]], 1), outer], 0)
    spots = np.full((2, GAP), -1, np.int32)
    spots[0, [0, 1, GAP - 2, GAP - 1]] = (0, 1, 2, 3)
    spots[1, [0, GAP - 1]] = (4, 5)
    on_left = np.arange(GAP) >= GAP // 2
    face_at = jnp.where(on_left, sides[:, None, :, 0:1], sides[:, None, :, 1:2])
    index = jnp.where(spots[None, :, None] >= 0, face_at * CELLS + spots[None, :, None], -1)
    index = index.reshape(-1, 1).astype(jnp.int32)
    own, tails = kernel(
        functools.partial(border_kernel, local, side),
        (shape((2, local, side + GAP, channels), bf), shape((2, local, GAP, channels), bf)),
        (index, cells.reshape(faces * CELLS, channels), g, p),
        name="border",
    )
    near, far = kernel(
        functools.partial(send_kernel, local, side, (px_blocks, ch_blocks)),
        (shape(own.shape, bf), shape(own.shape[1:], bf)),
        (flags, own, tails, wrapped),
        1,
        name="send",
    )

    pairs = lambda step: [((t + step if t % 2 else t - step) % ntile, t) for t in range(ntile)]
    swap = lambda a: lax.ppermute(a, "c", [(0, 1), (1, 0)])
    part = swap(own[0])
    near = lax.ppermute(near, TILE, pairs(1))
    far = lax.ppermute(far, TILE, pairs(2))
    grad_pre = kernel(
        functools.partial(grad_pre_kernel, local, side),
        shape((2 * row, channels), bf),
        (flags, own, part, near, far, second_weight),
        1,
        (pltpu.VMEM((4 * row, channels), bf), pltpu.VMEM((2 * row, channels), bf)),
        "grad_pre",
        2 * 18 * row * channels**2,
        4 * 2**20,
        2 * row * channels,
    )
    swapped = swap(grad_pre)

    half = channels // nc
    per_tile = channels // ntile
    other = swap(x)
    both = jnp.where(core == 0, jnp.stack([x, other], 0), jnp.stack([other, x], 0))
    shifted = jnp.stack(
        [jnp.pad(both, ((0, 0), (0, 0), (GAP + 1 - c, GAP - 1 + c), (0, 0))) for c in range(3)], 0
    ).reshape(3, 2 * row, channels)
    kept = np.arange(half)
    chosen = (kept // per_tile) * (nc * per_tile) + kept % per_tile
    choose = (chosen[:, None] + core * per_tile == np.arange(channels)[None, :]).astype(bf)
    x_turned = lax.dot_general(
        choose, shifted, (((1,), (2,)), ((), ())), preferred_element_type=jnp.float32
    ).astype(bf)
    x_turned = jnp.transpose(x_turned, (1, 0, 2)).reshape(3 * half, 2 * row)

    rows4 = (pltpu.VMEM((4 * row, channels), bf),)
    width = channels // nface
    lines = width // nxl
    parts = kernel(
        functools.partial(grad_first_kernel, row, nxl),
        shape((nface * nxl, 9, lines, half), bf),
        (flags, x_turned, grad_pre, swapped),
        1,
        rows4,
        "grad_first",
        2 * 18 * half * row * channels,
    )
    grad_input = kernel(
        functools.partial(grad_input_kernel, local, side),
        shape((local, side, channels), bf),
        (flags, grad_pre, swapped, g, first_weight),
        1,
        rows4,
        "grad_input",
        2 * 9 * row * channels**2,
        2 * 2**20,
    )
    scale_factor = 1.0 / math.sqrt(faces * ntile * side)
    got = lax.all_to_all(parts, FACE + ("xl",), 0, 0, tiled=True)
    total = jnp.sum(got.astype(jnp.float32), 0) * scale_factor
    total = jnp.transpose(total.reshape(9 * lines, half)).reshape(nxl, nz, per_tile, 9 * lines)
    total = jnp.transpose(total, (1, 0, 2, 3)).reshape(nz, nxl * per_tile, 9 * lines)
    got = lax.all_to_all(total, "z", 0, 0, tiled=True)
    total = jnp.sum(got, 0).reshape(nxl, per_tile, 9, lines)
    first_out = jnp.transpose(total, (2, 1, 0, 3)).reshape(3, 3, per_tile, width)
    return grad_input.reshape(saved_input.shape), first_out


def solution(mesh, sizes=(2, 4, 2, 16, 2)):
    fine = Mesh(mesh.devices.reshape(sizes), FACE + TILE)
    field = P(None, FACE, TILE, None, None)
    return jax.shard_map(
        functools.partial(on_device, sizes),
        mesh=fine,
        in_specs=(field, field, field, P(), P(), P(FACE, None), P(FACE, None)),
        out_specs=(field, P(None, None, TILE, FACE)),
        check_vma=False,
    )
```

```python
import functools
import math

import jax
import jax.numpy as jnp
import numpy as np
from jax import lax
from jax.experimental import pallas as pl
from jax.experimental.pallas import tpu as pltpu
from jax.sharding import Mesh
from jax.sharding import PartitionSpec as P

FACE = ("xh", "y")
TILE = ("xl", "z", "c")
CHIP = ("xl", "z")
GAP = 16
CELLS = 8
SEAM_AT = 6
VMEM = 40 * 2**20


def whole(n):
    return [pl.BlockSpec(memory_space=pltpu.VMEM)] * n


def pack_kernel(local, side, blocks, seams_ref, g_ref, p_ref, out_ref):
    px_blocks, ch_blocks = blocks
    channels = g_ref.shape[-1]
    px, ch = side // px_blocks, channels // ch_blocks
    count = px * 2 // ch_blocks
    shape = (local * CELLS, local * side)
    line = lax.broadcasted_iota(jnp.int32, shape, 0)
    pixel = lax.broadcasted_iota(jnp.int32, shape, 1)
    cell, base = line % CELLS, line // CELLS * side
    of_g = jnp.where(cell < 2, base + cell, jnp.where(cell < 4, base + side - 4 + cell, -1))
    of_p = jnp.where(cell == 4, base, jnp.where(cell == 5, base + side - 1, -1))
    take = lambda at, ref: jnp.dot(
        jnp.where(at == pixel, 1.0, 0.0).astype(jnp.bfloat16),
        ref[...].reshape(local * side, channels),
        preferred_element_type=jnp.float32,
    )
    cells = take(of_g, g_ref) + take(of_p, p_ref)
    line = lax.broadcasted_iota(jnp.int32, cells.shape, 0)
    lane = lax.broadcasted_iota(jnp.int32, cells.shape, 1)
    for face in range(local):
        for i in range(4):
            here = (line == face * CELLS + SEAM_AT) & (lane == i)
            cells = jnp.where(here, seams_ref[face, i].astype(jnp.float32), cells)
    cells = cells.astype(jnp.bfloat16)
    for b in range(px_blocks * ch_blocks):
        i, j = divmod(b, ch_blocks)
        for face in range(local):
            at = face * count
            for which, source in enumerate((g_ref, p_ref)):
                piece = source[face, i * px : (i + 1) * px, j * ch : (j + 1) * ch]
                if ch_blocks == 1:
                    out_ref[b, at + which * px : at + (which + 1) * px] = piece
                else:
                    out_ref[b, at : at + px, which * ch : (which + 1) * ch] = piece
        out_ref[b, local * count :] = cells


def pick_kernel(faces, local, count, want_ref, table_ref, out_ref):
    for i in range(faces):
        face = want_ref[i]
        at = pl.multiple_of(lax.rem(face, local) * count, 16)
        out_ref[i] = table_ref[lax.div(face, local), pl.ds(at, count)]


def border_kernel(local, side, index_ref, cells_ref, g_ref, p_ref, own_ref, wrap_ref):
    rows, width = index_ref.shape[0], cells_ref.shape[0]
    where = lax.broadcasted_iota(jnp.int32, (rows, width), 1) == index_ref[...]
    tails = jnp.dot(
        jnp.where(where, 1.0, 0.0).astype(jnp.bfloat16), cells_ref[...], preferred_element_type=jnp.float32
    ).astype(jnp.bfloat16)
    for which, source in enumerate((g_ref, p_ref)):
        for face in range(local):
            at = (which * local + face) * GAP
            own_ref[which, face, :side] = source[face]
            own_ref[which, face, side:] = tails[at : at + GAP]
            at += 2 * local * GAP
            wrap_ref[which, face] = tails[at : at + GAP]


def send_kernel(local, side, blocks, flags_ref, own_ref, tails_ref, pieces_ref, near_ref, far_ref):
    px_blocks, ch_blocks = blocks
    px = side // px_blocks
    channels = own_ref.shape[-1]
    ch = channels // ch_blocks
    near, far = flags_ref[1], flags_ref[2]

    def put_wrap(out, which, face):
        for b in range(px_blocks * ch_blocks):
            i, j = divmod(b, ch_blocks)
            piece = pieces_ref[b, face]
            if ch_blocks == 1:
                part = piece[which * px : (which + 1) * px]
            else:
                part = piece[:, which * ch : (which + 1) * ch]
            out[i * px : (i + 1) * px, j * ch : (j + 1) * ch] = part
        out[side:, :] = tails_ref[which, face]

    @pl.when(near == 1)
    def _():
        for face in range(local):
            put_wrap(near_ref.at[0, face], 0, face)
            put_wrap(near_ref.at[1, face], 1, face)

    @pl.when(near == 0)
    def _():
        near_ref[...] = own_ref[...]

    @pl.when(far == 1)
    def _():
        for face in range(local):
            put_wrap(far_ref.at[face], 0, face)

    @pl.when(far == 0)
    def _():
        far_ref[...] = own_ref[0]


def grad_pre_kernel(local, side, flags_ref, own_ref, part_ref, near_ref, far_ref, weight_ref, out_ref, g_pad, p_pad):
    pitch = side + 2 * GAP
    row = local * pitch
    core = flags_ref[0]

    def put(pad, slot, source, face):
        at = pl.multiple_of(slot * row + face * pitch, 16)
        border = source[face, side:]
        pad[pl.ds(at, GAP), :] = border
        pad[pl.ds(at + GAP, side), :] = source[face, :side]
        pad[pl.ds(at + GAP + side, GAP), :] = border

    for face in range(local):
        for role, source in enumerate((far_ref, near_ref.at[0], own_ref.at[0], part_ref)):
            put(g_pad, jnp.where(core == 0, role, 3 - role), source, face)
        for role, source in enumerate((near_ref.at[1], own_ref.at[1])):
            put(p_pad, jnp.where(core == 0, role, 1 - role), source, face)
    for slot in range(2):
        grad = conv_rows(g_pad, slot * row, row, weight_ref)
        pre = p_pad[slot * row : (slot + 1) * row, :].astype(jnp.float32)
        logistic = jax.nn.sigmoid(pre)
        slope = logistic * (1.0 + pre * (1.0 - logistic))
        out_ref[slot * row : (slot + 1) * row, :] = (grad * slope).astype(jnp.bfloat16)


def conv_rows(pad, start, row, weight_ref):
    sums = []
    for c in range(3):
        total = None
        for r in range(3):
            at = start + (2 - r) * row
            rows = pad[pl.ds(at if isinstance(at, int) else pl.multiple_of(at, 16), row), :]
            term = lax.dot_general(
                rows, weight_ref[r, c], (((1,), (1,)), ((), ())), preferred_element_type=jnp.float32
            )
            total = term if total is None else total + term
        sums.append(total)
    return pltpu.roll(sums[2], 1, 0) + sums[1] + pltpu.roll(sums[0], row - 1, 0)


def four_rows(rows4, core, row, pre_ref, swapped_ref):
    rows4[pl.ds(pl.multiple_of(core * 2 * row, 16), 2 * row), :] = pre_ref[...]
    rows4[pl.ds(pl.multiple_of((1 - core) * 2 * row, 16), 2 * row), :] = swapped_ref[...]


def grad_input_kernel(local, side, flags_ref, pre_ref, swapped_ref, own_ref, weight_ref, out_ref, rows4):
    pitch = side + 2 * GAP
    row = local * pitch
    core = flags_ref[0]
    four_rows(rows4, core, row, pre_ref, swapped_ref)
    grad = conv_rows(rows4, core * row, row, weight_ref)
    for face in range(local):
        at = face * pitch + GAP
        own = own_ref[face].astype(jnp.float32)
        out_ref[face] = (own + grad[at : at + side, :]).astype(jnp.bfloat16)


def grad_first_kernel(row, nxl, flags_ref, x_ref, pre_ref, swapped_ref, out_ref, rows4):
    four_rows(rows4, flags_ref[0], row, pre_ref, swapped_ref)
    dests, _, lines, half = out_ref.shape
    for r in range(3):
        terms = jnp.dot(x_ref[...], rows4[(2 - r) * row : (4 - r) * row, :], preferred_element_type=jnp.float32)
        for c in range(3):
            turned = terms[c * half : (c + 1) * half, :].T
            if nxl == 1:
                for d in range(dests):
                    out_ref[d, 3 * r + c] = turned[d * lines : (d + 1) * lines, :].astype(jnp.bfloat16)
                continue
            split = turned.reshape(dests // 2, 2, lines, half)
            left = split[:, 0].reshape(-1, half)
            right = split[:, 1].reshape(-1, half)
            low = lax.broadcasted_iota(jnp.int32, left.shape, 1) < half // 2
            ones = (
                jnp.where(low, left, pltpu.roll(right, half // 2, 1)),
                jnp.where(low, pltpu.roll(left, half // 2, 1), right),
            )
            for xl, one in enumerate(ones):
                for d in range(dests // 2):
                    out_ref[2 * d + xl, 3 * r + c] = one[d * lines : (d + 1) * lines, :].astype(jnp.bfloat16)


def kernel(body, out_shape, inputs, smem=0, scratch=(), name=None, flops=0, nbytes=2**20, exps=0):
    many = isinstance(out_shape, tuple)
    return pl.pallas_call(
        body,
        out_shape=out_shape,
        in_specs=[pl.BlockSpec(memory_space=pltpu.SMEM)] * smem + whole(len(inputs) - smem),
        out_specs=tuple(whole(len(out_shape))) if many else whole(1)[0],
        scratch_shapes=scratch,
        compiler_params=pltpu.CompilerParams(vmem_limit_bytes=VMEM),
        cost_estimate=pl.CostEstimate(flops=flops, bytes_accessed=nbytes, transcendentals=exps),
        name=name,
    )(*inputs)


def on_device(sizes, saved_input, saved_pre, cotangent, first_weight, second_weight, seams, corners):
    nxh, ny, nxl, nz, nc = sizes
    nface, ntile, nchip = nxh * ny, nxl * nz * nc, nxl * nz
    x, p, g = saved_input[0, :, 0], saved_pre[0, :, 0], cotangent[0, :, 0]
    local, side, channels = x.shape
    faces = nface * local
    row = local * (side + 2 * GAP)
    bf = jnp.bfloat16
    shape = jax.ShapeDtypeStruct
    core = lax.axis_index("c")
    tile = lax.axis_index(TILE)
    top = tile >= ntile // 2
    near_wraps = (tile == 0) | (tile == ntile - 1)
    far_wraps = (tile == 1) | (tile == ntile - 2)
    flags = jnp.stack([core, near_wraps.astype(jnp.int32), far_wraps.astype(jnp.int32)])

    px_blocks = 4
    ch_blocks = nface // px_blocks
    px = side // px_blocks
    count = px * 2 // ch_blocks
    sent = kernel(
        functools.partial(pack_kernel, local, side, (px_blocks, ch_blocks)),
        shape((nface, local * (count + CELLS), channels), bf),
        (seams, g, p),
        1,
        name="pack",
    )
    swap = lambda a: lax.ppermute(a, "c", [(0, 1), (1, 0)])
    table, other = lax.optimization_barrier((lax.all_to_all(sent, FACE, 0, 0, tiled=True), swap(x)))

    cells = table[:, local * count :].reshape(faces, CELLS, channels)
    all_seams = cells[:, SEAM_AT, :4].astype(jnp.int32)
    want = jnp.where(top, all_seams[:, 0], all_seams[:, 2])
    picked = kernel(
        functools.partial(pick_kernel, faces, local, count), shape((faces, count, channels), bf), (want, table), 1, name="pick"
    )
    wrapped = lax.all_to_all(picked.reshape(nface, local, count, channels), FACE, 0, 0, tiled=True)

    outer = jnp.where(top, corners[:, 0:2], corners[:, 2:4])
    sides = jnp.stack([jnp.stack([seams[:, 3], seams[:, 1]], 1), outer], 0)
    spots = np.full((2, GAP), -1, np.int32)
    spots[0, [0, 1, GAP - 2, GAP - 1]] = (0, 1, 2, 3)
    spots[1, [0, GAP - 1]] = (4, 5)
    on_left = np.arange(GAP) >= GAP // 2
    face_at = jnp.where(on_left, sides[:, None, :, 0:1], sides[:, None, :, 1:2])
    index = jnp.where(spots[None, :, None] >= 0, face_at * CELLS + spots[None, :, None], -1)
    index = index.reshape(-1, 1).astype(jnp.int32)
    own, tails = kernel(
        functools.partial(border_kernel, local, side),
        (shape((2, local, side + GAP, channels), bf), shape((2, local, GAP, channels), bf)),
        (index, cells.reshape(faces * CELLS, channels), g, p),
        name="border",
    )
    wrapped, part = lax.optimization_barrier((wrapped, swap(own[0])))
    near, far = kernel(
        functools.partial(send_kernel, local, side, (px_blocks, ch_blocks)),
        (shape(own.shape, bf), shape(own.shape[1:], bf)),
        (flags, own, tails, wrapped),
        1,
        name="send",
    )

    pairs = lambda step: [((t + step if t % 2 else t - step) % ntile, t) for t in range(ntile)]
    near = lax.ppermute(near, TILE, pairs(1))
    far = lax.ppermute(far, TILE, pairs(2))
    grad_pre = kernel(
        functools.partial(grad_pre_kernel, local, side),
        shape((2 * row, channels), bf),
        (flags, own, part, near, far, second_weight),
        1,
        (pltpu.VMEM((4 * row, channels), bf), pltpu.VMEM((2 * row, channels), bf)),
        "grad_pre",
        2 * 18 * row * channels**2,
        4 * 2**20,
        2 * row * channels,
    )
    swapped = swap(grad_pre)

    half = channels // nc
    per_tile = channels // ntile
    both = jnp.where(core == 0, jnp.stack([x, other], 0), jnp.stack([other, x], 0))
    shifted = jnp.stack(
        [jnp.pad(both, ((0, 0), (0, 0), (GAP + 1 - c, GAP - 1 + c), (0, 0))) for c in range(3)], 0
    ).reshape(3, 2 * row, channels)
    kept = np.arange(half)
    chosen = (kept // per_tile) * (nc * per_tile) + kept % per_tile
    choose = (chosen[:, None] + core * per_tile == np.arange(channels)[None, :]).astype(bf)
    x_turned = lax.dot_general(
        choose, shifted, (((1,), (2,)), ((), ())), preferred_element_type=jnp.float32
    ).astype(bf)
    x_turned = jnp.transpose(x_turned, (1, 0, 2)).reshape(3 * half, 2 * row)

    rows4 = (pltpu.VMEM((4 * row, channels), bf),)
    width = channels // nface
    lines = width // nxl
    parts = kernel(
        functools.partial(grad_first_kernel, row, nxl),
        shape((nface * nxl, 9, lines, half), bf),
        (flags, x_turned, grad_pre, swapped),
        1,
        rows4,
        "grad_first",
        2 * 18 * half * row * channels,
    )
    grad_input = kernel(
        functools.partial(grad_input_kernel, local, side),
        shape((local, side, channels), bf),
        (flags, grad_pre, swapped, g, first_weight),
        1,
        rows4,
        "grad_input",
        2 * 9 * row * channels**2,
        2 * 2**20,
    )
    scale_factor = 1.0 / math.sqrt(faces * ntile * side)
    got = lax.all_to_all(parts, FACE + ("xl",), 0, 0, tiled=True)
    total = jnp.sum(got.astype(jnp.float32), 0) * scale_factor
    total = jnp.transpose(total.reshape(9 * lines, half)).reshape(nxl, nz, per_tile, 9 * lines)
    total = jnp.transpose(total, (1, 0, 2, 3)).reshape(nz, nxl * per_tile, 9 * lines).astype(bf)
    got = lax.all_to_all(total, "z", 0, 0, tiled=True)
    total = jnp.sum(got.astype(jnp.float32), 0).reshape(nxl, per_tile, 9, lines)
    first_out = jnp.transpose(total, (2, 1, 0, 3)).reshape(3, 3, per_tile, width)
    return grad_input.reshape(saved_input.shape), first_out


def solution(mesh, sizes=(2, 4, 2, 16, 2)):
    fine = Mesh(mesh.devices.reshape(sizes), FACE + TILE)
    field = P(None, FACE, TILE, None, None)
    return jax.shard_map(
        functools.partial(on_device, sizes),
        mesh=fine,
        in_specs=(field, field, field, P(), P(), P(FACE, None), P(FACE, None)),
        out_specs=(field, P(None, None, TILE, FACE)),
        check_vma=False,
    )
```

```python
import functools
import math

import jax
import jax.numpy as jnp
import numpy as np
from jax import lax
from jax.experimental import pallas as pl
from jax.experimental.pallas import tpu as pltpu
from jax.sharding import Mesh
from jax.sharding import PartitionSpec as P

FACE = ("xh", "y")
TILE = ("xl", "z", "c")
CHIP = ("xl", "z")
GAP = 16
CELLS = 8
SEAM_AT = 6
VMEM = 40 * 2**20


def whole(n):
    return [pl.BlockSpec(memory_space=pltpu.VMEM)] * n


def pack_kernel(local, side, blocks, seams_ref, g_ref, p_ref, out_ref, ends, cells_held, end_sems, sems):
    px_blocks, ch_blocks = blocks
    channels = g_ref.shape[-1]
    px, ch = side // px_blocks, channels // ch_blocks
    count = px * 2 // ch_blocks
    fetches = [
        pltpu.make_async_copy(source.at[:, at : at + GAP], ends.at[which, end], end_sems.at[which, end])
        for which, source in enumerate((g_ref, p_ref))
        for end, at in enumerate((0, side - GAP))
    ]
    for fetch in fetches:
        fetch.start()
    moves = []
    for b in range(px_blocks * ch_blocks):
        i, j = divmod(b, ch_blocks)
        for face in range(local):
            at = face * count
            for which, source in enumerate((g_ref, p_ref)):
                piece = source.at[face, i * px : (i + 1) * px, j * ch : (j + 1) * ch]
                if ch_blocks == 1:
                    into = out_ref.at[b, at + which * px : at + (which + 1) * px]
                else:
                    into = out_ref.at[b, at : at + px, which * ch : (which + 1) * ch]
                moves.append(pltpu.make_async_copy(piece, into, sems.at[len(moves)]))
    for move in moves:
        move.start()
    held = 4 * local * GAP
    line = lax.broadcasted_iota(jnp.int32, (local * CELLS, held), 0)
    pixel = lax.broadcasted_iota(jnp.int32, (local * CELLS, held), 1)
    cell, face_at = line % CELLS, line // CELLS * GAP
    block = local * GAP
    at = jnp.where(cell < 2, face_at + cell, block + face_at + GAP - 4 + cell)
    at = jnp.where(cell == 4, 2 * block + face_at, at)
    at = jnp.where(cell == 5, 3 * block + face_at + GAP - 1, at)
    take = jnp.where((at == pixel) & (cell < SEAM_AT), 1.0, 0.0).astype(jnp.bfloat16)
    line = lax.broadcasted_iota(jnp.int32, (local * CELLS, channels), 0)
    lane = lax.broadcasted_iota(jnp.int32, (local * CELLS, channels), 1)
    seams = jnp.zeros((local * CELLS, channels), jnp.float32)
    for face in range(local):
        for i in range(4):
            here = (line == face * CELLS + SEAM_AT) & (lane == i)
            seams = jnp.where(here, seams_ref[face, i].astype(jnp.float32), seams)
    for fetch in fetches:
        fetch.wait()
    cells = jnp.dot(take, ends[...].reshape(held, channels), preferred_element_type=jnp.float32)
    cells_held[...] = (cells + seams).astype(jnp.bfloat16)
    for b in range(px_blocks * ch_blocks):
        into = out_ref.at[b, local * count : local * (count + CELLS)]
        moves.append(pltpu.make_async_copy(cells_held, into, sems.at[len(moves)]))
        moves[-1].start()
    for move in moves:
        move.wait()


def pick_kernel(faces, local, count, want_ref, table_ref, out_ref, sems):
    moves = []
    for i in range(faces):
        face = want_ref[i]
        at = pl.multiple_of(lax.rem(face, local) * count, 16)
        source = table_ref.at[lax.div(face, local), pl.ds(at, count)]
        moves.append(pltpu.make_async_copy(source, out_ref.at[i], sems.at[i]))
        moves[-1].start()
    for move in moves:
        move.wait()


def first_sum_kernel(scale, got_ref, out_ref):
    total = got_ref[0].astype(jnp.float32)
    for i in range(1, got_ref.shape[0]):
        total = total + got_ref[i].astype(jnp.float32)
    turned = (total * scale).reshape(-1, total.shape[-1]).T
    out_ref[...] = turned.reshape(out_ref.shape).astype(jnp.bfloat16)


def second_sum_kernel(got_ref, out_ref):
    total = got_ref[0].astype(jnp.float32)
    for i in range(1, got_ref.shape[0]):
        total = total + got_ref[i].astype(jnp.float32)
    _, _, per_tile, width = out_ref.shape
    lines = total.shape[1] // 9
    for tap in range(9):
        r, c = divmod(tap, 3)
        for h in range(width // lines):
            out_ref[r, c, :, h * lines : (h + 1) * lines] = total[
                h * per_tile : (h + 1) * per_tile, tap * lines : (tap + 1) * lines
            ]


def border_kernel(local, side, index_ref, cells_ref, g_ref, p_ref, own_ref, wrap_ref):
    rows, width = index_ref.shape[0], cells_ref.shape[0]
    where = lax.broadcasted_iota(jnp.int32, (rows, width), 1) == index_ref[...]
    tails = jnp.dot(
        jnp.where(where, 1.0, 0.0).astype(jnp.bfloat16), cells_ref[...], preferred_element_type=jnp.float32
    ).astype(jnp.bfloat16)
    for which, source in enumerate((g_ref, p_ref)):
        for face in range(local):
            at = (which * local + face) * GAP
            own_ref[which, face, :side] = source[face]
            own_ref[which, face, side:] = tails[at : at + GAP]
            at += 2 * local * GAP
            wrap_ref[which, face] = tails[at : at + GAP]


def send_kernel(local, side, blocks, flags_ref, own_ref, tails_ref, pieces_ref, near_ref, far_ref):
    px_blocks, ch_blocks = blocks
    px = side // px_blocks
    channels = own_ref.shape[-1]
    ch = channels // ch_blocks
    near, far = flags_ref[1], flags_ref[2]

    def put_wrap(out, which, face):
        for b in range(px_blocks * ch_blocks):
            i, j = divmod(b, ch_blocks)
            piece = pieces_ref[b, face]
            if ch_blocks == 1:
                part = piece[which * px : (which + 1) * px]
            else:
                part = piece[:, which * ch : (which + 1) * ch]
            out[i * px : (i + 1) * px, j * ch : (j + 1) * ch] = part
        out[side:, :] = tails_ref[which, face]

    @pl.when(near == 1)
    def _():
        for face in range(local):
            put_wrap(near_ref.at[0, face], 0, face)
            put_wrap(near_ref.at[1, face], 1, face)

    @pl.when(near == 0)
    def _():
        near_ref[...] = own_ref[...]

    @pl.when(far == 1)
    def _():
        for face in range(local):
            put_wrap(far_ref.at[face], 0, face)

    @pl.when(far == 0)
    def _():
        far_ref[...] = own_ref[0]


def grad_pre_kernel(local, side, flags_ref, own_ref, part_ref, near_ref, far_ref, weight_ref, out_ref, g_pad, p_pad):
    pitch = side + 2 * GAP
    row = local * pitch
    core = flags_ref[0]

    def put(pad, slot, source, face):
        at = pl.multiple_of(slot * row + face * pitch, 16)
        border = source[face, side:]
        pad[pl.ds(at, GAP), :] = border
        pad[pl.ds(at + GAP, side), :] = source[face, :side]
        pad[pl.ds(at + GAP + side, GAP), :] = border

    for face in range(local):
        for role, source in enumerate((far_ref, near_ref.at[0], own_ref.at[0], part_ref)):
            put(g_pad, jnp.where(core == 0, role, 3 - role), source, face)
        for role, source in enumerate((near_ref.at[1], own_ref.at[1])):
            put(p_pad, jnp.where(core == 0, role, 1 - role), source, face)
    for slot in range(2):
        grad = conv_rows(g_pad, slot * row, row, weight_ref)
        pre = p_pad[slot * row : (slot + 1) * row, :].astype(jnp.float32)
        logistic = jax.nn.sigmoid(pre)
        slope = logistic * (1.0 + pre * (1.0 - logistic))
        out_ref[slot * row : (slot + 1) * row, :] = (grad * slope).astype(jnp.bfloat16)


def conv_rows(pad, start, row, weight_ref):
    sums = []
    for c in range(3):
        total = None
        for r in range(3):
            at = start + (2 - r) * row
            rows = pad[pl.ds(at if isinstance(at, int) else pl.multiple_of(at, 16), row), :]
            term = lax.dot_general(
                rows, weight_ref[r, c], (((1,), (1,)), ((), ())), preferred_element_type=jnp.float32
            )
            total = term if total is None else total + term
        sums.append(total)
    return pltpu.roll(sums[2], 1, 0) + sums[1] + pltpu.roll(sums[0], row - 1, 0)


def four_rows(rows4, core, row, pre_ref, swapped_ref):
    rows4[pl.ds(pl.multiple_of(core * 2 * row, 16), 2 * row), :] = pre_ref[...]
    rows4[pl.ds(pl.multiple_of((1 - core) * 2 * row, 16), 2 * row), :] = swapped_ref[...]


def grad_input_kernel(local, side, flags_ref, pre_ref, swapped_ref, own_ref, weight_ref, out_ref, rows4):
    pitch = side + 2 * GAP
    row = local * pitch
    core = flags_ref[0]
    four_rows(rows4, core, row, pre_ref, swapped_ref)
    grad = conv_rows(rows4, core * row, row, weight_ref)
    for face in range(local):
        at = face * pitch + GAP
        own = own_ref[face].astype(jnp.float32)
        out_ref[face] = (own + grad[at : at + side, :]).astype(jnp.bfloat16)


def grad_first_kernel(row, nxl, per_tile, flags_ref, x_ref, pre_ref, swapped_ref, out_ref, rows4):
    four_rows(rows4, flags_ref[0], row, pre_ref, swapped_ref)
    dests, _, lines, half = out_ref.shape
    for r in range(3):
        terms = jnp.dot(x_ref[...], rows4[(2 - r) * row : (4 - r) * row, :], preferred_element_type=jnp.float32)
        for c in range(3):
            turned = terms[c * half : (c + 1) * half, :].T
            if nxl == 1:
                for d in range(dests):
                    out_ref[d, 3 * r + c] = turned[d * lines : (d + 1) * lines, :].astype(jnp.bfloat16)
                continue
            split = turned.reshape(dests // 2, 2, lines, half)
            left = split[:, 0].reshape(-1, half)
            right = split[:, 1].reshape(-1, half)
            low = lax.broadcasted_iota(jnp.int32, left.shape, 1) % (2 * per_tile) < per_tile
            ones = (
                jnp.where(low, left, pltpu.roll(right, per_tile, 1)),
                jnp.where(low, pltpu.roll(left, half - per_tile, 1), right),
            )
            for xl, one in enumerate(ones):
                for d in range(dests // 2):
                    out_ref[2 * d + xl, 3 * r + c] = one[d * lines : (d + 1) * lines, :].astype(jnp.bfloat16)


def kernel(body, out_shape, inputs, smem=0, scratch=(), name=None, flops=0, nbytes=2**20, exps=0, hbm=(0, 0), vmem=VMEM):
    many = isinstance(out_shape, tuple)
    spots = [pl.BlockSpec(memory_space=pltpu.HBM)] * hbm[0] + whole(len(inputs) - smem - hbm[0])
    return pl.pallas_call(
        body,
        out_shape=out_shape,
        in_specs=[pl.BlockSpec(memory_space=pltpu.SMEM)] * smem + spots,
        out_specs=tuple(whole(len(out_shape))) if many else pl.BlockSpec(memory_space=pltpu.HBM) if hbm[1] else whole(1)[0],
        scratch_shapes=scratch,
        compiler_params=pltpu.CompilerParams(vmem_limit_bytes=vmem),
        cost_estimate=pl.CostEstimate(flops=flops, bytes_accessed=nbytes, transcendentals=exps),
        name=name,
    )(*inputs)


def on_device(sizes, saved_input, saved_pre, cotangent, first_weight, second_weight, seams, corners):
    nxh, ny, nxl, nz, nc = sizes
    nface, ntile, nchip = nxh * ny, nxl * nz * nc, nxl * nz
    x, p, g = saved_input[0, :, 0], saved_pre[0, :, 0], cotangent[0, :, 0]
    local, side, channels = x.shape
    faces = nface * local
    row = local * (side + 2 * GAP)
    bf = jnp.bfloat16
    shape = jax.ShapeDtypeStruct
    core = lax.axis_index("c")
    tile = lax.axis_index(TILE)
    top = tile >= ntile // 2
    near_wraps = (tile == 0) | (tile == ntile - 1)
    far_wraps = (tile == 1) | (tile == ntile - 2)
    flags = jnp.stack([core, near_wraps.astype(jnp.int32), far_wraps.astype(jnp.int32)])

    px_blocks = 4
    ch_blocks = nface // px_blocks
    px = side // px_blocks
    count = px * 2 // ch_blocks
    sent = kernel(
        functools.partial(pack_kernel, local, side, (px_blocks, ch_blocks)),
        shape((nface, local * (count + CELLS), channels), bf),
        (seams, g, p),
        1,
        (
            pltpu.VMEM((2, 2, local, GAP, channels), bf),
            pltpu.VMEM((local * CELLS, channels), bf),
            pltpu.SemaphoreType.DMA((2, 2)),
            pltpu.SemaphoreType.DMA((nface * (2 * local + 1),)),
        ),
        "pack",
        hbm=(2, 1),
        vmem=None,
    )
    swap = lambda a: lax.ppermute(a, "c", [(0, 1), (1, 0)])
    table, other = lax.optimization_barrier((lax.all_to_all(sent, FACE, 0, 0, tiled=True), swap(x)))

    cells = table[:, local * count :].reshape(faces, CELLS, channels)
    all_seams = cells[:, SEAM_AT, :4].astype(jnp.int32)
    want = jnp.where(top, all_seams[:, 0], all_seams[:, 2])
    picked = kernel(
        functools.partial(pick_kernel, faces, local, count), shape((faces, count, channels), bf), (want, table), 1,
        (pltpu.SemaphoreType.DMA((faces,)),), "pick", hbm=(0, 1),
    )
    wrapped = lax.all_to_all(picked.reshape(nface, local, count, channels), FACE, 0, 0, tiled=True)

    outer = jnp.where(top, corners[:, 0:2], corners[:, 2:4])
    sides = jnp.stack([jnp.stack([seams[:, 3], seams[:, 1]], 1), outer], 0)
    spots = np.full((2, GAP), -1, np.int32)
    spots[0, [0, 1, GAP - 2, GAP - 1]] = (0, 1, 2, 3)
    spots[1, [0, GAP - 1]] = (4, 5)
    on_left = np.arange(GAP) >= GAP // 2
    face_at = jnp.where(on_left, sides[:, None, :, 0:1], sides[:, None, :, 1:2])
    index = jnp.where(spots[None, :, None] >= 0, face_at * CELLS + spots[None, :, None], -1)
    index = index.reshape(-1, 1).astype(jnp.int32)
    own, tails = kernel(
        functools.partial(border_kernel, local, side),
        (shape((2, local, side + GAP, channels), bf), shape((2, local, GAP, channels), bf)),
        (index, cells.reshape(faces * CELLS, channels), g, p),
        name="border",
    )
    wrapped, part = lax.optimization_barrier((wrapped, swap(own[0])))
    near, far = kernel(
        functools.partial(send_kernel, local, side, (px_blocks, ch_blocks)),
        (shape(own.shape, bf), shape(own.shape[1:], bf)),
        (flags, own, tails, wrapped),
        1,
        name="send",
    )

    pairs = lambda step: [((t + step if t % 2 else t - step) % ntile, t) for t in range(ntile)]
    near = lax.ppermute(near, TILE, pairs(1))
    far = lax.ppermute(far, TILE, pairs(2))
    grad_pre = kernel(
        functools.partial(grad_pre_kernel, local, side),
        shape((2 * row, channels), bf),
        (flags, own, part, near, far, second_weight),
        1,
        (pltpu.VMEM((4 * row, channels), bf), pltpu.VMEM((2 * row, channels), bf)),
        "grad_pre",
        2 * 18 * row * channels**2,
        4 * 2**20,
        2 * row * channels,
    )
    swapped = swap(grad_pre)

    half = channels // nc
    per_tile = channels // ntile
    both = jnp.where(core == 0, jnp.stack([x, other], 0), jnp.stack([other, x], 0))
    shifted = jnp.stack(
        [jnp.pad(both, ((0, 0), (0, 0), (GAP + 1 - c, GAP - 1 + c), (0, 0))) for c in range(3)], 0
    ).reshape(3, 2 * row, channels)
    kept = np.arange(channels).reshape(nxl, nz, nc, per_tile)[:, :, 0]
    chosen = np.transpose(kept, (1, 0, 2)).reshape(half)
    choose = (chosen[:, None] + core * per_tile == np.arange(channels)[None, :]).astype(bf)
    x_turned = lax.dot_general(
        choose, shifted, (((1,), (2,)), ((), ())), preferred_element_type=jnp.float32
    ).astype(bf)
    x_turned = jnp.transpose(x_turned, (1, 0, 2)).reshape(3 * half, 2 * row)

    rows4 = (pltpu.VMEM((4 * row, channels), bf),)
    width = channels // nface
    lines = width // nxl
    parts = kernel(
        functools.partial(grad_first_kernel, row, nxl, per_tile),
        shape((nface * nxl, 9, lines, half), bf),
        (flags, x_turned, grad_pre, swapped),
        1,
        rows4,
        "grad_first",
        2 * 18 * half * row * channels,
    )
    grad_input = kernel(
        functools.partial(grad_input_kernel, local, side),
        shape((local, side, channels), bf),
        (flags, grad_pre, swapped, g, first_weight),
        1,
        rows4,
        "grad_input",
        2 * 9 * row * channels**2,
        2 * 2**20,
    )
    scale_factor = 1.0 / math.sqrt(faces * ntile * side)
    got = lax.all_to_all(parts, FACE + ("xl",), 0, 0, tiled=True)
    total = kernel(
        functools.partial(first_sum_kernel, scale_factor),
        shape((nz, nxl * per_tile, 9 * lines), bf),
        (got,),
        name="first_sum",
    )
    got = lax.all_to_all(total, "z", 0, 0, tiled=True)
    first_out = kernel(second_sum_kernel, shape((3, 3, per_tile, width), jnp.float32), (got,), name="second_sum")
    return grad_input.reshape(saved_input.shape), first_out


def solution(mesh, sizes=(2, 4, 2, 16, 2)):
    fine = Mesh(mesh.devices.reshape(sizes), FACE + TILE)
    field = P(None, FACE, TILE, None, None)
    return jax.shard_map(
        functools.partial(on_device, sizes),
        mesh=fine,
        in_specs=(field, field, field, P(), P(), P(FACE, None), P(FACE, None)),
        out_specs=(field, P(None, None, TILE, FACE)),
        check_vma=False,
    )
```

```python
import functools
import math

import jax
import jax.numpy as jnp
import numpy as np
from jax import lax
from jax.experimental import pallas as pl
from jax.experimental.pallas import tpu as pltpu
from jax.sharding import Mesh
from jax.sharding import PartitionSpec as P

FACE = ("xh", "y")
TILE = ("xl", "z", "c")
CHIP = ("xl", "z")
GAP = 16
CELLS = 8
SEAM_AT = 6
VMEM = 40 * 2**20


def whole(n):
    return [pl.BlockSpec(memory_space=pltpu.VMEM)] * n


def pack_kernel(local, side, blocks, seams_ref, g_hbm, p_hbm, out_ref, g_ref, p_ref, sems):
    fetches = [
        pltpu.make_async_copy(g_hbm, g_ref, sems.at[0]),
        pltpu.make_async_copy(p_hbm, p_ref, sems.at[1]),
    ]
    for fetch in fetches:
        fetch.start()
    px_blocks, ch_blocks = blocks
    channels = g_ref.shape[-1]
    px, ch = side // px_blocks, channels // ch_blocks
    count = px * 2 // ch_blocks
    shape = (local * CELLS, local * side)
    line = lax.broadcasted_iota(jnp.int32, shape, 0)
    pixel = lax.broadcasted_iota(jnp.int32, shape, 1)
    cell, base = line % CELLS, line // CELLS * side
    of_g = jnp.where(cell < 2, base + cell, jnp.where(cell < 4, base + side - 4 + cell, -1))
    of_p = jnp.where(cell == 4, base, jnp.where(cell == 5, base + side - 1, -1))
    seams = jnp.zeros((local * CELLS, channels), jnp.float32)
    line = lax.broadcasted_iota(jnp.int32, seams.shape, 0)
    lane = lax.broadcasted_iota(jnp.int32, seams.shape, 1)
    for face in range(local):
        for i in range(4):
            here = (line == face * CELLS + SEAM_AT) & (lane == i)
            seams = jnp.where(here, seams_ref[face, i].astype(jnp.float32), seams)
    take = lambda at, ref: jnp.dot(
        jnp.where(at == pixel, 1.0, 0.0).astype(jnp.bfloat16),
        ref[...].reshape(local * side, channels),
        preferred_element_type=jnp.float32,
    )
    for fetch in fetches:
        fetch.wait()
    cells = (take(of_g, g_ref) + take(of_p, p_ref) + seams).astype(jnp.bfloat16)
    for b in range(px_blocks * ch_blocks):
        i, j = divmod(b, ch_blocks)
        for face in range(local):
            at = face * count
            for which, source in enumerate((g_ref, p_ref)):
                piece = source[face, i * px : (i + 1) * px, j * ch : (j + 1) * ch]
                if ch_blocks == 1:
                    out_ref[b, at + which * px : at + (which + 1) * px] = piece
                else:
                    out_ref[b, at : at + px, which * ch : (which + 1) * ch] = piece
        out_ref[b, local * count :] = cells


def pick_kernel(faces, local, count, want_ref, table_ref, out_ref):
    for i in range(faces):
        face = want_ref[i]
        at = pl.multiple_of(lax.rem(face, local) * count, 16)
        into, row = divmod(i, local)
        out_ref[into, row * count : (row + 1) * count] = table_ref[lax.div(face, local), pl.ds(at, count)]


def first_sum_kernel(scale, got_ref, out_ref):
    total = got_ref[0].astype(jnp.float32)
    for i in range(1, got_ref.shape[0]):
        total = total + got_ref[i].astype(jnp.float32)
    turned = (total * scale).T
    out_ref[...] = turned.reshape(out_ref.shape).astype(jnp.bfloat16)


def second_sum_kernel(got_ref, out_ref):
    total = got_ref[0].astype(jnp.float32)
    for i in range(1, got_ref.shape[0]):
        total = total + got_ref[i].astype(jnp.float32)
    _, _, per_tile, width = out_ref.shape
    lines = total.shape[1] // 9
    for tap in range(9):
        r, c = divmod(tap, 3)
        for h in range(width // lines):
            out_ref[r, c, :, h * lines : (h + 1) * lines] = total[
                h * per_tile : (h + 1) * per_tile, tap * lines : (tap + 1) * lines
            ]


def border_kernel(local, side, index_ref, cells_ref, g_ref, p_ref, own_ref, wrap_ref):
    rows, width = index_ref.shape[0], cells_ref.shape[0]
    where = lax.broadcasted_iota(jnp.int32, (rows, width), 1) == index_ref[...]
    tails = jnp.dot(
        jnp.where(where, 1.0, 0.0).astype(jnp.bfloat16), cells_ref[...], preferred_element_type=jnp.float32
    ).astype(jnp.bfloat16)
    for which, source in enumerate((g_ref, p_ref)):
        for face in range(local):
            at = (which * local + face) * GAP
            own_ref[which, face, :side] = source[face]
            own_ref[which, face, side:] = tails[at : at + GAP]
            at += 2 * local * GAP
            wrap_ref[which, face] = tails[at : at + GAP]


def send_kernel(local, side, blocks, flags_ref, own_ref, tails_ref, pieces_ref, near_ref, far_ref):
    px_blocks, ch_blocks = blocks
    px = side // px_blocks
    channels = own_ref.shape[-1]
    ch = channels // ch_blocks
    count = px * 2 // ch_blocks
    near, far = flags_ref[1], flags_ref[2]

    def put_wrap(out, which, face):
        for b in range(px_blocks * ch_blocks):
            i, j = divmod(b, ch_blocks)
            piece = pieces_ref[b, face * count : (face + 1) * count]
            if ch_blocks == 1:
                part = piece[which * px : (which + 1) * px]
            else:
                part = piece[:, which * ch : (which + 1) * ch]
            out[i * px : (i + 1) * px, j * ch : (j + 1) * ch] = part
        out[side:, :] = tails_ref[which, face]

    @pl.when(near == 1)
    def _():
        for face in range(local):
            put_wrap(near_ref.at[0, face], 0, face)
            put_wrap(near_ref.at[1, face], 1, face)

    @pl.when(near == 0)
    def _():
        near_ref[...] = own_ref[...]

    @pl.when(far == 1)
    def _():
        for face in range(local):
            put_wrap(far_ref.at[face], 0, face)

    @pl.when(far == 0)
    def _():
        far_ref[...] = own_ref[0]


def grad_pre_kernel(local, side, flags_ref, own_ref, part_ref, near_ref, far_ref, weight_ref, out_ref, g_pad, p_pad):
    pitch = side + 2 * GAP
    row = local * pitch
    core = flags_ref[0]

    def put(pad, slot, source, face):
        at = pl.multiple_of(slot * row + face * pitch, 16)
        border = source[face, side:]
        pad[pl.ds(at, GAP), :] = border
        pad[pl.ds(at + GAP, side), :] = source[face, :side]
        pad[pl.ds(at + GAP + side, GAP), :] = border

    for face in range(local):
        for role, source in enumerate((far_ref, near_ref.at[0], own_ref.at[0], part_ref)):
            put(g_pad, jnp.where(core == 0, role, 3 - role), source, face)
        for role, source in enumerate((near_ref.at[1], own_ref.at[1])):
            put(p_pad, jnp.where(core == 0, role, 1 - role), source, face)
    for slot in range(2):
        grad = conv_rows(g_pad, slot * row, row, weight_ref)
        pre = p_pad[slot * row : (slot + 1) * row, :].astype(jnp.float32)
        logistic = jax.nn.sigmoid(pre)
        slope = logistic * (1.0 + pre * (1.0 - logistic))
        out_ref[slot * row : (slot + 1) * row, :] = (grad * slope).astype(jnp.bfloat16)


def conv_rows(pad, start, row, weight_ref):
    sums = []
    for c in range(3):
        total = None
        for r in range(3):
            at = start + (2 - r) * row
            rows = pad[pl.ds(at if isinstance(at, int) else pl.multiple_of(at, 16), row), :]
            term = lax.dot_general(
                rows, weight_ref[r, c], (((1,), (1,)), ((), ())), preferred_element_type=jnp.float32
            )
            total = term if total is None else total + term
        sums.append(total)
    return pltpu.roll(sums[2], 1, 0) + sums[1] + pltpu.roll(sums[0], row - 1, 0)


def four_rows(rows4, core, row, pre_ref, swapped_ref):
    rows4[pl.ds(pl.multiple_of(core * 2 * row, 16), 2 * row), :] = pre_ref[...]
    rows4[pl.ds(pl.multiple_of((1 - core) * 2 * row, 16), 2 * row), :] = swapped_ref[...]


def grad_input_kernel(local, side, flags_ref, pre_ref, swapped_ref, own_ref, weight_ref, out_ref, rows4):
    pitch = side + 2 * GAP
    row = local * pitch
    core = flags_ref[0]
    four_rows(rows4, core, row, pre_ref, swapped_ref)
    grad = conv_rows(rows4, core * row, row, weight_ref)
    for face in range(local):
        at = face * pitch + GAP
        own = own_ref[face].astype(jnp.float32)
        out_ref[face] = (own + grad[at : at + side, :]).astype(jnp.bfloat16)


def grad_first_kernel(row, nxl, per_tile, flags_ref, x_ref, pre_ref, swapped_ref, out_ref, rows4):
    four_rows(rows4, flags_ref[0], row, pre_ref, swapped_ref)
    dests, lines, half = out_ref.shape[0], out_ref.shape[1] // 9, out_ref.shape[2]
    for r in range(3):
        terms = jnp.dot(x_ref[...], rows4[(2 - r) * row : (4 - r) * row, :], preferred_element_type=jnp.float32)
        for c in range(3):
            turned = terms[c * half : (c + 1) * half, :].T
            at = (3 * r + c) * lines
            if nxl == 1:
                for d in range(dests):
                    out_ref[d, at : at + lines] = turned[d * lines : (d + 1) * lines, :].astype(jnp.bfloat16)
                continue
            split = turned.reshape(dests // 2, 2, lines, half)
            left = split[:, 0].reshape(-1, half)
            right = split[:, 1].reshape(-1, half)
            low = lax.broadcasted_iota(jnp.int32, left.shape, 1) % (2 * per_tile) < per_tile
            ones = (
                jnp.where(low, left, pltpu.roll(right, per_tile, 1)),
                jnp.where(low, pltpu.roll(left, half - per_tile, 1), right),
            )
            for xl, one in enumerate(ones):
                for d in range(dests // 2):
                    out_ref[2 * d + xl, at : at + lines] = one[d * lines : (d + 1) * lines, :].astype(jnp.bfloat16)


def kernel(body, out_shape, inputs, smem=0, scratch=(), name=None, flops=0, nbytes=2**20, exps=0, hbm=0, vmem=VMEM):
    many = isinstance(out_shape, tuple)
    spots = [pl.BlockSpec(memory_space=pltpu.HBM)] * hbm + whole(len(inputs) - smem - hbm)
    return pl.pallas_call(
        body,
        out_shape=out_shape,
        in_specs=[pl.BlockSpec(memory_space=pltpu.SMEM)] * smem + spots,
        out_specs=tuple(whole(len(out_shape))) if many else whole(1)[0],
        scratch_shapes=scratch,
        compiler_params=pltpu.CompilerParams(vmem_limit_bytes=vmem),
        cost_estimate=pl.CostEstimate(flops=flops, bytes_accessed=nbytes, transcendentals=exps),
        name=name,
    )(*inputs)


def on_device(sizes, saved_input, saved_pre, cotangent, first_weight, second_weight, seams, corners):
    nxh, ny, nxl, nz, nc = sizes
    nface, ntile, nchip = nxh * ny, nxl * nz * nc, nxl * nz
    x, p, g = saved_input[0, :, 0], saved_pre[0, :, 0], cotangent[0, :, 0]
    local, side, channels = x.shape
    faces = nface * local
    row = local * (side + 2 * GAP)
    bf = jnp.bfloat16
    shape = jax.ShapeDtypeStruct
    core = lax.axis_index("c")
    tile = lax.axis_index(TILE)
    top = tile >= ntile // 2
    near_wraps = (tile == 0) | (tile == ntile - 1)
    far_wraps = (tile == 1) | (tile == ntile - 2)
    flags = jnp.stack([core, near_wraps.astype(jnp.int32), far_wraps.astype(jnp.int32)])

    px_blocks = 4
    ch_blocks = nface // px_blocks
    px = side // px_blocks
    count = px * 2 // ch_blocks
    sent = kernel(
        functools.partial(pack_kernel, local, side, (px_blocks, ch_blocks)),
        shape((nface, local * (count + CELLS), channels), bf),
        (seams, g, p),
        1,
        (
            pltpu.VMEM((local, side, channels), bf),
            pltpu.VMEM((local, side, channels), bf),
            pltpu.SemaphoreType.DMA((2,)),
        ),
        "pack",
        hbm=2,
        vmem=None,
    )
    swap = lambda a: lax.ppermute(a, "c", [(0, 1), (1, 0)])
    table, other = lax.optimization_barrier((lax.all_to_all(sent, FACE, 0, 0, tiled=True), swap(x)))

    cells = table[:, local * count :].reshape(faces, CELLS, channels)
    all_seams = cells[:, SEAM_AT, :4].astype(jnp.int32)
    want = jnp.where(top, all_seams[:, 0], all_seams[:, 2])
    picked = kernel(
        functools.partial(pick_kernel, faces, local, count),
        shape((nface, local * count, channels), bf),
        (want, table),
        1,
        name="pick",
    )
    wrapped = lax.all_to_all(picked, FACE, 0, 0, tiled=True)

    outer = jnp.where(top, corners[:, 0:2], corners[:, 2:4])
    sides = jnp.stack([jnp.stack([seams[:, 3], seams[:, 1]], 1), outer], 0)
    spots = np.full((2, GAP), -1, np.int32)
    spots[0, [0, 1, GAP - 2, GAP - 1]] = (0, 1, 2, 3)
    spots[1, [0, GAP - 1]] = (4, 5)
    on_left = np.arange(GAP) >= GAP // 2
    face_at = jnp.where(on_left, sides[:, None, :, 0:1], sides[:, None, :, 1:2])
    index = jnp.where(spots[None, :, None] >= 0, face_at * CELLS + spots[None, :, None], -1)
    index = index.reshape(-1, 1).astype(jnp.int32)
    own, tails = kernel(
        functools.partial(border_kernel, local, side),
        (shape((2, local, side + GAP, channels), bf), shape((2, local, GAP, channels), bf)),
        (index, cells.reshape(faces * CELLS, channels), g, p),
        name="border",
    )
    wrapped, part = lax.optimization_barrier((wrapped, swap(own[0])))
    near, far = kernel(
        functools.partial(send_kernel, local, side, (px_blocks, ch_blocks)),
        (shape(own.shape, bf), shape(own.shape[1:], bf)),
        (flags, own, tails, wrapped),
        1,
        name="send",
    )

    pairs = lambda step: [((t + step if t % 2 else t - step) % ntile, t) for t in range(ntile)]
    near = lax.ppermute(near, TILE, pairs(1))
    far = lax.ppermute(far, TILE, pairs(2))
    grad_pre = kernel(
        functools.partial(grad_pre_kernel, local, side),
        shape((2 * row, channels), bf),
        (flags, own, part, near, far, second_weight),
        1,
        (pltpu.VMEM((4 * row, channels), bf), pltpu.VMEM((2 * row, channels), bf)),
        "grad_pre",
        2 * 18 * row * channels**2,
        4 * 2**20,
        2 * row * channels,
    )
    swapped = swap(grad_pre)

    half = channels // nc
    per_tile = channels // ntile
    both = jnp.where(core == 0, jnp.stack([x, other], 0), jnp.stack([other, x], 0))
    shifted = jnp.stack(
        [jnp.pad(both, ((0, 0), (0, 0), (GAP + 1 - c, GAP - 1 + c), (0, 0))) for c in range(3)], 0
    ).reshape(3, 2 * row, channels)
    kept = np.arange(channels).reshape(nxl, nz, nc, per_tile)[:, :, 0]
    chosen = np.transpose(kept, (1, 0, 2)).reshape(half)
    choose = (chosen[:, None] + core * per_tile == np.arange(channels)[None, :]).astype(bf)
    x_turned = lax.dot_general(
        choose, shifted, (((1,), (2,)), ((), ())), preferred_element_type=jnp.float32
    ).astype(bf)
    x_turned = jnp.transpose(x_turned, (1, 0, 2)).reshape(3 * half, 2 * row)

    rows4 = (pltpu.VMEM((4 * row, channels), bf),)
    width = channels // nface
    lines = width // nxl
    parts = kernel(
        functools.partial(grad_first_kernel, row, nxl, per_tile),
        shape((nface * nxl, 9 * lines, half), bf),
        (flags, x_turned, grad_pre, swapped),
        1,
        rows4,
        "grad_first",
        2 * 18 * half * row * channels,
    )
    grad_input = kernel(
        functools.partial(grad_input_kernel, local, side),
        shape((local, side, channels), bf),
        (flags, grad_pre, swapped, g, first_weight),
        1,
        rows4,
        "grad_input",
        2 * 9 * row * channels**2,
        2 * 2**20,
    )
    scale_factor = 1.0 / math.sqrt(faces * ntile * side)
    got = lax.all_to_all(parts, FACE + ("xl",), 0, 0, tiled=True)
    total = kernel(
        functools.partial(first_sum_kernel, scale_factor),
        shape((nz, nxl * per_tile, 9 * lines), bf),
        (got,),
        name="first_sum",
    )
    got = lax.all_to_all(total, "z", 0, 0, tiled=True)
    first_out = kernel(second_sum_kernel, shape((3, 3, per_tile, width), jnp.float32), (got,), name="second_sum")
    return grad_input.reshape(saved_input.shape), first_out


def solution(mesh, sizes=(2, 4, 2, 16, 2)):
    fine = Mesh(mesh.devices.reshape(sizes), FACE + TILE)
    field = P(None, FACE, TILE, None, None)
    return jax.shard_map(
        functools.partial(on_device, sizes),
        mesh=fine,
        in_specs=(field, field, field, P(), P(), P(FACE, None), P(FACE, None)),
        out_specs=(field, P(None, None, TILE, FACE)),
        check_vma=False,
    )
```

```python
import functools
import math

import jax
import jax.numpy as jnp
import numpy as np
from jax import lax
from jax.experimental import pallas as pl
from jax.experimental.pallas import tpu as pltpu
from jax.sharding import Mesh
from jax.sharding import PartitionSpec as P

FACE = ("xh", "y")
TILE = ("xl", "z", "c")
CHIP = ("xl", "z")
GAP = 16
CELLS = 8
SEAM_AT = 6
VMEM = 40 * 2**20


def whole(n):
    return [pl.BlockSpec(memory_space=pltpu.VMEM)] * n


def pack_kernel(local, side, blocks, seams_ref, g_hbm, p_hbm, out_ref, g_ref, p_ref, sems):
    fetches = [
        pltpu.make_async_copy(g_hbm, g_ref, sems.at[0]),
        pltpu.make_async_copy(p_hbm, p_ref, sems.at[1]),
    ]
    for fetch in fetches:
        fetch.start()
    px_blocks, ch_blocks = blocks
    channels = g_ref.shape[-1]
    px, ch = side // px_blocks, channels // ch_blocks
    count = px * 2 // ch_blocks
    shape = (local * CELLS, local * side)
    line = lax.broadcasted_iota(jnp.int32, shape, 0)
    pixel = lax.broadcasted_iota(jnp.int32, shape, 1)
    cell, base = line % CELLS, line // CELLS * side
    of_g = jnp.where(cell < 2, base + cell, jnp.where(cell < 4, base + side - 4 + cell, -1))
    of_p = jnp.where(cell == 4, base, jnp.where(cell == 5, base + side - 1, -1))
    seams = jnp.zeros((local * CELLS, channels), jnp.float32)
    line = lax.broadcasted_iota(jnp.int32, seams.shape, 0)
    lane = lax.broadcasted_iota(jnp.int32, seams.shape, 1)
    for face in range(local):
        for i in range(4):
            here = (line == face * CELLS + SEAM_AT) & (lane == i)
            seams = jnp.where(here, seams_ref[face, i].astype(jnp.float32), seams)
    take = lambda at, ref: jnp.dot(
        jnp.where(at == pixel, 1.0, 0.0).astype(jnp.bfloat16),
        ref[...].reshape(local * side, channels),
        preferred_element_type=jnp.float32,
    )
    for fetch in fetches:
        fetch.wait()
    cells = (take(of_g, g_ref) + take(of_p, p_ref) + seams).astype(jnp.bfloat16)
    for b in range(px_blocks * ch_blocks):
        i, j = divmod(b, ch_blocks)
        for face in range(local):
            at = face * count
            for which, source in enumerate((g_ref, p_ref)):
                piece = source[face, i * px : (i + 1) * px, j * ch : (j + 1) * ch]
                if ch_blocks == 1:
                    out_ref[b, at + which * px : at + (which + 1) * px] = piece
                else:
                    out_ref[b, at : at + px, which * ch : (which + 1) * ch] = piece
        out_ref[b, local * count :] = cells


def pick_kernel(faces, local, count, want_ref, table_ref, out_ref):
    for i in range(faces):
        face = want_ref[i]
        at = pl.multiple_of(lax.rem(face, local) * count, 16)
        into, row = divmod(i, local)
        out_ref[into, row * count : (row + 1) * count] = table_ref[lax.div(face, local), pl.ds(at, count)]


def first_sum_kernel(scale, got_ref, out_ref):
    total = got_ref[0].astype(jnp.float32)
    for i in range(1, got_ref.shape[0]):
        total = total + got_ref[i].astype(jnp.float32)
    turned = (total * scale).T
    out_ref[...] = turned.reshape(out_ref.shape).astype(jnp.bfloat16)


def second_sum_kernel(got_ref, out_ref):
    total = got_ref[0].astype(jnp.float32)
    for i in range(1, got_ref.shape[0]):
        total = total + got_ref[i].astype(jnp.float32)
    _, _, per_tile, width = out_ref.shape
    lines = total.shape[1] // 9
    for tap in range(9):
        r, c = divmod(tap, 3)
        for h in range(width // lines):
            out_ref[r, c, :, h * lines : (h + 1) * lines] = total[
                h * per_tile : (h + 1) * per_tile, tap * lines : (tap + 1) * lines
            ]


def border_kernel(
    local, side, tiles, flags_ref, seams_ref, corners_ref, table_ref, g_ref, p_ref, x_ref, own_ref, wrap_ref, mine_ref, kept_ref
):
    below = flags_ref[3]
    held = local * CELLS
    cells = table_ref[:, table_ref.shape[1] - held :].reshape(table_ref.shape[0] * held, -1)
    rows, width = 4 * local * GAP, cells.shape[0]
    row = lax.broadcasted_iota(jnp.int32, (rows, 1), 0)
    spot, block = row % GAP, row // GAP
    of_g = jnp.where(spot < 2, spot, jnp.where(spot >= GAP - 2, spot - (GAP - 4), -1))
    of_p = jnp.where(spot == 0, 4, jnp.where(spot == GAP - 1, 5, -1))
    cell = jnp.where(block % (2 * local) < local, of_g, of_p)
    face_at = jnp.zeros((rows, 1), jnp.int32)
    for face in range(local):
        for beyond in range(2):
            if beyond:
                left, right = corners_ref[face, 2 * below], corners_ref[face, 2 * below + 1]
            else:
                left, right = seams_ref[face, 3], seams_ref[face, 1]
            here = (block % local == face) & (block // (2 * local) == beyond)
            face_at = jnp.where(here, jnp.where(spot < GAP // 2, right, left), face_at)
    index = jnp.where(cell < 0, -1, face_at * CELLS + cell)
    where = lax.broadcasted_iota(jnp.int32, (rows, width), 1) == index
    tails = jnp.dot(
        jnp.where(where, 1.0, 0.0).astype(jnp.bfloat16), cells, preferred_element_type=jnp.float32
    ).astype(jnp.bfloat16)
    for which, source in enumerate((g_ref, p_ref)):
        for face in range(local):
            at = (which * local + face) * GAP
            own_ref[which, face, :side] = source[face]
            own_ref[which, face, side:] = tails[at : at + GAP]
            if which == 0:
                mine_ref[face, :side] = source[face]
                mine_ref[face, side : side + GAP] = tails[at : at + GAP]
            at += 2 * local * GAP
            wrap_ref[which, face] = tails[at : at + GAP]
    nxl, nz, nc, per_tile = tiles
    channels, half = x_ref.shape[-1], kept_ref.shape[-1]
    line = lax.broadcasted_iota(jnp.int32, (channels, nc * half), 0)
    lane = lax.broadcasted_iota(jnp.int32, (channels, nc * half), 1)
    of_core = jnp.where(lane < half, flags_ref[0], 1 - flags_ref[0])
    place = lane % half
    xl, z = place // per_tile % nxl, place // (per_tile * nxl)
    wanted = ((xl * nz + z) * nc + of_core) * per_tile + place % per_tile
    chosen = jnp.dot(
        x_ref[...].reshape(local * side, channels),
        jnp.where(line == wanted, 1.0, 0.0).astype(jnp.bfloat16),
        preferred_element_type=jnp.float32,
    ).astype(jnp.bfloat16)
    kept_ref[...] = chosen[:, :half]
    for face in range(local):
        for part in range(2):
            at = face * side + part * side // 2
            mine_ref[face, side + GAP :, part * half : (part + 1) * half] = chosen[at : at + side // 2, half:]


def turn_kernel(local, side, flags_ref, kept_ref, part_ref, out_ref, lines):
    pitch = side + 2 * GAP
    row = local * pitch
    half = kept_ref.shape[-1]
    lines[...] = jnp.zeros_like(lines)
    for face in range(local):
        at = pl.multiple_of(flags_ref[0] * row + face * pitch + GAP, 16)
        lines[pl.ds(at, side), :] = kept_ref[face * side : (face + 1) * side].astype(jnp.float32)
        for part in range(2):
            at = pl.multiple_of((1 - flags_ref[0]) * row + face * pitch + GAP + part * side // 2, 16)
            lines[pl.ds(at, side // 2), :] = part_ref[face, side + GAP :, part * half : (part + 1) * half].astype(jnp.float32)
    for c in range(3):
        moved = lines[...] if c == 1 else pltpu.roll(lines[...], (1 - c) % (2 * row), 0)
        out_ref[c * half : (c + 1) * half, :] = moved.T.astype(jnp.bfloat16)


def send_kernel(local, side, blocks, flags_ref, own_ref, tails_ref, pieces_ref, near_ref, far_ref):
    px_blocks, ch_blocks = blocks
    px = side // px_blocks
    channels = own_ref.shape[-1]
    ch = channels // ch_blocks
    count = px * 2 // ch_blocks
    near, far = flags_ref[1], flags_ref[2]

    def put_wrap(out, which, face):
        for b in range(px_blocks * ch_blocks):
            i, j = divmod(b, ch_blocks)
            piece = pieces_ref[b, face * count : (face + 1) * count]
            if ch_blocks == 1:
                part = piece[which * px : (which + 1) * px]
            else:
                part = piece[:, which * ch : (which + 1) * ch]
            out[i * px : (i + 1) * px, j * ch : (j + 1) * ch] = part
        out[side:, :] = tails_ref[which, face]

    @pl.when(near == 1)
    def _():
        for face in range(local):
            put_wrap(near_ref.at[0, face], 0, face)
            put_wrap(near_ref.at[1, face], 1, face)

    @pl.when(near == 0)
    def _():
        near_ref[...] = own_ref[...]

    @pl.when(far == 1)
    def _():
        for face in range(local):
            put_wrap(far_ref.at[face], 0, face)

    @pl.when(far == 0)
    def _():
        far_ref[...] = own_ref[0]


def grad_pre_kernel(local, side, flags_ref, own_ref, part_ref, near_ref, far_ref, weight_ref, out_ref, g_pad, p_pad):
    pitch = side + 2 * GAP
    row = local * pitch
    core = flags_ref[0]

    def put(pad, slot, source, face):
        at = pl.multiple_of(slot * row + face * pitch, 16)
        border = source[face, side : side + GAP]
        pad[pl.ds(at, GAP), :] = border
        pad[pl.ds(at + GAP, side), :] = source[face, :side]
        pad[pl.ds(at + GAP + side, GAP), :] = border

    for face in range(local):
        for role, source in enumerate((far_ref, near_ref.at[0], own_ref.at[0], part_ref)):
            put(g_pad, jnp.where(core == 0, role, 3 - role), source, face)
        for role, source in enumerate((near_ref.at[1], own_ref.at[1])):
            put(p_pad, jnp.where(core == 0, role, 1 - role), source, face)
    for slot in range(2):
        grad = conv_rows(g_pad, slot * row, row, weight_ref)
        pre = p_pad[slot * row : (slot + 1) * row, :].astype(jnp.float32)
        logistic = jax.nn.sigmoid(pre)
        slope = logistic * (1.0 + pre * (1.0 - logistic))
        out_ref[slot * row : (slot + 1) * row, :] = (grad * slope).astype(jnp.bfloat16)


def conv_rows(pad, start, row, weight_ref):
    sums = []
    for c in range(3):
        total = None
        for r in range(3):
            at = start + (2 - r) * row
            rows = pad[pl.ds(at if isinstance(at, int) else pl.multiple_of(at, 16), row), :]
            term = lax.dot_general(
                rows, weight_ref[r, c], (((1,), (1,)), ((), ())), preferred_element_type=jnp.float32
            )
            total = term if total is None else total + term
        sums.append(total)
    return pltpu.roll(sums[2], 1, 0) + sums[1] + pltpu.roll(sums[0], row - 1, 0)


def four_rows(rows4, core, row, pre_ref, swapped_ref):
    rows4[pl.ds(pl.multiple_of(core * 2 * row, 16), 2 * row), :] = pre_ref[...]
    rows4[pl.ds(pl.multiple_of((1 - core) * 2 * row, 16), 2 * row), :] = swapped_ref[...]


def grad_input_kernel(local, side, flags_ref, pre_ref, swapped_ref, own_ref, weight_ref, out_ref, rows4):
    pitch = side + 2 * GAP
    row = local * pitch
    core = flags_ref[0]
    four_rows(rows4, core, row, pre_ref, swapped_ref)
    grad = conv_rows(rows4, core * row, row, weight_ref)
    for face in range(local):
        at = face * pitch + GAP
        own = own_ref[face].astype(jnp.float32)
        out_ref[face] = (own + grad[at : at + side, :]).astype(jnp.bfloat16)


def grad_first_kernel(row, nxl, per_tile, flags_ref, x_ref, pre_ref, swapped_ref, out_ref, rows4):
    four_rows(rows4, flags_ref[0], row, pre_ref, swapped_ref)
    dests, lines, half = out_ref.shape[0], out_ref.shape[1] // 9, out_ref.shape[2]
    for r in range(3):
        terms = jnp.dot(x_ref[...], rows4[(2 - r) * row : (4 - r) * row, :], preferred_element_type=jnp.float32)
        for c in range(3):
            turned = terms[c * half : (c + 1) * half, :].T
            at = (3 * r + c) * lines
            if nxl == 1:
                for d in range(dests):
                    out_ref[d, at : at + lines] = turned[d * lines : (d + 1) * lines, :].astype(jnp.bfloat16)
                continue
            split = turned.reshape(dests // 2, 2, lines, half)
            left = split[:, 0].reshape(-1, half)
            right = split[:, 1].reshape(-1, half)
            low = lax.broadcasted_iota(jnp.int32, left.shape, 1) % (2 * per_tile) < per_tile
            ones = (
                jnp.where(low, left, pltpu.roll(right, per_tile, 1)),
                jnp.where(low, pltpu.roll(left, half - per_tile, 1), right),
            )
            for xl, one in enumerate(ones):
                for d in range(dests // 2):
                    out_ref[2 * d + xl, at : at + lines] = one[d * lines : (d + 1) * lines, :].astype(jnp.bfloat16)


def kernel(body, out_shape, inputs, smem=0, scratch=(), name=None, flops=0, nbytes=2**20, exps=0, hbm=0, vmem=VMEM):
    many = isinstance(out_shape, tuple)
    spots = [pl.BlockSpec(memory_space=pltpu.HBM)] * hbm + whole(len(inputs) - smem - hbm)
    return pl.pallas_call(
        body,
        out_shape=out_shape,
        in_specs=[pl.BlockSpec(memory_space=pltpu.SMEM)] * smem + spots,
        out_specs=tuple(whole(len(out_shape))) if many else whole(1)[0],
        scratch_shapes=scratch,
        compiler_params=pltpu.CompilerParams(vmem_limit_bytes=vmem),
        cost_estimate=pl.CostEstimate(flops=flops, bytes_accessed=nbytes, transcendentals=exps),
        name=name,
    )(*inputs)


def on_device(sizes, saved_input, saved_pre, cotangent, first_weight, second_weight, seams, corners):
    nxh, ny, nxl, nz, nc = sizes
    nface, ntile, nchip = nxh * ny, nxl * nz * nc, nxl * nz
    x, p, g = saved_input[0, :, 0], saved_pre[0, :, 0], cotangent[0, :, 0]
    local, side, channels = x.shape
    faces = nface * local
    row = local * (side + 2 * GAP)
    bf = jnp.bfloat16
    shape = jax.ShapeDtypeStruct
    core = lax.axis_index("c")
    tile = lax.axis_index(TILE)
    top = tile >= ntile // 2
    near_wraps = (tile == 0) | (tile == ntile - 1)
    far_wraps = (tile == 1) | (tile == ntile - 2)
    flags = jnp.stack([core, *(flag.astype(jnp.int32) for flag in (near_wraps, far_wraps, ~top))])

    px_blocks = 4
    ch_blocks = nface // px_blocks
    px = side // px_blocks
    count = px * 2 // ch_blocks
    sent = kernel(
        functools.partial(pack_kernel, local, side, (px_blocks, ch_blocks)),
        shape((nface, local * (count + CELLS), channels), bf),
        (seams, g, p),
        1,
        (
            pltpu.VMEM((local, side, channels), bf),
            pltpu.VMEM((local, side, channels), bf),
            pltpu.SemaphoreType.DMA((2,)),
        ),
        "pack",
        hbm=2,
        vmem=None,
    )
    swap = lambda a: lax.ppermute(a, "c", [(0, 1), (1, 0)])
    sent, flags, top = lax.optimization_barrier((sent, flags, top))
    table = lax.all_to_all(sent, FACE, 0, 0, tiled=True)

    cells = table[:, local * count :].reshape(faces, CELLS, channels)
    all_seams = cells[:, SEAM_AT, :4].astype(jnp.int32)
    want = jnp.where(top, all_seams[:, 0], all_seams[:, 2])
    picked = kernel(
        functools.partial(pick_kernel, faces, local, count),
        shape((nface, local * count, channels), bf),
        (want, table),
        1,
        name="pick",
    )
    picked, table = lax.optimization_barrier((picked, table))
    wrapped = lax.all_to_all(picked, FACE, 0, 0, tiled=True)

    half = channels // nc
    per_tile = channels // ntile
    own, tails, mine, kept = kernel(
        functools.partial(border_kernel, local, side, (nxl, nz, nc, per_tile)),
        (
            shape((2, local, side + GAP, channels), bf),
            shape((2, local, GAP, channels), bf),
            shape((local, side + GAP + side // 2, channels), bf),
            shape((local * side, half), bf),
        ),
        (flags, seams, corners, table, g, p, x),
        3,
        name="border",
    )
    wrapped, part = lax.optimization_barrier((wrapped, swap(mine)))
    near, far = kernel(
        functools.partial(send_kernel, local, side, (px_blocks, ch_blocks)),
        (shape(own.shape, bf), shape(own.shape[1:], bf)),
        (flags, own, tails, wrapped),
        1,
        name="send",
    )

    pairs = lambda step: [((t + step if t % 2 else t - step) % ntile, t) for t in range(ntile)]
    near = lax.ppermute(near, TILE, pairs(1))
    far = lax.ppermute(far, TILE, pairs(2))
    grad_pre = kernel(
        functools.partial(grad_pre_kernel, local, side),
        shape((2 * row, channels), bf),
        (flags, own, part, near, far, second_weight),
        1,
        (pltpu.VMEM((4 * row, channels), bf), pltpu.VMEM((2 * row, channels), bf)),
        "grad_pre",
        2 * 18 * row * channels**2,
        4 * 2**20,
        2 * row * channels,
    )
    swapped = swap(grad_pre)

    x_turned = kernel(
        functools.partial(turn_kernel, local, side),
        shape((3 * half, 2 * row), bf),
        (flags, kept, part),
        1,
        (pltpu.VMEM((2 * row, half), jnp.float32),),
        "turn",
    )

    rows4 = (pltpu.VMEM((4 * row, channels), bf),)
    width = channels // nface
    lines = width // nxl
    parts = kernel(
        functools.partial(grad_first_kernel, row, nxl, per_tile),
        shape((nface * nxl, 9 * lines, half), bf),
        (flags, x_turned, grad_pre, swapped),
        1,
        rows4,
        "grad_first",
        2 * 18 * half * row * channels,
    )
    grad_input = kernel(
        functools.partial(grad_input_kernel, local, side),
        shape((local, side, channels), bf),
        (flags, grad_pre, swapped, g, first_weight),
        1,
        rows4,
        "grad_input",
        2 * 9 * row * channels**2,
        2 * 2**20,
    )
    scale_factor = 1.0 / math.sqrt(faces * ntile * side)
    got = lax.all_to_all(parts, FACE + ("xl",), 0, 0, tiled=True)
    total = kernel(
        functools.partial(first_sum_kernel, scale_factor),
        shape((nz, nxl * per_tile, 9 * lines), bf),
        (got,),
        name="first_sum",
    )
    got = lax.all_to_all(total, "z", 0, 0, tiled=True)
    first_out = kernel(second_sum_kernel, shape((3, 3, per_tile, width), jnp.float32), (got,), name="second_sum")
    return grad_input.reshape(saved_input.shape), first_out


def solution(mesh, sizes=(2, 4, 2, 16, 2)):
    fine = Mesh(mesh.devices.reshape(sizes), FACE + TILE)
    field = P(None, FACE, TILE, None, None)
    return jax.shard_map(
        functools.partial(on_device, sizes),
        mesh=fine,
        in_specs=(field, field, field, P(), P(), P(FACE, None), P(FACE, None)),
        out_specs=(field, P(None, None, TILE, FACE)),
        check_vma=False,
    )
```

```python
import functools
import math

import jax
import jax.numpy as jnp
import numpy as np
from jax import lax
from jax.experimental import pallas as pl
from jax.experimental.pallas import tpu as pltpu
from jax.sharding import Mesh
from jax.sharding import PartitionSpec as P

FACE = ("xh", "y")
TILE = ("xl", "z", "c")
CHIP = ("xl", "z")
GAP = 16
CELLS = 8
SEAM_AT = 6
VMEM = 40 * 2**20


def whole(n):
    return [pl.BlockSpec(memory_space=pltpu.VMEM)] * n


def pack_kernel(local, side, blocks, seams_ref, g_hbm, p_hbm, out_ref, g_ref, p_ref, sems):
    fetches = [
        pltpu.make_async_copy(g_hbm, g_ref, sems.at[0]),
        pltpu.make_async_copy(p_hbm, p_ref, sems.at[1]),
    ]
    for fetch in fetches:
        fetch.start()
    px_blocks, ch_blocks = blocks
    channels = g_ref.shape[-1]
    px, ch = side // px_blocks, channels // ch_blocks
    count = px * 2 // ch_blocks
    shape = (local * CELLS, local * side)
    line = lax.broadcasted_iota(jnp.int32, shape, 0)
    pixel = lax.broadcasted_iota(jnp.int32, shape, 1)
    cell, base = line % CELLS, line // CELLS * side
    of_g = jnp.where(cell < 2, base + cell, jnp.where(cell < 4, base + side - 4 + cell, -1))
    of_p = jnp.where(cell == 4, base, jnp.where(cell == 5, base + side - 1, -1))
    seams = jnp.zeros((local * CELLS, channels), jnp.float32)
    line = lax.broadcasted_iota(jnp.int32, seams.shape, 0)
    lane = lax.broadcasted_iota(jnp.int32, seams.shape, 1)
    for face in range(local):
        for i in range(4):
            here = (line == face * CELLS + SEAM_AT) & (lane == i)
            seams = jnp.where(here, seams_ref[face, i].astype(jnp.float32), seams)
    take = lambda at, ref: jnp.dot(
        jnp.where(at == pixel, 1.0, 0.0).astype(jnp.bfloat16),
        ref[...].reshape(local * side, channels),
        preferred_element_type=jnp.float32,
    )
    for fetch in fetches:
        fetch.wait()
    cells = (take(of_g, g_ref) + take(of_p, p_ref) + seams).astype(jnp.bfloat16)
    for b in range(px_blocks * ch_blocks):
        i, j = divmod(b, ch_blocks)
        for face in range(local):
            at = face * count
            for which, source in enumerate((g_ref, p_ref)):
                piece = source[face, i * px : (i + 1) * px, j * ch : (j + 1) * ch]
                if ch_blocks == 1:
                    out_ref[b, at + which * px : at + (which + 1) * px] = piece
                else:
                    out_ref[b, at : at + px, which * ch : (which + 1) * ch] = piece
        out_ref[b, local * count :] = cells


def pick_kernel(faces, local, count, want_ref, table_ref, out_ref):
    for i in range(faces):
        face = want_ref[i]
        at = pl.multiple_of(lax.rem(face, local) * count, 16)
        into, row = divmod(i, local)
        out_ref[into, row * count : (row + 1) * count] = table_ref[lax.div(face, local), pl.ds(at, count)]


def first_sum_kernel(scale, got_ref, out_ref):
    total = got_ref[0].astype(jnp.float32)
    for i in range(1, got_ref.shape[0]):
        total = total + got_ref[i].astype(jnp.float32)
    turned = (total * scale).T
    out_ref[...] = turned.reshape(out_ref.shape).astype(jnp.bfloat16)


def second_sum_kernel(got_ref, out_ref):
    total = got_ref[0].astype(jnp.float32)
    for i in range(1, got_ref.shape[0]):
        total = total + got_ref[i].astype(jnp.float32)
    _, _, per_tile, width = out_ref.shape
    lines = total.shape[1] // 9
    for tap in range(9):
        r, c = divmod(tap, 3)
        for h in range(width // lines):
            out_ref[r, c, :, h * lines : (h + 1) * lines] = total[
                h * per_tile : (h + 1) * per_tile, tap * lines : (tap + 1) * lines
            ]


def border_kernel(
    local, side, tiles, flags_ref, seams_ref, corners_ref, table_ref, g_ref, p_ref, x_ref, own_ref, wrap_ref, mine_ref, kept_ref
):
    below = flags_ref[3]
    held = local * CELLS
    cells = table_ref[:, table_ref.shape[1] - held :].reshape(table_ref.shape[0] * held, -1)
    rows, width = 4 * GAP, cells.shape[0]
    row = lax.broadcasted_iota(jnp.int32, (rows, 1), 0)
    spot, block = row % GAP, row // GAP
    of_g = block % 2 == 1
    each = jnp.where(of_g, 4, 2)
    k = spot % each
    cell = jnp.where(of_g, k, jnp.where(spot < 2 * local, 4 + k, -1))
    is_left = k * 2 >= each
    face_at = jnp.zeros((rows, 1), jnp.int32)
    for face in range(local):
        for beyond in range(2):
            if beyond:
                left, right = corners_ref[face, 2 * below], corners_ref[face, 2 * below + 1]
            else:
                left, right = seams_ref[face, 3], seams_ref[face, 1]
            here = (spot // each == face) & (block // 2 == beyond)
            face_at = jnp.where(here, jnp.where(is_left, left, right), face_at)
    index = jnp.where(cell < 0, -1, face_at * CELLS + cell)
    where = lax.broadcasted_iota(jnp.int32, (rows, width), 1) == index
    tails = jnp.dot(
        jnp.where(where, 1.0, 0.0).astype(jnp.bfloat16), cells, preferred_element_type=jnp.float32
    ).astype(jnp.bfloat16)
    full = local * side
    for which, source in enumerate((p_ref, g_ref)):
        at = which * (full + GAP)
        own_ref[at : at + full] = source[...].reshape(full, -1)
        own_ref[at + full : at + full + GAP] = tails[which * GAP : (which + 1) * GAP]
    mine_ref[:full] = g_ref[...].reshape(full, -1)
    mine_ref[full : full + GAP] = tails[GAP : 2 * GAP]
    wrap_ref[...] = tails[2 * GAP :]
    nxl, nz, nc, per_tile = tiles
    channels, half = x_ref.shape[-1], kept_ref.shape[-1]
    line = lax.broadcasted_iota(jnp.int32, (channels, nc * half), 0)
    lane = lax.broadcasted_iota(jnp.int32, (channels, nc * half), 1)
    of_core = jnp.where(lane < half, flags_ref[0], 1 - flags_ref[0])
    place = lane % half
    xl, z = place // per_tile % nxl, place // (per_tile * nxl)
    wanted = ((xl * nz + z) * nc + of_core) * per_tile + place % per_tile
    chosen = jnp.dot(
        x_ref[...].reshape(local * side, channels),
        jnp.where(line == wanted, 1.0, 0.0).astype(jnp.bfloat16),
        preferred_element_type=jnp.float32,
    ).astype(jnp.bfloat16)
    kept_ref[...] = chosen[:, :half]
    for face in range(local):
        for part in range(2):
            at = face * side + part * side // 2
            into = full + GAP + face * side // 2
            mine_ref[into : into + side // 2, part * half : (part + 1) * half] = chosen[at : at + side // 2, half:]


def turn_kernel(local, side, flags_ref, kept_ref, part_ref, out_ref, lines):
    pitch = side + 2 * GAP
    row = local * pitch
    half = kept_ref.shape[-1]
    start = local * side + GAP
    lines[...] = jnp.zeros_like(lines)
    for face in range(local):
        at = pl.multiple_of(flags_ref[0] * row + face * pitch + GAP, 16)
        lines[pl.ds(at, side), :] = kept_ref[face * side : (face + 1) * side].astype(jnp.float32)
        for part in range(2):
            at = pl.multiple_of((1 - flags_ref[0]) * row + face * pitch + GAP + part * side // 2, 16)
            lines[pl.ds(at, side // 2), :] = part_ref[
                start + face * side // 2 : start + (face + 1) * side // 2, part * half : (part + 1) * half
            ].astype(jnp.float32)
    for c in range(3):
        moved = lines[...] if c == 1 else pltpu.roll(lines[...], (1 - c) % (2 * row), 0)
        out_ref[c * half : (c + 1) * half, :] = moved.T.astype(jnp.bfloat16)


def send_kernel(local, side, blocks, flags_ref, own_ref, tails_ref, pieces_ref, near_ref, far_ref):
    px_blocks, ch_blocks = blocks
    px = side // px_blocks
    ch = own_ref.shape[-1] // ch_blocks
    count = px * 2 // ch_blocks
    full = local * side
    near, far = flags_ref[1], flags_ref[2]

    def put_wrap(out, start, of_g):
        for face in range(local):
            for b in range(px_blocks * ch_blocks):
                i, j = divmod(b, ch_blocks)
                piece = pieces_ref[b, face * count : (face + 1) * count]
                which = 0 if of_g else 1
                if ch_blocks == 1:
                    part = piece[which * px : (which + 1) * px]
                else:
                    part = piece[:, which * ch : (which + 1) * ch]
                at = start + face * side + i * px
                out[at : at + px, j * ch : (j + 1) * ch] = part
        tail = GAP if of_g else 0
        out[start + full : start + full + GAP, :] = tails_ref[tail : tail + GAP]

    @pl.when(near == 1)
    def _():
        put_wrap(near_ref, 0, False)
        put_wrap(near_ref, full + GAP, True)

    @pl.when(near == 0)
    def _():
        near_ref[...] = own_ref[...]

    @pl.when(far == 1)
    def _():
        put_wrap(far_ref, 0, True)

    @pl.when(far == 0)
    def _():
        far_ref[...] = own_ref[full + GAP :]


def grad_pre_kernel(local, side, flags_ref, own_ref, part_ref, near_ref, far_ref, weight_ref, out_ref, g_pad, p_pad):
    pitch = side + 2 * GAP
    row = local * pitch
    core = flags_ref[0]

    full = local * side
    line = lax.broadcasted_iota(jnp.int32, (local * GAP, GAP), 0)
    lane = lax.broadcasted_iota(jnp.int32, (local * GAP, GAP), 1)
    spot, at_face = line % GAP, line // GAP
    last = spot - (GAP - 4)
    of_g = jnp.where(spot < 2, spot, jnp.where(spot >= GAP - 2, last, -1)) + jnp.where(
        (spot < 2) | (spot >= GAP - 2), 4 * at_face, 0
    )
    of_p = jnp.where(spot == 0, 2 * at_face, jnp.where(spot == GAP - 1, 2 * at_face + 1, -1))
    spread_g = jnp.where(lane == of_g, 1.0, 0.0).astype(jnp.bfloat16)
    spread_p = jnp.where(lane == of_p, 1.0, 0.0).astype(jnp.bfloat16)

    def put(pad, slot, source, start, spread):
        tails = source[start + full : start + full + GAP, :]
        borders = jnp.dot(spread, tails, preferred_element_type=jnp.float32).astype(jnp.bfloat16)
        for face in range(local):
            at = pl.multiple_of(slot * row + face * pitch, 16)
            border = borders[face * GAP : (face + 1) * GAP]
            pad[pl.ds(at, GAP), :] = border
            pad[pl.ds(at + GAP, side), :] = source[start + face * side : start + (face + 1) * side, :]
            pad[pl.ds(at + GAP + side, GAP), :] = border

    second = full + GAP
    for role, (source, start) in enumerate(((far_ref, 0), (near_ref, second), (own_ref, second), (part_ref, 0))):
        put(g_pad, jnp.where(core == 0, role, 3 - role), source, start, spread_g)
    for role, source in enumerate((near_ref, own_ref)):
        put(p_pad, jnp.where(core == 0, role, 1 - role), source, 0, spread_p)
    for slot in range(2):
        grad = conv_rows(g_pad, slot * row, row, weight_ref)
        pre = p_pad[slot * row : (slot + 1) * row, :].astype(jnp.float32)
        logistic = jax.nn.sigmoid(pre)
        slope = logistic * (1.0 + pre * (1.0 - logistic))
        out_ref[slot * row : (slot + 1) * row, :] = (grad * slope).astype(jnp.bfloat16)


def conv_rows(pad, start, row, weight_ref):
    sums = []
    for c in range(3):
        total = None
        for r in range(3):
            at = start + (2 - r) * row
            rows = pad[pl.ds(at if isinstance(at, int) else pl.multiple_of(at, 16), row), :]
            term = lax.dot_general(
                rows, weight_ref[r, c], (((1,), (1,)), ((), ())), preferred_element_type=jnp.float32
            )
            total = term if total is None else total + term
        sums.append(total)
    return pltpu.roll(sums[2], 1, 0) + sums[1] + pltpu.roll(sums[0], row - 1, 0)


def four_rows(rows4, core, row, pre_ref, swapped_ref):
    rows4[pl.ds(pl.multiple_of(core * 2 * row, 16), 2 * row), :] = pre_ref[...]
    rows4[pl.ds(pl.multiple_of((1 - core) * 2 * row, 16), 2 * row), :] = swapped_ref[...]


def grad_input_kernel(local, side, flags_ref, pre_ref, swapped_ref, own_ref, weight_ref, out_ref, rows4):
    pitch = side + 2 * GAP
    row = local * pitch
    core = flags_ref[0]
    four_rows(rows4, core, row, pre_ref, swapped_ref)
    grad = conv_rows(rows4, core * row, row, weight_ref)
    for face in range(local):
        at = face * pitch + GAP
        own = own_ref[face].astype(jnp.float32)
        out_ref[face] = (own + grad[at : at + side, :]).astype(jnp.bfloat16)


def grad_first_kernel(row, nxl, per_tile, flags_ref, x_ref, pre_ref, swapped_ref, out_ref, rows4):
    four_rows(rows4, flags_ref[0], row, pre_ref, swapped_ref)
    dests, lines, half = out_ref.shape[0], out_ref.shape[1] // 9, out_ref.shape[2]
    for r in range(3):
        terms = jnp.dot(x_ref[...], rows4[(2 - r) * row : (4 - r) * row, :], preferred_element_type=jnp.float32)
        for c in range(3):
            turned = terms[c * half : (c + 1) * half, :].T
            at = (3 * r + c) * lines
            if nxl == 1:
                for d in range(dests):
                    out_ref[d, at : at + lines] = turned[d * lines : (d + 1) * lines, :].astype(jnp.bfloat16)
                continue
            split = turned.reshape(dests // 2, 2, lines, half)
            left = split[:, 0].reshape(-1, half)
            right = split[:, 1].reshape(-1, half)
            low = lax.broadcasted_iota(jnp.int32, left.shape, 1) % (2 * per_tile) < per_tile
            ones = (
                jnp.where(low, left, pltpu.roll(right, per_tile, 1)),
                jnp.where(low, pltpu.roll(left, half - per_tile, 1), right),
            )
            for xl, one in enumerate(ones):
                for d in range(dests // 2):
                    out_ref[2 * d + xl, at : at + lines] = one[d * lines : (d + 1) * lines, :].astype(jnp.bfloat16)


def kernel(body, out_shape, inputs, smem=0, scratch=(), name=None, flops=0, nbytes=2**20, exps=0, hbm=0, vmem=VMEM):
    many = isinstance(out_shape, tuple)
    spots = [pl.BlockSpec(memory_space=pltpu.HBM)] * hbm + whole(len(inputs) - smem - hbm)
    return pl.pallas_call(
        body,
        out_shape=out_shape,
        in_specs=[pl.BlockSpec(memory_space=pltpu.SMEM)] * smem + spots,
        out_specs=tuple(whole(len(out_shape))) if many else whole(1)[0],
        scratch_shapes=scratch,
        compiler_params=pltpu.CompilerParams(vmem_limit_bytes=vmem),
        cost_estimate=pl.CostEstimate(flops=flops, bytes_accessed=nbytes, transcendentals=exps),
        name=name,
    )(*inputs)


def on_device(sizes, saved_input, saved_pre, cotangent, first_weight, second_weight, seams, corners):
    nxh, ny, nxl, nz, nc = sizes
    nface, ntile, nchip = nxh * ny, nxl * nz * nc, nxl * nz
    x, p, g = saved_input[0, :, 0], saved_pre[0, :, 0], cotangent[0, :, 0]
    local, side, channels = x.shape
    faces = nface * local
    row = local * (side + 2 * GAP)
    bf = jnp.bfloat16
    shape = jax.ShapeDtypeStruct
    core = lax.axis_index("c")
    tile = lax.axis_index(TILE)
    top = tile >= ntile // 2
    near_wraps = (tile == 0) | (tile == ntile - 1)
    far_wraps = (tile == 1) | (tile == ntile - 2)
    flags = jnp.stack([core, *(flag.astype(jnp.int32) for flag in (near_wraps, far_wraps, ~top))])

    px_blocks = 4
    ch_blocks = nface // px_blocks
    px = side // px_blocks
    count = px * 2 // ch_blocks
    sent = kernel(
        functools.partial(pack_kernel, local, side, (px_blocks, ch_blocks)),
        shape((nface, local * (count + CELLS), channels), bf),
        (seams, g, p),
        1,
        (
            pltpu.VMEM((local, side, channels), bf),
            pltpu.VMEM((local, side, channels), bf),
            pltpu.SemaphoreType.DMA((2,)),
        ),
        "pack",
        hbm=2,
        vmem=None,
    )
    swap = lambda a: lax.ppermute(a, "c", [(0, 1), (1, 0)])
    sent, flags, top = lax.optimization_barrier((sent, flags, top))
    table = lax.all_to_all(sent, FACE, 0, 0, tiled=True)

    cells = table[:, local * count :].reshape(faces, CELLS, channels)
    all_seams = cells[:, SEAM_AT, :4].astype(jnp.int32)
    want = jnp.where(top, all_seams[:, 0], all_seams[:, 2])
    picked = kernel(
        functools.partial(pick_kernel, faces, local, count),
        shape((nface, local * count, channels), bf),
        (want, table),
        1,
        name="pick",
    )
    picked, table = lax.optimization_barrier((picked, table))
    wrapped = lax.all_to_all(picked, FACE, 0, 0, tiled=True)

    half = channels // nc
    per_tile = channels // ntile
    own, tails, mine, kept = kernel(
        functools.partial(border_kernel, local, side, (nxl, nz, nc, per_tile)),
        (
            shape((2 * (local * side + GAP), channels), bf),
            shape((2 * GAP, channels), bf),
            shape((local * side + GAP + local * side // 2, channels), bf),
            shape((local * side, half), bf),
        ),
        (flags, seams, corners, table, g, p, x),
        3,
        name="border",
    )
    wrapped, part = lax.optimization_barrier((wrapped, swap(mine)))
    near, far = kernel(
        functools.partial(send_kernel, local, side, (px_blocks, ch_blocks)),
        (shape(own.shape, bf), shape((own.shape[0] // 2, channels), bf)),
        (flags, own, tails, wrapped),
        1,
        name="send",
    )

    pairs = lambda step: [((t + step if t % 2 else t - step) % ntile, t) for t in range(ntile)]
    near = lax.ppermute(near, TILE, pairs(1))
    far = lax.ppermute(far, TILE, pairs(2))
    grad_pre = kernel(
        functools.partial(grad_pre_kernel, local, side),
        shape((2 * row, channels), bf),
        (flags, own, part, near, far, second_weight),
        1,
        (pltpu.VMEM((4 * row, channels), bf), pltpu.VMEM((2 * row, channels), bf)),
        "grad_pre",
        2 * 18 * row * channels**2,
        4 * 2**20,
        2 * row * channels,
    )
    swapped = swap(grad_pre)

    x_turned = kernel(
        functools.partial(turn_kernel, local, side),
        shape((3 * half, 2 * row), bf),
        (flags, kept, part),
        1,
        (pltpu.VMEM((2 * row, half), jnp.float32),),
        "turn",
    )

    rows4 = (pltpu.VMEM((4 * row, channels), bf),)
    width = channels // nface
    lines = width // nxl
    parts = kernel(
        functools.partial(grad_first_kernel, row, nxl, per_tile),
        shape((nface * nxl, 9 * lines, half), bf),
        (flags, x_turned, grad_pre, swapped),
        1,
        rows4,
        "grad_first",
        2 * 18 * half * row * channels,
    )
    grad_input = kernel(
        functools.partial(grad_input_kernel, local, side),
        shape((local, side, channels), bf),
        (flags, grad_pre, swapped, g, first_weight),
        1,
        rows4,
        "grad_input",
        2 * 9 * row * channels**2,
        2 * 2**20,
    )
    scale_factor = 1.0 / math.sqrt(faces * ntile * side)
    got = lax.all_to_all(parts, FACE + ("xl",), 0, 0, tiled=True)
    total = kernel(
        functools.partial(first_sum_kernel, scale_factor),
        shape((nz, nxl * per_tile, 9 * lines), bf),
        (got,),
        name="first_sum",
    )
    got = lax.all_to_all(total, "z", 0, 0, tiled=True)
    first_out = kernel(second_sum_kernel, shape((3, 3, per_tile, width), jnp.float32), (got,), name="second_sum")
    return grad_input.reshape(saved_input.shape), first_out


def solution(mesh, sizes=(2, 4, 2, 16, 2)):
    fine = Mesh(mesh.devices.reshape(sizes), FACE + TILE)
    field = P(None, FACE, TILE, None, None)
    return jax.shard_map(
        functools.partial(on_device, sizes),
        mesh=fine,
        in_specs=(field, field, field, P(), P(), P(FACE, None), P(FACE, None)),
        out_specs=(field, P(None, None, TILE, FACE)),
        check_vma=False,
    )
```

```python
import functools
import math

import jax
import jax.numpy as jnp
import numpy as np
from jax import lax
from jax.experimental import pallas as pl
from jax.experimental.pallas import tpu as pltpu
from jax.sharding import Mesh
from jax.sharding import PartitionSpec as P

FACE = ("xh", "y")
TILE = ("xl", "z", "c")
CHIP = ("xl", "z")
GAP = 16
CELLS = 8
SEAM_AT = 6
VMEM = 40 * 2**20


def whole(n):
    return [pl.BlockSpec(memory_space=pltpu.VMEM)] * n


def pack_kernel(local, side, blocks, seams_ref, g_hbm, p_hbm, out_ref, g_ref, p_ref, sems):
    fetches = [
        pltpu.make_async_copy(g_hbm, g_ref, sems.at[0]),
        pltpu.make_async_copy(p_hbm, p_ref, sems.at[1]),
    ]
    for fetch in fetches:
        fetch.start()
    px_blocks, ch_blocks = blocks
    channels = g_ref.shape[-1]
    px, ch = side // px_blocks, channels // ch_blocks
    count = px * 2 // ch_blocks
    shape = (local * CELLS, local * side)
    line = lax.broadcasted_iota(jnp.int32, shape, 0)
    pixel = lax.broadcasted_iota(jnp.int32, shape, 1)
    cell, base = line % CELLS, line // CELLS * side
    of_g = jnp.where(cell < 2, base + cell, jnp.where(cell < 4, base + side - 4 + cell, -1))
    of_p = jnp.where(cell == 4, base, jnp.where(cell == 5, base + side - 1, -1))
    seams = jnp.zeros((local * CELLS, channels), jnp.float32)
    line = lax.broadcasted_iota(jnp.int32, seams.shape, 0)
    lane = lax.broadcasted_iota(jnp.int32, seams.shape, 1)
    for face in range(local):
        for i in range(4):
            here = (line == face * CELLS + SEAM_AT) & (lane == i)
            seams = jnp.where(here, seams_ref[face, i].astype(jnp.float32), seams)
    take = lambda at, ref: jnp.dot(
        jnp.where(at == pixel, 1.0, 0.0).astype(jnp.bfloat16),
        ref[...].reshape(local * side, channels),
        preferred_element_type=jnp.float32,
    )
    for fetch in fetches:
        fetch.wait()
    cells = (take(of_g, g_ref) + take(of_p, p_ref) + seams).astype(jnp.bfloat16)
    for b in range(px_blocks * ch_blocks):
        i, j = divmod(b, ch_blocks)
        for face in range(local):
            at = face * count
            for which, source in enumerate((g_ref, p_ref)):
                piece = source[face, i * px : (i + 1) * px, j * ch : (j + 1) * ch]
                if ch_blocks == 1:
                    out_ref[b, at + which * px : at + (which + 1) * px] = piece
                else:
                    out_ref[b, at : at + px, which * ch : (which + 1) * ch] = piece
        out_ref[b, local * count :] = cells


def pick_kernel(faces, local, count, want_ref, table_ref, out_ref):
    for i in range(faces):
        face = want_ref[i]
        at = pl.multiple_of(lax.rem(face, local) * count, 16)
        into, row = divmod(i, local)
        out_ref[into, row * count : (row + 1) * count] = table_ref[lax.div(face, local), pl.ds(at, count)]


def first_sum_kernel(scale, got_ref, out_ref):
    total = got_ref[0].astype(jnp.float32)
    for i in range(1, got_ref.shape[0]):
        total = total + got_ref[i].astype(jnp.float32)
    turned = (total * scale).T
    out_ref[...] = turned.reshape(out_ref.shape).astype(jnp.bfloat16)


def second_sum_kernel(got_ref, out_ref):
    total = got_ref[0].astype(jnp.float32)
    for i in range(1, got_ref.shape[0]):
        total = total + got_ref[i].astype(jnp.float32)
    _, _, per_tile, width = out_ref.shape
    lines = total.shape[1] // 9
    for tap in range(9):
        r, c = divmod(tap, 3)
        for h in range(width // lines):
            out_ref[r, c, :, h * lines : (h + 1) * lines] = total[
                h * per_tile : (h + 1) * per_tile, tap * lines : (tap + 1) * lines
            ]


def border_kernel(
    local, side, tiles, flags_ref, seams_ref, corners_ref, table_ref, g_ref, p_ref, x_ref, own_ref, wrap_ref, mine_ref, kept_ref
):
    below = flags_ref[3]
    held = local * CELLS
    cells = table_ref[:, table_ref.shape[1] - held :].reshape(table_ref.shape[0] * held, -1)
    rows, width = 4 * GAP, cells.shape[0]
    row = lax.broadcasted_iota(jnp.int32, (rows, 1), 0)
    spot, block = row % GAP, row // GAP
    of_g = block % 2 == 1
    each = jnp.where(of_g, 4, 2)
    k = spot % each
    cell = jnp.where(of_g, k, jnp.where(spot < 2 * local, 4 + k, -1))
    is_left = k * 2 >= each
    face_at = jnp.zeros((rows, 1), jnp.int32)
    for face in range(local):
        for beyond in range(2):
            if beyond:
                left, right = corners_ref[face, 2 * below], corners_ref[face, 2 * below + 1]
            else:
                left, right = seams_ref[face, 3], seams_ref[face, 1]
            here = (spot // each == face) & (block // 2 == beyond)
            face_at = jnp.where(here, jnp.where(is_left, left, right), face_at)
    index = jnp.where(cell < 0, -1, face_at * CELLS + cell)
    where = lax.broadcasted_iota(jnp.int32, (rows, width), 1) == index
    tails = jnp.dot(
        jnp.where(where, 1.0, 0.0).astype(jnp.bfloat16), cells, preferred_element_type=jnp.float32
    ).astype(jnp.bfloat16)
    full = local * side
    for which, source in enumerate((p_ref, g_ref)):
        at = which * (full + GAP)
        own_ref[at : at + full] = source[...].reshape(full, -1)
        own_ref[at + full : at + full + GAP] = tails[which * GAP : (which + 1) * GAP]
    mine_ref[:full] = g_ref[...].reshape(full, -1)
    mine_ref[full : full + GAP] = tails[GAP : 2 * GAP]
    wrap_ref[...] = tails[2 * GAP :]
    nxl, nz, nc, per_tile = tiles
    channels, half = x_ref.shape[-1], kept_ref.shape[-1]
    line = lax.broadcasted_iota(jnp.int32, (channels, nc * half), 0)
    lane = lax.broadcasted_iota(jnp.int32, (channels, nc * half), 1)
    of_core = jnp.where(lane < half, flags_ref[0], 1 - flags_ref[0])
    place = lane % half
    xl, z = place // per_tile % nxl, place // (per_tile * nxl)
    wanted = ((xl * nz + z) * nc + of_core) * per_tile + place % per_tile
    chosen = jnp.dot(
        x_ref[...].reshape(local * side, channels),
        jnp.where(line == wanted, 1.0, 0.0).astype(jnp.bfloat16),
        preferred_element_type=jnp.float32,
    ).astype(jnp.bfloat16)
    kept_ref[...] = chosen[:, :half]
    for face in range(local):
        for part in range(2):
            at = face * side + part * side // 2
            into = full + GAP + face * side // 2
            mine_ref[into : into + side // 2, part * half : (part + 1) * half] = chosen[at : at + side // 2, half:]


def turn_kernel(local, side, flags_ref, kept_ref, part_ref, out_ref, lines):
    pitch = side + 2 * GAP
    row = local * pitch
    half = kept_ref.shape[-1]
    start = local * side + GAP
    lines[...] = jnp.zeros_like(lines)
    for face in range(local):
        at = pl.multiple_of(flags_ref[0] * row + face * pitch + GAP, 16)
        lines[pl.ds(at, side), :] = kept_ref[face * side : (face + 1) * side].astype(jnp.float32)
        for part in range(2):
            at = pl.multiple_of((1 - flags_ref[0]) * row + face * pitch + GAP + part * side // 2, 16)
            lines[pl.ds(at, side // 2), :] = part_ref[
                start + face * side // 2 : start + (face + 1) * side // 2, part * half : (part + 1) * half
            ].astype(jnp.float32)
    for c in range(3):
        moved = lines[...] if c == 1 else pltpu.roll(lines[...], (1 - c) % (2 * row), 0)
        out_ref[c * half : (c + 1) * half, :] = moved.T.astype(jnp.bfloat16)


def send_kernel(local, side, blocks, flags_ref, own_ref, tails_ref, pieces_ref, near_ref, far_ref):
    px_blocks, ch_blocks = blocks
    px = side // px_blocks
    ch = own_ref.shape[-1] // ch_blocks
    count = px * 2 // ch_blocks
    full = local * side
    near, far = flags_ref[1], flags_ref[2]

    def put_wrap(out, start, of_g):
        for face in range(local):
            for b in range(px_blocks * ch_blocks):
                i, j = divmod(b, ch_blocks)
                piece = pieces_ref[b, face * count : (face + 1) * count]
                which = 0 if of_g else 1
                if ch_blocks == 1:
                    part = piece[which * px : (which + 1) * px]
                else:
                    part = piece[:, which * ch : (which + 1) * ch]
                at = start + face * side + i * px
                out[at : at + px, j * ch : (j + 1) * ch] = part
        tail = GAP if of_g else 0
        out[start + full : start + full + GAP, :] = tails_ref[tail : tail + GAP]

    @pl.when(near == 1)
    def _():
        put_wrap(near_ref, 0, False)
        put_wrap(near_ref, full + GAP, True)

    @pl.when(near == 0)
    def _():
        near_ref[...] = own_ref[...]

    @pl.when(far == 1)
    def _():
        put_wrap(far_ref, 0, True)

    @pl.when(far == 0)
    def _():
        far_ref[...] = own_ref[full + GAP :]


def put_row(pad, local, side, source, start, each):
    pitch = side + 2 * GAP
    full = local * side
    line = lax.broadcasted_iota(jnp.int32, (local * GAP, GAP), 0)
    lane = lax.broadcasted_iota(jnp.int32, (local * GAP, GAP), 1)
    spot, at_face = line % GAP, line // GAP
    n = each // 2
    k = jnp.where(spot < n, spot, jnp.where(spot >= GAP - n, spot - (GAP - each), GAP))
    spread = jnp.where(lane == k + each * at_face, 1.0, 0.0)
    spread = jnp.where(k < each, spread, 0.0).astype(jnp.bfloat16)
    tails = source[start + full : start + full + GAP, :]
    borders = jnp.dot(spread, tails, preferred_element_type=jnp.float32).astype(jnp.bfloat16)
    for face in range(local):
        at = face * pitch
        border = borders[face * GAP : (face + 1) * GAP]
        pad[at : at + GAP, :] = border
        pad[at + GAP : at + GAP + side, :] = source[start + face * side : start + (face + 1) * side, :]
        pad[at + GAP + side : at + pitch, :] = border


def row_taps(pairs, row):
    sums = []
    for c in range(3):
        total = None
        for rows, weight in pairs:
            term = lax.dot_general(
                rows, weight(c), (((1,), (1,)), ((), ())), preferred_element_type=jnp.float32
            )
            total = term if total is None else total + term
        sums.append(total)
    return pltpu.roll(sums[2], 1, 0) + sums[1] + pltpu.roll(sums[0], row - 1, 0)


def silu_slope(pre):
    pre = pre.astype(jnp.float32)
    logistic = jax.nn.sigmoid(pre)
    return logistic * (1.0 + pre * (1.0 - logistic))


def near_half_kernel(local, side, flags_ref, own_ref, part_ref, weight_ref, hidden_ref, slope_ref, own_pad, part_pad, pre_pad):
    row = own_pad.shape[0]
    toward = 2 * flags_ref[0]
    second = local * side + GAP
    put_row(own_pad, local, side, own_ref, second, 4)
    put_row(part_pad, local, side, part_ref, 0, 4)
    put_row(pre_pad, local, side, own_ref, 0, 2)
    own, part = own_pad[...], part_pad[...]
    hidden_ref[:row] = row_taps([(own, lambda c: weight_ref[toward, c])], row)
    hidden_ref[row:] = row_taps([(own, lambda c: weight_ref[1, c]), (part, lambda c: weight_ref[toward, c])], row)
    slope_ref[...] = silu_slope(pre_pad[...])


def grad_pre_kernel(local, side, flags_ref, near_ref, far_ref, hidden_ref, slope_ref, weight_ref, out_ref, near_pad, far_pad, pre_pad):
    row = near_pad.shape[0]
    core = flags_ref[0]
    away = 2 - 2 * core
    second = local * side + GAP
    put_row(near_pad, local, side, near_ref, second, 4)
    put_row(far_pad, local, side, far_ref, 0, 4)
    put_row(pre_pad, local, side, near_ref, 0, 2)
    near, far = near_pad[...], far_pad[...]
    outer = hidden_ref[:row] + row_taps(
        [(far, lambda c: weight_ref[away, c]), (near, lambda c: weight_ref[1, c])], row
    )
    inner = hidden_ref[row:] + row_taps([(near, lambda c: weight_ref[away, c])], row)
    outer = (outer * silu_slope(pre_pad[...])).astype(jnp.bfloat16)
    inner = (inner * slope_ref[...]).astype(jnp.bfloat16)
    out_ref[pl.ds(pl.multiple_of(core * row, 16), row), :] = outer
    out_ref[pl.ds(pl.multiple_of((1 - core) * row, 16), row), :] = inner


def conv_rows(pad, start, row, weight_ref):
    sums = []
    for c in range(3):
        total = None
        for r in range(3):
            at = start + (2 - r) * row
            rows = pad[pl.ds(at if isinstance(at, int) else pl.multiple_of(at, 16), row), :]
            term = lax.dot_general(
                rows, weight_ref[r, c], (((1,), (1,)), ((), ())), preferred_element_type=jnp.float32
            )
            total = term if total is None else total + term
        sums.append(total)
    return pltpu.roll(sums[2], 1, 0) + sums[1] + pltpu.roll(sums[0], row - 1, 0)


def four_rows(rows4, core, row, pre_ref, swapped_ref):
    rows4[pl.ds(pl.multiple_of(core * 2 * row, 16), 2 * row), :] = pre_ref[...]
    rows4[pl.ds(pl.multiple_of((1 - core) * 2 * row, 16), 2 * row), :] = swapped_ref[...]


def grad_input_kernel(local, side, flags_ref, pre_ref, swapped_ref, own_ref, weight_ref, out_ref, rows4):
    pitch = side + 2 * GAP
    row = local * pitch
    core = flags_ref[0]
    four_rows(rows4, core, row, pre_ref, swapped_ref)
    grad = conv_rows(rows4, core * row, row, weight_ref)
    for face in range(local):
        at = face * pitch + GAP
        own = own_ref[face].astype(jnp.float32)
        out_ref[face] = (own + grad[at : at + side, :]).astype(jnp.bfloat16)


def emit(out_ref, start, terms, nxl, per_tile):
    dests, half = out_ref.shape[0], out_ref.shape[2]
    lines = terms.shape[1] // dests
    for c in range(3):
        turned = terms[c * half : (c + 1) * half, :].T
        at = pl.multiple_of(start + c * lines, 16)
        if nxl == 1:
            for d in range(dests):
                out_ref[d, pl.ds(at, lines)] = turned[d * lines : (d + 1) * lines, :].astype(jnp.bfloat16)
            continue
        split = turned.reshape(dests // 2, 2, lines, half)
        left = split[:, 0].reshape(-1, half)
        right = split[:, 1].reshape(-1, half)
        low = lax.broadcasted_iota(jnp.int32, left.shape, 1) % (2 * per_tile) < per_tile
        ones = (
            jnp.where(low, left, pltpu.roll(right, per_tile, 1)),
            jnp.where(low, pltpu.roll(left, half - per_tile, 1), right),
        )
        for xl, one in enumerate(ones):
            for d in range(dests // 2):
                out_ref[2 * d + xl, pl.ds(at, lines)] = one[d * lines : (d + 1) * lines, :].astype(jnp.bfloat16)


def first_half_kernel(row, nxl, per_tile, flags_ref, x_ref, pre_ref, out_ref, middle_ref):
    core = flags_ref[0]
    lanes = pl.ds(pl.multiple_of(core * row, 128), row)
    rows = pl.ds(pl.multiple_of((1 - core) * row, 16), row)
    middle_ref[...] = jnp.dot(x_ref[:, lanes], pre_ref[rows, :], preferred_element_type=jnp.float32)
    emit(out_ref, 0, jnp.dot(x_ref[...], pre_ref[...], preferred_element_type=jnp.float32), nxl, per_tile)


def grad_first_kernel(row, nxl, per_tile, flags_ref, x_ref, swapped_ref, done_ref, middle_ref, out_ref):
    core = flags_ref[0]
    lanes = pl.ds(pl.multiple_of((1 - core) * row, 128), row)
    rows = pl.ds(pl.multiple_of(core * row, 16), row)
    count = done_ref.shape[1]
    emit(
        out_ref,
        count,
        middle_ref[...] + jnp.dot(x_ref[:, lanes], swapped_ref[rows, :], preferred_element_type=jnp.float32),
        nxl,
        per_tile,
    )
    terms = jnp.dot(x_ref[...], swapped_ref[...], preferred_element_type=jnp.float32)
    emit(out_ref, core * 2 * count, terms, nxl, per_tile)
    at = pl.multiple_of((1 - core) * 2 * count, 16)
    for d in range(done_ref.shape[0]):
        out_ref[d, pl.ds(at, count)] = done_ref[d]


def kernel(body, out_shape, inputs, smem=0, scratch=(), name=None, flops=0, nbytes=2**20, exps=0, hbm=0, vmem=VMEM):
    many = isinstance(out_shape, tuple)
    spots = [pl.BlockSpec(memory_space=pltpu.HBM)] * hbm + whole(len(inputs) - smem - hbm)
    return pl.pallas_call(
        body,
        out_shape=out_shape,
        in_specs=[pl.BlockSpec(memory_space=pltpu.SMEM)] * smem + spots,
        out_specs=tuple(whole(len(out_shape))) if many else whole(1)[0],
        scratch_shapes=scratch,
        compiler_params=pltpu.CompilerParams(vmem_limit_bytes=vmem),
        cost_estimate=pl.CostEstimate(flops=flops, bytes_accessed=nbytes, transcendentals=exps),
        name=name,
    )(*inputs)


def on_device(sizes, saved_input, saved_pre, cotangent, first_weight, second_weight, seams, corners):
    nxh, ny, nxl, nz, nc = sizes
    nface, ntile, nchip = nxh * ny, nxl * nz * nc, nxl * nz
    x, p, g = saved_input[0, :, 0], saved_pre[0, :, 0], cotangent[0, :, 0]
    local, side, channels = x.shape
    faces = nface * local
    row = local * (side + 2 * GAP)
    bf = jnp.bfloat16
    shape = jax.ShapeDtypeStruct
    core = lax.axis_index("c")
    tile = lax.axis_index(TILE)
    top = tile >= ntile // 2
    near_wraps = (tile == 0) | (tile == ntile - 1)
    far_wraps = (tile == 1) | (tile == ntile - 2)
    flags = jnp.stack([core, *(flag.astype(jnp.int32) for flag in (near_wraps, far_wraps, ~top))])

    px_blocks = 4
    ch_blocks = nface // px_blocks
    px = side // px_blocks
    count = px * 2 // ch_blocks
    sent = kernel(
        functools.partial(pack_kernel, local, side, (px_blocks, ch_blocks)),
        shape((nface, local * (count + CELLS), channels), bf),
        (seams, g, p),
        1,
        (
            pltpu.VMEM((local, side, channels), bf),
            pltpu.VMEM((local, side, channels), bf),
            pltpu.SemaphoreType.DMA((2,)),
        ),
        "pack",
        hbm=2,
        vmem=None,
    )
    swap = lambda a: lax.ppermute(a, "c", [(0, 1), (1, 0)])
    sent, flags, top = lax.optimization_barrier((sent, flags, top))
    table = lax.all_to_all(sent, FACE, 0, 0, tiled=True)

    cells = table[:, local * count :].reshape(faces, CELLS, channels)
    all_seams = cells[:, SEAM_AT, :4].astype(jnp.int32)
    want = jnp.where(top, all_seams[:, 0], all_seams[:, 2])
    picked = kernel(
        functools.partial(pick_kernel, faces, local, count),
        shape((nface, local * count, channels), bf),
        (want, table),
        1,
        name="pick",
    )
    picked, table = lax.optimization_barrier((picked, table))
    wrapped = lax.all_to_all(picked, FACE, 0, 0, tiled=True)

    half = channels // nc
    per_tile = channels // ntile
    own, tails, mine, kept = kernel(
        functools.partial(border_kernel, local, side, (nxl, nz, nc, per_tile)),
        (
            shape((2 * (local * side + GAP), channels), bf),
            shape((2 * GAP, channels), bf),
            shape((local * side + GAP + local * side // 2, channels), bf),
            shape((local * side, half), bf),
        ),
        (flags, seams, corners, table, g, p, x),
        3,
        name="border",
    )
    wrapped, part = lax.optimization_barrier((wrapped, swap(mine)))
    near, far = kernel(
        functools.partial(send_kernel, local, side, (px_blocks, ch_blocks)),
        (shape(own.shape, bf), shape((own.shape[0] // 2, channels), bf)),
        (flags, own, tails, wrapped),
        1,
        name="send",
    )

    pairs = lambda step: [((t + step if t % 2 else t - step) % ntile, t) for t in range(ntile)]
    near = lax.ppermute(near, TILE, pairs(1))
    far = lax.ppermute(far, TILE, pairs(2))
    x_turned = kernel(
        functools.partial(turn_kernel, local, side),
        shape((3 * half, 2 * row), bf),
        (flags, kept, part),
        1,
        (pltpu.VMEM((2 * row, half), jnp.float32),),
        "turn",
    )

    pads = tuple(pltpu.VMEM((row, channels), bf) for _ in range(3))
    hidden, slope = kernel(
        functools.partial(near_half_kernel, local, side),
        (shape((2 * row, channels), jnp.float32), shape((row, channels), jnp.float32)),
        (flags, own, part, second_weight),
        1,
        pads,
        "near_half",
        2 * 9 * row * channels**2,
        2 * 2**20,
        row * channels,
    )
    near, far, x_turned, hidden, slope = lax.optimization_barrier((near, far, x_turned, hidden, slope))
    grad_pre = kernel(
        functools.partial(grad_pre_kernel, local, side),
        shape((2 * row, channels), bf),
        (flags, near, far, hidden, slope, second_weight),
        1,
        pads,
        "grad_pre",
        2 * 9 * row * channels**2,
        4 * 2**20,
        row * channels,
    )
    swapped = swap(grad_pre)

    rows4 = (pltpu.VMEM((4 * row, channels), bf),)
    width = channels // nface
    lines = width // nxl
    done, middle = kernel(
        functools.partial(first_half_kernel, row, nxl, per_tile),
        (shape((nface * nxl, 3 * lines, half), bf), shape((3 * half, channels), jnp.float32)),
        (flags, x_turned, grad_pre),
        1,
        name="first_half",
    )
    swapped, done, middle = lax.optimization_barrier((swapped, done, middle))
    parts = kernel(
        functools.partial(grad_first_kernel, row, nxl, per_tile),
        shape((nface * nxl, 9 * lines, half), bf),
        (flags, x_turned, swapped, done, middle),
        1,
        name="grad_first",
        flops=2 * 9 * half * row * channels,
    )
    grad_input = kernel(
        functools.partial(grad_input_kernel, local, side),
        shape((local, side, channels), bf),
        (flags, grad_pre, swapped, g, first_weight),
        1,
        rows4,
        "grad_input",
        2 * 9 * row * channels**2,
        2 * 2**20,
    )
    scale_factor = 1.0 / math.sqrt(faces * ntile * side)
    got = lax.all_to_all(parts, FACE + ("xl",), 0, 0, tiled=True)
    total = kernel(
        functools.partial(first_sum_kernel, scale_factor),
        shape((nz, nxl * per_tile, 9 * lines), bf),
        (got,),
        name="first_sum",
    )
    got = lax.all_to_all(total, "z", 0, 0, tiled=True)
    first_out = kernel(second_sum_kernel, shape((3, 3, per_tile, width), jnp.float32), (got,), name="second_sum")
    return grad_input.reshape(saved_input.shape), first_out


def solution(mesh, sizes=(2, 4, 2, 16, 2)):
    fine = Mesh(mesh.devices.reshape(sizes), FACE + TILE)
    field = P(None, FACE, TILE, None, None)
    return jax.shard_map(
        functools.partial(on_device, sizes),
        mesh=fine,
        in_specs=(field, field, field, P(), P(), P(FACE, None), P(FACE, None)),
        out_specs=(field, P(None, None, TILE, FACE)),
        check_vma=False,
    )
```

```python
import functools
import math

import jax
import jax.numpy as jnp
import numpy as np
from jax import lax
from jax.experimental import pallas as pl
from jax.experimental.pallas import tpu as pltpu
from jax.sharding import Mesh
from jax.sharding import PartitionSpec as P

FACE = ("xh", "y")
TILE = ("xl", "z", "c")
CHIP = ("xl", "z")
GAP = 16
CELLS = 8
SEAM_AT = 6
VMEM = 40 * 2**20


def whole(n):
    return [pl.BlockSpec(memory_space=pltpu.VMEM)] * n


def leave(built, out_hbm, sems, b):
    return pltpu.make_async_copy(built.at[b], out_hbm.at[b], sems.at[b])


def pack_kernel(local, side, blocks, seams_ref, g_hbm, p_hbm, out_hbm, g_ref, p_ref, out_ref, sems, out_sems):
    fetches = [
        pltpu.make_async_copy(g_hbm, g_ref, sems.at[0]),
        pltpu.make_async_copy(p_hbm, p_ref, sems.at[1]),
    ]
    for fetch in fetches:
        fetch.start()
    px_blocks, ch_blocks = blocks
    channels = g_ref.shape[-1]
    px, ch = side // px_blocks, channels // ch_blocks
    count = px * 2 // ch_blocks
    shape = (local * CELLS, local * side)
    line = lax.broadcasted_iota(jnp.int32, shape, 0)
    pixel = lax.broadcasted_iota(jnp.int32, shape, 1)
    cell, base = line % CELLS, line // CELLS * side
    of_g = jnp.where(cell < 2, base + cell, jnp.where(cell < 4, base + side - 4 + cell, -1))
    of_p = jnp.where(cell == 4, base, jnp.where(cell == 5, base + side - 1, -1))
    seams = jnp.zeros((local * CELLS, channels), jnp.float32)
    line = lax.broadcasted_iota(jnp.int32, seams.shape, 0)
    lane = lax.broadcasted_iota(jnp.int32, seams.shape, 1)
    for face in range(local):
        for i in range(4):
            here = (line == face * CELLS + SEAM_AT) & (lane == i)
            seams = jnp.where(here, seams_ref[face, i].astype(jnp.float32), seams)
    take = lambda at, ref: jnp.dot(
        jnp.where(at == pixel, 1.0, 0.0).astype(jnp.bfloat16),
        ref[...].reshape(local * side, channels),
        preferred_element_type=jnp.float32,
    )
    for fetch in fetches:
        fetch.wait()
    cells = (take(of_g, g_ref) + take(of_p, p_ref) + seams).astype(jnp.bfloat16)
    for b in range(px_blocks * ch_blocks):
        i, j = divmod(b, ch_blocks)
        for face in range(local):
            at = face * count
            for which, source in enumerate((g_ref, p_ref)):
                piece = source[face, i * px : (i + 1) * px, j * ch : (j + 1) * ch]
                if ch_blocks == 1:
                    out_ref[b, at + which * px : at + (which + 1) * px] = piece
                else:
                    out_ref[b, at : at + px, which * ch : (which + 1) * ch] = piece
        out_ref[b, local * count :] = cells
        leave(out_ref, out_hbm, out_sems, b).start()
    for b in range(px_blocks * ch_blocks):
        leave(out_ref, out_hbm, out_sems, b).wait()


def pick_kernel(faces, local, count, want_ref, table_ref, out_hbm, out_ref, sems):
    for i in range(faces):
        face = want_ref[i]
        at = pl.multiple_of(lax.rem(face, local) * count, 16)
        into, row = divmod(i, local)
        out_ref[into, row * count : (row + 1) * count] = table_ref[lax.div(face, local), pl.ds(at, count)]
        if row == local - 1:
            leave(out_ref, out_hbm, sems, into).start()
    for b in range(faces // local):
        leave(out_ref, out_hbm, sems, b).wait()


def first_sum_kernel(scale, got_ref, out_ref):
    total = got_ref[0].astype(jnp.float32)
    for i in range(1, got_ref.shape[0]):
        total = total + got_ref[i].astype(jnp.float32)
    turned = (total * scale).T
    out_ref[...] = turned.reshape(out_ref.shape).astype(jnp.bfloat16)


def second_sum_kernel(got_ref, out_ref):
    total = got_ref[0].astype(jnp.float32)
    for i in range(1, got_ref.shape[0]):
        total = total + got_ref[i].astype(jnp.float32)
    _, _, per_tile, width = out_ref.shape
    lines = total.shape[1] // 9
    for tap in range(9):
        r, c = divmod(tap, 3)
        for h in range(width // lines):
            out_ref[r, c, :, h * lines : (h + 1) * lines] = total[
                h * per_tile : (h + 1) * per_tile, tap * lines : (tap + 1) * lines
            ]


def border_kernel(
    local, side, tiles, flags_ref, seams_ref, corners_ref, table_ref, g_ref, p_ref, x_ref, own_ref, wrap_ref, mine_ref, kept_ref
):
    below = flags_ref[3]
    held = local * CELLS
    cells = table_ref[:, table_ref.shape[1] - held :].reshape(table_ref.shape[0] * held, -1)
    rows, width = 4 * GAP, cells.shape[0]
    row = lax.broadcasted_iota(jnp.int32, (rows, 1), 0)
    spot, block = row % GAP, row // GAP
    of_g = block % 2 == 1
    each = jnp.where(of_g, 4, 2)
    k = spot % each
    cell = jnp.where(of_g, k, jnp.where(spot < 2 * local, 4 + k, -1))
    is_left = k * 2 >= each
    face_at = jnp.zeros((rows, 1), jnp.int32)
    for face in range(local):
        for beyond in range(2):
            if beyond:
                left, right = corners_ref[face, 2 * below], corners_ref[face, 2 * below + 1]
            else:
                left, right = seams_ref[face, 3], seams_ref[face, 1]
            here = (spot // each == face) & (block // 2 == beyond)
            face_at = jnp.where(here, jnp.where(is_left, left, right), face_at)
    index = jnp.where(cell < 0, -1, face_at * CELLS + cell)
    where = lax.broadcasted_iota(jnp.int32, (rows, width), 1) == index
    tails = jnp.dot(
        jnp.where(where, 1.0, 0.0).astype(jnp.bfloat16), cells, preferred_element_type=jnp.float32
    ).astype(jnp.bfloat16)
    full = local * side
    for which, source in enumerate((p_ref, g_ref)):
        at = which * (full + GAP)
        own_ref[at : at + full] = source[...].reshape(full, -1)
        own_ref[at + full : at + full + GAP] = tails[which * GAP : (which + 1) * GAP]
    mine_ref[:full] = g_ref[...].reshape(full, -1)
    mine_ref[full : full + GAP] = tails[GAP : 2 * GAP]
    wrap_ref[...] = tails[2 * GAP :]
    nxl, nz, nc, per_tile = tiles
    channels, half = x_ref.shape[-1], kept_ref.shape[-1]
    line = lax.broadcasted_iota(jnp.int32, (channels, nc * half), 0)
    lane = lax.broadcasted_iota(jnp.int32, (channels, nc * half), 1)
    of_core = jnp.where(lane < half, flags_ref[0], 1 - flags_ref[0])
    place = lane % half
    xl, z = place // per_tile % nxl, place // (per_tile * nxl)
    wanted = ((xl * nz + z) * nc + of_core) * per_tile + place % per_tile
    chosen = jnp.dot(
        x_ref[...].reshape(local * side, channels),
        jnp.where(line == wanted, 1.0, 0.0).astype(jnp.bfloat16),
        preferred_element_type=jnp.float32,
    ).astype(jnp.bfloat16)
    kept_ref[...] = chosen[:, :half]
    for face in range(local):
        for part in range(2):
            at = face * side + part * side // 2
            into = full + GAP + face * side // 2
            mine_ref[into : into + side // 2, part * half : (part + 1) * half] = chosen[at : at + side // 2, half:]


def turn_kernel(local, side, flags_ref, kept_ref, part_ref, out_ref, lines):
    pitch = side + 2 * GAP
    row = local * pitch
    half = kept_ref.shape[-1]
    start = local * side + GAP
    lines[...] = jnp.zeros_like(lines)
    for face in range(local):
        at = pl.multiple_of(flags_ref[0] * row + face * pitch + GAP, 16)
        lines[pl.ds(at, side), :] = kept_ref[face * side : (face + 1) * side].astype(jnp.float32)
        for part in range(2):
            at = pl.multiple_of((1 - flags_ref[0]) * row + face * pitch + GAP + part * side // 2, 16)
            lines[pl.ds(at, side // 2), :] = part_ref[
                start + face * side // 2 : start + (face + 1) * side // 2, part * half : (part + 1) * half
            ].astype(jnp.float32)
    for c in range(3):
        moved = lines[...] if c == 1 else pltpu.roll(lines[...], (1 - c) % (2 * row), 0)
        out_ref[c * half : (c + 1) * half, :] = moved.T.astype(jnp.bfloat16)


def send_kernel(local, side, blocks, flags_ref, own_ref, tails_ref, pieces_ref, near_ref, far_ref):
    px_blocks, ch_blocks = blocks
    px = side // px_blocks
    ch = own_ref.shape[-1] // ch_blocks
    count = px * 2 // ch_blocks
    full = local * side
    near, far = flags_ref[1], flags_ref[2]

    def put_wrap(out, start, of_g):
        for face in range(local):
            for b in range(px_blocks * ch_blocks):
                i, j = divmod(b, ch_blocks)
                piece = pieces_ref[b, face * count : (face + 1) * count]
                which = 0 if of_g else 1
                if ch_blocks == 1:
                    part = piece[which * px : (which + 1) * px]
                else:
                    part = piece[:, which * ch : (which + 1) * ch]
                at = start + face * side + i * px
                out[at : at + px, j * ch : (j + 1) * ch] = part
        tail = GAP if of_g else 0
        out[start + full : start + full + GAP, :] = tails_ref[tail : tail + GAP]

    @pl.when(near == 1)
    def _():
        put_wrap(near_ref, 0, False)
        put_wrap(near_ref, full + GAP, True)

    @pl.when(near == 0)
    def _():
        near_ref[...] = own_ref[...]

    @pl.when(far == 1)
    def _():
        put_wrap(far_ref, 0, True)

    @pl.when(far == 0)
    def _():
        far_ref[...] = own_ref[full + GAP :]


def put_row(pad, local, side, source, start, each):
    pitch = side + 2 * GAP
    full = local * side
    line = lax.broadcasted_iota(jnp.int32, (local * GAP, GAP), 0)
    lane = lax.broadcasted_iota(jnp.int32, (local * GAP, GAP), 1)
    spot, at_face = line % GAP, line // GAP
    n = each // 2
    k = jnp.where(spot < n, spot, jnp.where(spot >= GAP - n, spot - (GAP - each), GAP))
    spread = jnp.where(lane == k + each * at_face, 1.0, 0.0)
    spread = jnp.where(k < each, spread, 0.0).astype(jnp.bfloat16)
    tails = source[start + full : start + full + GAP, :]
    borders = jnp.dot(spread, tails, preferred_element_type=jnp.float32).astype(jnp.bfloat16)
    for face in range(local):
        at = face * pitch
        border = borders[face * GAP : (face + 1) * GAP]
        pad[at : at + GAP, :] = border
        pad[at + GAP : at + GAP + side, :] = source[start + face * side : start + (face + 1) * side, :]
        pad[at + GAP + side : at + pitch, :] = border


def row_taps(pairs, row):
    sums = []
    for c in range(3):
        total = None
        for rows, weight in pairs:
            term = lax.dot_general(
                rows, weight(c), (((1,), (1,)), ((), ())), preferred_element_type=jnp.float32
            )
            total = term if total is None else total + term
        sums.append(total)
    return pltpu.roll(sums[2], 1, 0) + sums[1] + pltpu.roll(sums[0], row - 1, 0)


def silu_slope(pre):
    pre = pre.astype(jnp.float32)
    logistic = jax.nn.sigmoid(pre)
    return logistic * (1.0 + pre * (1.0 - logistic))


def near_half_kernel(local, side, flags_ref, own_ref, part_ref, weight_ref, hidden_ref, slope_ref, own_pad, part_pad, pre_pad):
    row = own_pad.shape[0]
    toward = 2 * flags_ref[0]
    second = local * side + GAP
    put_row(own_pad, local, side, own_ref, second, 4)
    put_row(part_pad, local, side, part_ref, 0, 4)
    put_row(pre_pad, local, side, own_ref, 0, 2)
    own, part = own_pad[...], part_pad[...]
    hidden_ref[:row] = row_taps([(own, lambda c: weight_ref[toward, c])], row)
    hidden_ref[row:] = row_taps([(own, lambda c: weight_ref[1, c]), (part, lambda c: weight_ref[toward, c])], row)
    slope_ref[...] = silu_slope(pre_pad[...])


def grad_pre_kernel(local, side, flags_ref, near_ref, far_ref, hidden_ref, slope_ref, weight_ref, out_ref, near_pad, far_pad, pre_pad):
    row = near_pad.shape[0]
    core = flags_ref[0]
    away = 2 - 2 * core
    second = local * side + GAP
    put_row(near_pad, local, side, near_ref, second, 4)
    put_row(far_pad, local, side, far_ref, 0, 4)
    put_row(pre_pad, local, side, near_ref, 0, 2)
    near, far = near_pad[...], far_pad[...]
    outer = hidden_ref[:row] + row_taps(
        [(far, lambda c: weight_ref[away, c]), (near, lambda c: weight_ref[1, c])], row
    )
    inner = hidden_ref[row:] + row_taps([(near, lambda c: weight_ref[away, c])], row)
    outer = (outer * silu_slope(pre_pad[...])).astype(jnp.bfloat16)
    inner = (inner * slope_ref[...]).astype(jnp.bfloat16)
    out_ref[pl.ds(pl.multiple_of(core * row, 16), row), :] = outer
    out_ref[pl.ds(pl.multiple_of((1 - core) * row, 16), row), :] = inner


def conv_rows(pad, start, row, weight_ref):
    sums = []
    for c in range(3):
        total = None
        for r in range(3):
            at = start + (2 - r) * row
            rows = pad[pl.ds(at if isinstance(at, int) else pl.multiple_of(at, 16), row), :]
            term = lax.dot_general(
                rows, weight_ref[r, c], (((1,), (1,)), ((), ())), preferred_element_type=jnp.float32
            )
            total = term if total is None else total + term
        sums.append(total)
    return pltpu.roll(sums[2], 1, 0) + sums[1] + pltpu.roll(sums[0], row - 1, 0)


def four_rows(rows4, core, row, pre_ref, swapped_ref):
    rows4[pl.ds(pl.multiple_of(core * 2 * row, 16), 2 * row), :] = pre_ref[...]
    rows4[pl.ds(pl.multiple_of((1 - core) * 2 * row, 16), 2 * row), :] = swapped_ref[...]


def grad_input_kernel(local, side, flags_ref, pre_ref, swapped_ref, own_ref, weight_ref, out_ref, rows4):
    pitch = side + 2 * GAP
    row = local * pitch
    core = flags_ref[0]
    four_rows(rows4, core, row, pre_ref, swapped_ref)
    grad = conv_rows(rows4, core * row, row, weight_ref)
    for face in range(local):
        at = face * pitch + GAP
        own = own_ref[face].astype(jnp.float32)
        out_ref[face] = (own + grad[at : at + side, :]).astype(jnp.bfloat16)


def emit(out_ref, start, terms, nxl, per_tile):
    dests, half = out_ref.shape[0], out_ref.shape[2]
    lines = terms.shape[1] // dests
    for c in range(3):
        turned = terms[c * half : (c + 1) * half, :].T
        at = pl.multiple_of(start + c * lines, 16)
        if nxl == 1:
            for d in range(dests):
                out_ref[d, pl.ds(at, lines)] = turned[d * lines : (d + 1) * lines, :].astype(jnp.bfloat16)
            continue
        split = turned.reshape(dests // 2, 2, lines, half)
        left = split[:, 0].reshape(-1, half)
        right = split[:, 1].reshape(-1, half)
        low = lax.broadcasted_iota(jnp.int32, left.shape, 1) % (2 * per_tile) < per_tile
        ones = (
            jnp.where(low, left, pltpu.roll(right, per_tile, 1)),
            jnp.where(low, pltpu.roll(left, half - per_tile, 1), right),
        )
        for xl, one in enumerate(ones):
            for d in range(dests // 2):
                out_ref[2 * d + xl, pl.ds(at, lines)] = one[d * lines : (d + 1) * lines, :].astype(jnp.bfloat16)


def first_half_kernel(row, nxl, per_tile, flags_ref, x_ref, pre_ref, out_ref, middle_ref):
    core = flags_ref[0]
    lanes = pl.ds(pl.multiple_of(core * row, 128), row)
    rows = pl.ds(pl.multiple_of((1 - core) * row, 16), row)
    middle_ref[...] = jnp.dot(x_ref[:, lanes], pre_ref[rows, :], preferred_element_type=jnp.float32)
    emit(out_ref, 0, jnp.dot(x_ref[...], pre_ref[...], preferred_element_type=jnp.float32), nxl, per_tile)


def grad_first_kernel(row, nxl, per_tile, flags_ref, x_ref, swapped_ref, done_ref, middle_ref, out_ref):
    core = flags_ref[0]
    lanes = pl.ds(pl.multiple_of((1 - core) * row, 128), row)
    rows = pl.ds(pl.multiple_of(core * row, 16), row)
    count = done_ref.shape[1]
    emit(
        out_ref,
        count,
        middle_ref[...] + jnp.dot(x_ref[:, lanes], swapped_ref[rows, :], preferred_element_type=jnp.float32),
        nxl,
        per_tile,
    )
    terms = jnp.dot(x_ref[...], swapped_ref[...], preferred_element_type=jnp.float32)
    emit(out_ref, core * 2 * count, terms, nxl, per_tile)
    at = pl.multiple_of((1 - core) * 2 * count, 16)
    for d in range(done_ref.shape[0]):
        out_ref[d, pl.ds(at, count)] = done_ref[d]


def kernel(body, out_shape, inputs, smem=0, scratch=(), name=None, flops=0, nbytes=2**20, exps=0, hbm=0, vmem=VMEM, out_hbm=False):
    many = isinstance(out_shape, tuple)
    spots = [pl.BlockSpec(memory_space=pltpu.HBM)] * hbm + whole(len(inputs) - smem - hbm)
    return pl.pallas_call(
        body,
        out_shape=out_shape,
        in_specs=[pl.BlockSpec(memory_space=pltpu.SMEM)] * smem + spots,
        out_specs=tuple(whole(len(out_shape))) if many else pl.BlockSpec(memory_space=pltpu.HBM) if out_hbm else whole(1)[0],
        scratch_shapes=scratch,
        compiler_params=pltpu.CompilerParams(vmem_limit_bytes=vmem),
        cost_estimate=pl.CostEstimate(flops=flops, bytes_accessed=nbytes, transcendentals=exps),
        name=name,
    )(*inputs)


def on_device(sizes, saved_input, saved_pre, cotangent, first_weight, second_weight, seams, corners):
    nxh, ny, nxl, nz, nc = sizes
    nface, ntile, nchip = nxh * ny, nxl * nz * nc, nxl * nz
    x, p, g = saved_input[0, :, 0], saved_pre[0, :, 0], cotangent[0, :, 0]
    local, side, channels = x.shape
    faces = nface * local
    row = local * (side + 2 * GAP)
    bf = jnp.bfloat16
    shape = jax.ShapeDtypeStruct
    core = lax.axis_index("c")
    tile = lax.axis_index(TILE)
    top = tile >= ntile // 2
    near_wraps = (tile == 0) | (tile == ntile - 1)
    far_wraps = (tile == 1) | (tile == ntile - 2)
    flags = jnp.stack([core, *(flag.astype(jnp.int32) for flag in (near_wraps, far_wraps, ~top))])

    px_blocks = 4
    ch_blocks = nface // px_blocks
    px = side // px_blocks
    count = px * 2 // ch_blocks
    sent = kernel(
        functools.partial(pack_kernel, local, side, (px_blocks, ch_blocks)),
        shape((nface, local * (count + CELLS), channels), bf),
        (seams, g, p),
        1,
        (
            pltpu.VMEM((local, side, channels), bf),
            pltpu.VMEM((local, side, channels), bf),
            pltpu.VMEM((nface, local * (count + CELLS), channels), bf),
            pltpu.SemaphoreType.DMA((2,)),
            pltpu.SemaphoreType.DMA((nface,)),
        ),
        "pack",
        hbm=2,
        vmem=None,
        out_hbm=True,
    )
    swap = lambda a: lax.ppermute(a, "c", [(0, 1), (1, 0)])
    sent, flags, top = lax.optimization_barrier((sent, flags, top))
    table = lax.all_to_all(sent, FACE, 0, 0, tiled=True)

    cells = table[:, local * count :].reshape(faces, CELLS, channels)
    all_seams = cells[:, SEAM_AT, :4].astype(jnp.int32)
    want = jnp.where(top, all_seams[:, 0], all_seams[:, 2])
    picked = kernel(
        functools.partial(pick_kernel, faces, local, count),
        shape((nface, local * count, channels), bf),
        (want, table),
        1,
        (pltpu.VMEM((nface, local * count, channels), bf), pltpu.SemaphoreType.DMA((nface,))),
        "pick",
        out_hbm=True,
    )
    picked, table = lax.optimization_barrier((picked, table))
    wrapped = lax.all_to_all(picked, FACE, 0, 0, tiled=True)

    half = channels // nc
    per_tile = channels // ntile
    own, tails, mine, kept = kernel(
        functools.partial(border_kernel, local, side, (nxl, nz, nc, per_tile)),
        (
            shape((2 * (local * side + GAP), channels), bf),
            shape((2 * GAP, channels), bf),
            shape((local * side + GAP + local * side // 2, channels), bf),
            shape((local * side, half), bf),
        ),
        (flags, seams, corners, table, g, p, x),
        3,
        name="border",
    )
    wrapped, part = lax.optimization_barrier((wrapped, swap(mine)))
    near, far = kernel(
        functools.partial(send_kernel, local, side, (px_blocks, ch_blocks)),
        (shape(own.shape, bf), shape((own.shape[0] // 2, channels), bf)),
        (flags, own, tails, wrapped),
        1,
        name="send",
    )

    pairs = lambda step: [((t + step if t % 2 else t - step) % ntile, t) for t in range(ntile)]
    near = lax.ppermute(near, TILE, pairs(1))
    far = lax.ppermute(far, TILE, pairs(2))
    x_turned = kernel(
        functools.partial(turn_kernel, local, side),
        shape((3 * half, 2 * row), bf),
        (flags, kept, part),
        1,
        (pltpu.VMEM((2 * row, half), jnp.float32),),
        "turn",
    )

    pads = tuple(pltpu.VMEM((row, channels), bf) for _ in range(3))
    hidden, slope = kernel(
        functools.partial(near_half_kernel, local, side),
        (shape((2 * row, channels), jnp.float32), shape((row, channels), jnp.float32)),
        (flags, own, part, second_weight),
        1,
        pads,
        "near_half",
        2 * 9 * row * channels**2,
        2 * 2**20,
        row * channels,
    )
    near, far, x_turned, hidden, slope = lax.optimization_barrier((near, far, x_turned, hidden, slope))
    grad_pre = kernel(
        functools.partial(grad_pre_kernel, local, side),
        shape((2 * row, channels), bf),
        (flags, near, far, hidden, slope, second_weight),
        1,
        pads,
        "grad_pre",
        2 * 9 * row * channels**2,
        4 * 2**20,
        row * channels,
    )
    swapped = swap(grad_pre)

    rows4 = (pltpu.VMEM((4 * row, channels), bf),)
    width = channels // nface
    lines = width // nxl
    done, middle = kernel(
        functools.partial(first_half_kernel, row, nxl, per_tile),
        (shape((nface * nxl, 3 * lines, half), bf), shape((3 * half, channels), jnp.float32)),
        (flags, x_turned, grad_pre),
        1,
        name="first_half",
    )
    swapped, done, middle = lax.optimization_barrier((swapped, done, middle))
    parts = kernel(
        functools.partial(grad_first_kernel, row, nxl, per_tile),
        shape((nface * nxl, 9 * lines, half), bf),
        (flags, x_turned, swapped, done, middle),
        1,
        name="grad_first",
        flops=2 * 9 * half * row * channels,
    )
    grad_input = kernel(
        functools.partial(grad_input_kernel, local, side),
        shape((local, side, channels), bf),
        (flags, grad_pre, swapped, g, first_weight),
        1,
        rows4,
        "grad_input",
        2 * 9 * row * channels**2,
        2 * 2**20,
    )
    scale_factor = 1.0 / math.sqrt(faces * ntile * side)
    got = lax.all_to_all(parts, FACE + ("xl",), 0, 0, tiled=True)
    total = kernel(
        functools.partial(first_sum_kernel, scale_factor),
        shape((nz, nxl * per_tile, 9 * lines), bf),
        (got,),
        name="first_sum",
    )
    got = lax.all_to_all(total, "z", 0, 0, tiled=True)
    first_out = kernel(second_sum_kernel, shape((3, 3, per_tile, width), jnp.float32), (got,), name="second_sum")
    return grad_input.reshape(saved_input.shape), first_out


def solution(mesh, sizes=(2, 4, 2, 16, 2)):
    fine = Mesh(mesh.devices.reshape(sizes), FACE + TILE)
    field = P(None, FACE, TILE, None, None)
    return jax.shard_map(
        functools.partial(on_device, sizes),
        mesh=fine,
        in_specs=(field, field, field, P(), P(), P(FACE, None), P(FACE, None)),
        out_specs=(field, P(None, None, TILE, FACE)),
        check_vma=False,
    )
```

```python
import functools
import math

import jax
import jax.numpy as jnp
import numpy as np
from jax import lax
from jax.experimental import pallas as pl
from jax.experimental.pallas import tpu as pltpu
from jax.sharding import Mesh
from jax.sharding import PartitionSpec as P

FACE = ("xh", "y")
TILE = ("xl", "z", "c")
CHIP = ("xl", "z")
GAP = 16
CELLS = 8
SEAM_AT = 6
VMEM = 40 * 2**20


def whole(n):
    return [pl.BlockSpec(memory_space=pltpu.VMEM)] * n


def pack_kernel(local, side, blocks, seams_ref, g_hbm, p_hbm, out_ref, g_ref, p_ref, sems):
    fetches = [
        pltpu.make_async_copy(g_hbm, g_ref, sems.at[0]),
        pltpu.make_async_copy(p_hbm, p_ref, sems.at[1]),
    ]
    for fetch in fetches:
        fetch.start()
    px_blocks, ch_blocks = blocks
    channels = g_ref.shape[-1]
    px, ch = side // px_blocks, channels // ch_blocks
    count = px * 2 // ch_blocks
    shape = (local * CELLS, local * side)
    line = lax.broadcasted_iota(jnp.int32, shape, 0)
    pixel = lax.broadcasted_iota(jnp.int32, shape, 1)
    cell, base = line % CELLS, line // CELLS * side
    of_g = jnp.where(cell < 2, base + cell, jnp.where(cell < 4, base + side - 4 + cell, -1))
    of_p = jnp.where(cell == 4, base, jnp.where(cell == 5, base + side - 1, -1))
    seams = jnp.zeros((local * CELLS, channels), jnp.float32)
    line = lax.broadcasted_iota(jnp.int32, seams.shape, 0)
    lane = lax.broadcasted_iota(jnp.int32, seams.shape, 1)
    for face in range(local):
        for i in range(4):
            here = (line == face * CELLS + SEAM_AT) & (lane == i)
            seams = jnp.where(here, seams_ref[face, i].astype(jnp.float32), seams)
    take = lambda at, ref: jnp.dot(
        jnp.where(at == pixel, 1.0, 0.0).astype(jnp.bfloat16),
        ref[...].reshape(local * side, channels),
        preferred_element_type=jnp.float32,
    )
    for fetch in fetches:
        fetch.wait()
    cells = (take(of_g, g_ref) + take(of_p, p_ref) + seams).astype(jnp.bfloat16)
    for b in range(px_blocks * ch_blocks):
        i, j = divmod(b, ch_blocks)
        for face in range(local):
            at = face * count
            for which, source in enumerate((g_ref, p_ref)):
                piece = source[face, i * px : (i + 1) * px, j * ch : (j + 1) * ch]
                if ch_blocks == 1:
                    out_ref[b, at + which * px : at + (which + 1) * px] = piece
                else:
                    out_ref[b, at : at + px, which * ch : (which + 1) * ch] = piece
        out_ref[b, local * count :] = cells


def pick_kernel(faces, local, count, want_ref, table_ref, out_ref):
    for i in range(faces):
        face = want_ref[i]
        at = pl.multiple_of(lax.rem(face, local) * count, 16)
        into, row = divmod(i, local)
        out_ref[into, row * count : (row + 1) * count] = table_ref[lax.div(face, local), pl.ds(at, count)]


def first_sum_kernel(scale, got_ref, out_ref):
    total = got_ref[0].astype(jnp.float32)
    for i in range(1, got_ref.shape[0]):
        total = total + got_ref[i].astype(jnp.float32)
    turned = (total * scale).T
    out_ref[...] = turned.reshape(out_ref.shape).astype(jnp.bfloat16)


def second_sum_kernel(got_ref, out_ref):
    total = got_ref[0].astype(jnp.float32)
    for i in range(1, got_ref.shape[0]):
        total = total + got_ref[i].astype(jnp.float32)
    _, _, per_tile, width = out_ref.shape
    lines = total.shape[1] // 9
    for tap in range(9):
        r, c = divmod(tap, 3)
        for h in range(width // lines):
            out_ref[r, c, :, h * lines : (h + 1) * lines] = total[
                h * per_tile : (h + 1) * per_tile, tap * lines : (tap + 1) * lines
            ]


def border_kernel(
    local, side, tiles, flags_ref, seams_ref, corners_ref, table_ref, g_ref, p_ref, x_ref, own_ref, wrap_ref, mine_ref, kept_ref
):
    below = flags_ref[3]
    held = local * CELLS
    cells = table_ref[:, table_ref.shape[1] - held :].reshape(table_ref.shape[0] * held, -1)
    rows, width = 4 * GAP, cells.shape[0]
    row = lax.broadcasted_iota(jnp.int32, (rows, 1), 0)
    spot, block = row % GAP, row // GAP
    of_g = block % 2 == 1
    each = jnp.where(of_g, 4, 2)
    k = spot % each
    cell = jnp.where(of_g, k, jnp.where(spot < 2 * local, 4 + k, -1))
    is_left = k * 2 >= each
    face_at = jnp.zeros((rows, 1), jnp.int32)
    for face in range(local):
        for beyond in range(2):
            if beyond:
                left, right = corners_ref[face, 2 * below], corners_ref[face, 2 * below + 1]
            else:
                left, right = seams_ref[face, 3], seams_ref[face, 1]
            here = (spot // each == face) & (block // 2 == beyond)
            face_at = jnp.where(here, jnp.where(is_left, left, right), face_at)
    index = jnp.where(cell < 0, -1, face_at * CELLS + cell)
    where = lax.broadcasted_iota(jnp.int32, (rows, width), 1) == index
    tails = jnp.dot(
        jnp.where(where, 1.0, 0.0).astype(jnp.bfloat16), cells, preferred_element_type=jnp.float32
    ).astype(jnp.bfloat16)
    full = local * side
    for which, source in enumerate((p_ref, g_ref)):
        at = which * (full + GAP)
        own_ref[at : at + full] = source[...].reshape(full, -1)
        own_ref[at + full : at + full + GAP] = tails[which * GAP : (which + 1) * GAP]
    mine_ref[:full] = g_ref[...].reshape(full, -1)
    mine_ref[full : full + GAP] = tails[GAP : 2 * GAP]
    wrap_ref[...] = tails[2 * GAP :]
    nxl, nz, nc, per_tile = tiles
    channels, half = x_ref.shape[-1], kept_ref.shape[-1]
    line = lax.broadcasted_iota(jnp.int32, (channels, nc * half), 0)
    lane = lax.broadcasted_iota(jnp.int32, (channels, nc * half), 1)
    of_core = jnp.where(lane < half, flags_ref[0], 1 - flags_ref[0])
    place = lane % half
    xl, z = place // per_tile % nxl, place // (per_tile * nxl)
    wanted = ((xl * nz + z) * nc + of_core) * per_tile + place % per_tile
    chosen = jnp.dot(
        x_ref[...].reshape(local * side, channels),
        jnp.where(line == wanted, 1.0, 0.0).astype(jnp.bfloat16),
        preferred_element_type=jnp.float32,
    ).astype(jnp.bfloat16)
    kept_ref[...] = chosen[:, :half]
    for face in range(local):
        for part in range(2):
            at = face * side + part * side // 2
            into = full + GAP + face * side // 2
            mine_ref[into : into + side // 2, part * half : (part + 1) * half] = chosen[at : at + side // 2, half:]


def turn_kernel(local, side, flags_ref, kept_ref, part_ref, out_ref, lines):
    pitch = side + 2 * GAP
    row = local * pitch
    half = kept_ref.shape[-1]
    start = local * side + GAP
    lines[...] = jnp.zeros_like(lines)
    for face in range(local):
        at = pl.multiple_of(flags_ref[0] * row + face * pitch + GAP, 16)
        lines[pl.ds(at, side), :] = kept_ref[face * side : (face + 1) * side].astype(jnp.float32)
        for part in range(2):
            at = pl.multiple_of((1 - flags_ref[0]) * row + face * pitch + GAP + part * side // 2, 16)
            lines[pl.ds(at, side // 2), :] = part_ref[
                start + face * side // 2 : start + (face + 1) * side // 2, part * half : (part + 1) * half
            ].astype(jnp.float32)
    for c in range(3):
        moved = lines[...] if c == 1 else pltpu.roll(lines[...], (1 - c) % (2 * row), 0)
        out_ref[c * half : (c + 1) * half, :] = moved.T.astype(jnp.bfloat16)


def send_kernel(local, side, blocks, flags_ref, own_ref, tails_ref, pieces_ref, near_ref, far_ref):
    px_blocks, ch_blocks = blocks
    px = side // px_blocks
    ch = own_ref.shape[-1] // ch_blocks
    count = px * 2 // ch_blocks
    full = local * side
    near, far = flags_ref[1], flags_ref[2]

    def put_wrap(out, start, of_g):
        for face in range(local):
            for b in range(px_blocks * ch_blocks):
                i, j = divmod(b, ch_blocks)
                piece = pieces_ref[b, face * count : (face + 1) * count]
                which = 0 if of_g else 1
                if ch_blocks == 1:
                    part = piece[which * px : (which + 1) * px]
                else:
                    part = piece[:, which * ch : (which + 1) * ch]
                at = start + face * side + i * px
                out[at : at + px, j * ch : (j + 1) * ch] = part
        tail = GAP if of_g else 0
        out[start + full : start + full + GAP, :] = tails_ref[tail : tail + GAP]

    @pl.when(near == 1)
    def _():
        put_wrap(near_ref, 0, False)
        put_wrap(near_ref, full + GAP, True)

    @pl.when(near == 0)
    def _():
        near_ref[...] = own_ref[...]

    @pl.when(far == 1)
    def _():
        put_wrap(far_ref, 0, True)

    @pl.when(far == 0)
    def _():
        far_ref[...] = own_ref[full + GAP :]


def put_row(pad, local, side, source, start, each):
    pitch = side + 2 * GAP
    full = local * side
    line = lax.broadcasted_iota(jnp.int32, (local * GAP, GAP), 0)
    lane = lax.broadcasted_iota(jnp.int32, (local * GAP, GAP), 1)
    spot, at_face = line % GAP, line // GAP
    n = each // 2
    k = jnp.where(spot < n, spot, jnp.where(spot >= GAP - n, spot - (GAP - each), GAP))
    spread = jnp.where(lane == k + each * at_face, 1.0, 0.0)
    spread = jnp.where(k < each, spread, 0.0).astype(jnp.bfloat16)
    tails = source[start + full : start + full + GAP, :]
    borders = jnp.dot(spread, tails, preferred_element_type=jnp.float32).astype(jnp.bfloat16)
    for face in range(local):
        at = face * pitch
        border = borders[face * GAP : (face + 1) * GAP]
        pad[at : at + GAP, :] = border
        pad[at + GAP : at + GAP + side, :] = source[start + face * side : start + (face + 1) * side, :]
        pad[at + GAP + side : at + pitch, :] = border


def row_taps(pairs, row):
    sums = []
    for c in range(3):
        total = None
        for rows, weight in pairs:
            term = lax.dot_general(
                rows, weight(c), (((1,), (1,)), ((), ())), preferred_element_type=jnp.float32
            )
            total = term if total is None else total + term
        sums.append(total)
    return pltpu.roll(sums[2], 1, 0) + sums[1] + pltpu.roll(sums[0], row - 1, 0)


def silu_slope(pre):
    pre = pre.astype(jnp.float32)
    logistic = jax.nn.sigmoid(pre)
    return logistic * (1.0 + pre * (1.0 - logistic))


def near_half_kernel(local, side, flags_ref, own_ref, part_ref, weight_ref, hidden_ref, slope_ref, own_pad, part_pad, pre_pad):
    row = own_pad.shape[0]
    toward = 2 * flags_ref[0]
    second = local * side + GAP
    put_row(own_pad, local, side, own_ref, second, 4)
    put_row(part_pad, local, side, part_ref, 0, 4)
    put_row(pre_pad, local, side, own_ref, 0, 2)
    own, part = own_pad[...], part_pad[...]
    hidden_ref[:row] = row_taps([(own, lambda c: weight_ref[toward, c])], row)
    hidden_ref[row:] = row_taps([(own, lambda c: weight_ref[1, c]), (part, lambda c: weight_ref[toward, c])], row)
    slope_ref[...] = silu_slope(pre_pad[...])


def grad_pre_kernel(local, side, flags_ref, near_ref, far_ref, hidden_ref, slope_ref, weight_ref, out_ref, near_pad, far_pad, pre_pad):
    row = near_pad.shape[0]
    core = flags_ref[0]
    away = 2 - 2 * core
    second = local * side + GAP
    put_row(near_pad, local, side, near_ref, second, 4)
    put_row(far_pad, local, side, far_ref, 0, 4)
    put_row(pre_pad, local, side, near_ref, 0, 2)
    near, far = near_pad[...], far_pad[...]
    outer = hidden_ref[:row] + row_taps(
        [(far, lambda c: weight_ref[away, c]), (near, lambda c: weight_ref[1, c])], row
    )
    inner = hidden_ref[row:] + row_taps([(near, lambda c: weight_ref[away, c])], row)
    outer = (outer * silu_slope(pre_pad[...])).astype(jnp.bfloat16)
    inner = (inner * slope_ref[...]).astype(jnp.bfloat16)
    out_ref[pl.ds(pl.multiple_of(core * row, 16), row), :] = outer
    out_ref[pl.ds(pl.multiple_of((1 - core) * row, 16), row), :] = inner


def conv_rows(pad, start, row, weight_ref):
    sums = []
    for c in range(3):
        total = None
        for r in range(3):
            at = start + (2 - r) * row
            rows = pad[pl.ds(at if isinstance(at, int) else pl.multiple_of(at, 16), row), :]
            term = lax.dot_general(
                rows, weight_ref[r, c], (((1,), (1,)), ((), ())), preferred_element_type=jnp.float32
            )
            total = term if total is None else total + term
        sums.append(total)
    return pltpu.roll(sums[2], 1, 0) + sums[1] + pltpu.roll(sums[0], row - 1, 0)


def four_rows(rows4, core, row, pre_ref, swapped_ref):
    rows4[pl.ds(pl.multiple_of(core * 2 * row, 16), 2 * row), :] = pre_ref[...]
    rows4[pl.ds(pl.multiple_of((1 - core) * 2 * row, 16), 2 * row), :] = swapped_ref[...]


def grad_input_kernel(local, side, flags_ref, pre_ref, swapped_ref, own_ref, weight_ref, out_ref, rows4):
    pitch = side + 2 * GAP
    row = local * pitch
    core = flags_ref[0]
    four_rows(rows4, core, row, pre_ref, swapped_ref)
    grad = conv_rows(rows4, core * row, row, weight_ref)
    for face in range(local):
        at = face * pitch + GAP
        own = own_ref[face].astype(jnp.float32)
        out_ref[face] = (own + grad[at : at + side, :]).astype(jnp.bfloat16)


def emit(out_ref, start, terms, nxl, per_tile):
    dests, half = out_ref.shape[0], out_ref.shape[2]
    lines = terms.shape[1] // dests
    for c in range(3):
        turned = terms[c * half : (c + 1) * half, :].T
        at = pl.multiple_of(start + c * lines, 16)
        if nxl == 1:
            for d in range(dests):
                out_ref[d, pl.ds(at, lines)] = turned[d * lines : (d + 1) * lines, :].astype(jnp.bfloat16)
            continue
        split = turned.reshape(dests // 2, 2, lines, half)
        left = split[:, 0].reshape(-1, half)
        right = split[:, 1].reshape(-1, half)
        low = lax.broadcasted_iota(jnp.int32, left.shape, 1) % (2 * per_tile) < per_tile
        ones = (
            jnp.where(low, left, pltpu.roll(right, per_tile, 1)),
            jnp.where(low, pltpu.roll(left, half - per_tile, 1), right),
        )
        for xl, one in enumerate(ones):
            for d in range(dests // 2):
                out_ref[2 * d + xl, pl.ds(at, lines)] = one[d * lines : (d + 1) * lines, :].astype(jnp.bfloat16)


def first_half_kernel(row, nxl, per_tile, flags_ref, x_ref, pre_ref, out_ref, middle_ref):
    core = flags_ref[0]
    lanes = pl.ds(pl.multiple_of(core * row, 128), row)
    rows = pl.ds(pl.multiple_of((1 - core) * row, 16), row)
    middle_ref[...] = jnp.dot(x_ref[:, lanes], pre_ref[rows, :], preferred_element_type=jnp.float32)
    emit(out_ref, 0, jnp.dot(x_ref[...], pre_ref[...], preferred_element_type=jnp.float32), nxl, per_tile)


def grad_first_kernel(row, nxl, per_tile, flags_ref, x_ref, swapped_ref, done_ref, middle_ref, out_ref):
    core = flags_ref[0]
    lanes = pl.ds(pl.multiple_of((1 - core) * row, 128), row)
    rows = pl.ds(pl.multiple_of(core * row, 16), row)
    count = done_ref.shape[1]
    emit(
        out_ref,
        count,
        middle_ref[...] + jnp.dot(x_ref[:, lanes], swapped_ref[rows, :], preferred_element_type=jnp.float32),
        nxl,
        per_tile,
    )
    terms = jnp.dot(x_ref[...], swapped_ref[...], preferred_element_type=jnp.float32)
    emit(out_ref, core * 2 * count, terms, nxl, per_tile)
    at = pl.multiple_of((1 - core) * 2 * count, 16)
    for d in range(done_ref.shape[0]):
        out_ref[d, pl.ds(at, count)] = done_ref[d]


def kernel(body, out_shape, inputs, smem=0, scratch=(), name=None, flops=0, nbytes=2**20, exps=0, hbm=0, vmem=VMEM):
    many = isinstance(out_shape, tuple)
    spots = [pl.BlockSpec(memory_space=pltpu.HBM)] * hbm + whole(len(inputs) - smem - hbm)
    return pl.pallas_call(
        body,
        out_shape=out_shape,
        in_specs=[pl.BlockSpec(memory_space=pltpu.SMEM)] * smem + spots,
        out_specs=tuple(whole(len(out_shape))) if many else whole(1)[0],
        scratch_shapes=scratch,
        compiler_params=pltpu.CompilerParams(vmem_limit_bytes=vmem),
        cost_estimate=pl.CostEstimate(flops=flops, bytes_accessed=nbytes, transcendentals=exps),
        name=name,
    )(*inputs)


def on_device(sizes, saved_input, saved_pre, cotangent, first_weight, second_weight, seams, corners):
    nxh, ny, nxl, nz, nc = sizes
    nface, ntile, nchip = nxh * ny, nxl * nz * nc, nxl * nz
    x, p, g = saved_input[0, :, 0], saved_pre[0, :, 0], cotangent[0, :, 0]
    local, side, channels = x.shape
    faces = nface * local
    row = local * (side + 2 * GAP)
    bf = jnp.bfloat16
    shape = jax.ShapeDtypeStruct
    core = lax.axis_index("c")
    tile = lax.axis_index(TILE)
    top = tile >= ntile // 2
    near_wraps = (tile == 0) | (tile == ntile - 1)
    far_wraps = (tile == 1) | (tile == ntile - 2)
    flags = jnp.stack([core, *(flag.astype(jnp.int32) for flag in (near_wraps, far_wraps, ~top))])

    px_blocks = 4
    ch_blocks = nface // px_blocks
    px = side // px_blocks
    count = px * 2 // ch_blocks
    sent = kernel(
        functools.partial(pack_kernel, local, side, (px_blocks, ch_blocks)),
        shape((nface, local * (count + CELLS), channels), bf),
        (seams, g, p),
        1,
        (
            pltpu.VMEM((local, side, channels), bf),
            pltpu.VMEM((local, side, channels), bf),
            pltpu.SemaphoreType.DMA((2,)),
        ),
        "pack",
        hbm=2,
        vmem=None,
    )
    swap = lambda a: lax.ppermute(a, "c", [(0, 1), (1, 0)])
    sent, flags, top = lax.optimization_barrier((sent, flags, top))
    table = lax.all_to_all(sent, FACE, 0, 0, tiled=True)

    cells = table[:, local * count :].reshape(faces, CELLS, channels)
    all_seams = cells[:, SEAM_AT, :4].astype(jnp.int32)
    want = jnp.where(top, all_seams[:, 0], all_seams[:, 2])
    picked = kernel(
        functools.partial(pick_kernel, faces, local, count),
        shape((nface, local * count, channels), bf),
        (want, table),
        1,
        name="pick",
    )
    picked, table = lax.optimization_barrier((picked, table))
    wrapped = lax.all_to_all(picked, FACE, 0, 0, tiled=True)

    half = channels // nc
    per_tile = channels // ntile
    own, tails, mine, kept = kernel(
        functools.partial(border_kernel, local, side, (nxl, nz, nc, per_tile)),
        (
            shape((2 * (local * side + GAP), channels), bf),
            shape((2 * GAP, channels), bf),
            shape((local * side + GAP + local * side // 2, channels), bf),
            shape((local * side, half), bf),
        ),
        (flags, seams, corners, table, g, p, x),
        3,
        name="border",
    )
    wrapped, part = lax.optimization_barrier((wrapped, swap(mine)))
    near, far = kernel(
        functools.partial(send_kernel, local, side, (px_blocks, ch_blocks)),
        (shape(own.shape, bf), shape((own.shape[0] // 2, channels), bf)),
        (flags, own, tails, wrapped),
        1,
        name="send",
    )

    pairs = lambda step: [((t + step if t % 2 else t - step) % ntile, t) for t in range(ntile)]
    near = lax.ppermute(near, TILE, pairs(1))
    far = lax.ppermute(far, TILE, pairs(2))
    x_turned = kernel(
        functools.partial(turn_kernel, local, side),
        shape((3 * half, 2 * row), bf),
        (flags, kept, part),
        1,
        (pltpu.VMEM((2 * row, half), jnp.float32),),
        "turn",
    )

    pads = tuple(pltpu.VMEM((row, channels), bf) for _ in range(3))
    hidden, slope = kernel(
        functools.partial(near_half_kernel, local, side),
        (shape((2 * row, channels), jnp.float32), shape((row, channels), jnp.float32)),
        (flags, own, part, second_weight),
        1,
        pads,
        "near_half",
        2 * 9 * row * channels**2,
        2 * 2**20,
        row * channels,
    )
    near, far, x_turned, hidden, slope = lax.optimization_barrier((near, far, x_turned, hidden, slope))
    grad_pre = kernel(
        functools.partial(grad_pre_kernel, local, side),
        shape((2 * row, channels), bf),
        (flags, near, far, hidden, slope, second_weight),
        1,
        pads,
        "grad_pre",
        2 * 9 * row * channels**2,
        4 * 2**20,
        row * channels,
    )
    swapped = swap(grad_pre)

    rows4 = (pltpu.VMEM((4 * row, channels), bf),)
    width = channels // nface
    lines = width // nxl
    done, middle = kernel(
        functools.partial(first_half_kernel, row, nxl, per_tile),
        (shape((nface * nxl, 3 * lines, half), bf), shape((3 * half, channels), jnp.float32)),
        (flags, x_turned, grad_pre),
        1,
        name="first_half",
    )
    swapped, done, middle = lax.optimization_barrier((swapped, done, middle))
    parts = kernel(
        functools.partial(grad_first_kernel, row, nxl, per_tile),
        shape((nface * nxl, 9 * lines, half), bf),
        (flags, x_turned, swapped, done, middle),
        1,
        name="grad_first",
        flops=2 * 9 * half * row * channels,
    )
    grad_input = kernel(
        functools.partial(grad_input_kernel, local, side),
        shape((local, side, channels), bf),
        (flags, grad_pre, swapped, g, first_weight),
        1,
        rows4,
        "grad_input",
        2 * 9 * row * channels**2,
        2 * 2**20,
    )
    scale_factor = 1.0 / math.sqrt(faces * ntile * side)
    got, grad_input = lax.optimization_barrier((lax.all_to_all(parts, FACE + ("xl",), 0, 0, tiled=True), grad_input))
    total = kernel(
        functools.partial(first_sum_kernel, scale_factor),
        shape((nz, nxl * per_tile, 9 * lines), bf),
        (got,),
        name="first_sum",
    )
    got = lax.all_to_all(total, "z", 0, 0, tiled=True)
    first_out = kernel(second_sum_kernel, shape((3, 3, per_tile, width), jnp.float32), (got,), name="second_sum")
    return grad_input.reshape(saved_input.shape), first_out


def solution(mesh, sizes=(2, 4, 2, 16, 2)):
    fine = Mesh(mesh.devices.reshape(sizes), FACE + TILE)
    field = P(None, FACE, TILE, None, None)
    return jax.shard_map(
        functools.partial(on_device, sizes),
        mesh=fine,
        in_specs=(field, field, field, P(), P(), P(FACE, None), P(FACE, None)),
        out_specs=(field, P(None, None, TILE, FACE)),
        check_vma=False,
    )
```

```python
import functools
import math

import jax
import jax.numpy as jnp
import numpy as np
from jax import lax
from jax.experimental import pallas as pl
from jax.experimental.pallas import tpu as pltpu
from jax.sharding import Mesh
from jax.sharding import PartitionSpec as P

FACE = ("xh", "y")
TILE = ("xl", "z", "c")
CHIP = ("xl", "z")
GAP = 16
CELLS = 8
SEAM_AT = 6
VMEM = 40 * 2**20


def whole(n):
    return [pl.BlockSpec(memory_space=pltpu.VMEM)] * n


def leave(built, out_hbm, sems, b):
    return pltpu.make_async_copy(built.at[b], out_hbm.at[b], sems.at[b])


def pack_kernel(local, side, blocks, seams_ref, g_hbm, p_hbm, out_hbm, g_ref, p_ref, out_ref, sems, out_sems):
    fetches = [
        pltpu.make_async_copy(g_hbm, g_ref, sems.at[0]),
        pltpu.make_async_copy(p_hbm, p_ref, sems.at[1]),
    ]
    for fetch in fetches:
        fetch.start()
    px_blocks, ch_blocks = blocks
    channels = g_ref.shape[-1]
    px, ch = side // px_blocks, channels // ch_blocks
    count = px * 2 // ch_blocks
    shape = (local * CELLS, local * side)
    line = lax.broadcasted_iota(jnp.int32, shape, 0)
    pixel = lax.broadcasted_iota(jnp.int32, shape, 1)
    cell, base = line % CELLS, line // CELLS * side
    of_g = jnp.where(cell < 2, base + cell, jnp.where(cell < 4, base + side - 4 + cell, -1))
    of_p = jnp.where(cell == 4, base, jnp.where(cell == 5, base + side - 1, -1))
    seams = jnp.zeros((local * CELLS, channels), jnp.float32)
    line = lax.broadcasted_iota(jnp.int32, seams.shape, 0)
    lane = lax.broadcasted_iota(jnp.int32, seams.shape, 1)
    for face in range(local):
        for i in range(4):
            here = (line == face * CELLS + SEAM_AT) & (lane == i)
            seams = jnp.where(here, seams_ref[face, i].astype(jnp.float32), seams)
    take = lambda at, ref: jnp.dot(
        jnp.where(at == pixel, 1.0, 0.0).astype(jnp.bfloat16),
        ref[...].reshape(local * side, channels),
        preferred_element_type=jnp.float32,
    )
    for fetch in fetches:
        fetch.wait()
    cells = (take(of_g, g_ref) + take(of_p, p_ref) + seams).astype(jnp.bfloat16)
    for b in range(px_blocks * ch_blocks):
        i, j = divmod(b, ch_blocks)
        for face in range(local):
            at = face * count
            for which, source in enumerate((g_ref, p_ref)):
                piece = source[face, i * px : (i + 1) * px, j * ch : (j + 1) * ch]
                if ch_blocks == 1:
                    out_ref[b, at + which * px : at + (which + 1) * px] = piece
                else:
                    out_ref[b, at : at + px, which * ch : (which + 1) * ch] = piece
        out_ref[b, local * count :] = cells
        leave(out_ref, out_hbm, out_sems, b).start()
    for b in range(px_blocks * ch_blocks):
        leave(out_ref, out_hbm, out_sems, b).wait()


def pick_kernel(faces, local, count, want_ref, table_ref, out_hbm, out_ref, sems):
    for i in range(faces):
        face = want_ref[i]
        at = pl.multiple_of(lax.rem(face, local) * count, 16)
        into, row = divmod(i, local)
        out_ref[into, row * count : (row + 1) * count] = table_ref[lax.div(face, local), pl.ds(at, count)]
        if row == local - 1:
            leave(out_ref, out_hbm, sems, into).start()
    for b in range(faces // local):
        leave(out_ref, out_hbm, sems, b).wait()


def first_sum_kernel(scale, got_ref, out_ref):
    total = got_ref[0].astype(jnp.float32)
    for i in range(1, got_ref.shape[0]):
        total = total + got_ref[i].astype(jnp.float32)
    turned = (total * scale).T
    out_ref[...] = turned.reshape(out_ref.shape).astype(jnp.bfloat16)


def second_sum_kernel(got_ref, out_ref):
    total = got_ref[0].astype(jnp.float32)
    for i in range(1, got_ref.shape[0]):
        total = total + got_ref[i].astype(jnp.float32)
    _, _, per_tile, width = out_ref.shape
    lines = total.shape[1] // 9
    for tap in range(9):
        r, c = divmod(tap, 3)
        for h in range(width // lines):
            out_ref[r, c, :, h * lines : (h + 1) * lines] = total[
                h * per_tile : (h + 1) * per_tile, tap * lines : (tap + 1) * lines
            ]


def border_kernel(
    local, side, tiles, flags_ref, seams_ref, corners_ref, table_ref, g_ref, p_ref, x_ref, own_ref, wrap_ref, mine_ref, kept_ref
):
    below = flags_ref[3]
    held = local * CELLS
    cells = table_ref[:, table_ref.shape[1] - held :].reshape(table_ref.shape[0] * held, -1)
    rows, width = 4 * GAP, cells.shape[0]
    row = lax.broadcasted_iota(jnp.int32, (rows, 1), 0)
    spot, block = row % GAP, row // GAP
    of_g = block % 2 == 1
    each = jnp.where(of_g, 4, 2)
    k = spot % each
    cell = jnp.where(of_g, k, jnp.where(spot < 2 * local, 4 + k, -1))
    is_left = k * 2 >= each
    face_at = jnp.zeros((rows, 1), jnp.int32)
    for face in range(local):
        for beyond in range(2):
            if beyond:
                left, right = corners_ref[face, 2 * below], corners_ref[face, 2 * below + 1]
            else:
                left, right = seams_ref[face, 3], seams_ref[face, 1]
            here = (spot // each == face) & (block // 2 == beyond)
            face_at = jnp.where(here, jnp.where(is_left, left, right), face_at)
    index = jnp.where(cell < 0, -1, face_at * CELLS + cell)
    where = lax.broadcasted_iota(jnp.int32, (rows, width), 1) == index
    tails = jnp.dot(
        jnp.where(where, 1.0, 0.0).astype(jnp.bfloat16), cells, preferred_element_type=jnp.float32
    ).astype(jnp.bfloat16)
    full = local * side
    for which, source in enumerate((p_ref, g_ref)):
        at = which * (full + GAP)
        own_ref[at : at + full] = source[...].reshape(full, -1)
        own_ref[at + full : at + full + GAP] = tails[which * GAP : (which + 1) * GAP]
    mine_ref[:full] = g_ref[...].reshape(full, -1)
    mine_ref[full : full + GAP] = tails[GAP : 2 * GAP]
    wrap_ref[...] = tails[2 * GAP :]
    nxl, nz, nc, per_tile = tiles
    channels, half = x_ref.shape[-1], kept_ref.shape[-1]
    line = lax.broadcasted_iota(jnp.int32, (channels, nc * half), 0)
    lane = lax.broadcasted_iota(jnp.int32, (channels, nc * half), 1)
    of_core = jnp.where(lane < half, flags_ref[0], 1 - flags_ref[0])
    place = lane % half
    xl, z = place // per_tile % nxl, place // (per_tile * nxl)
    wanted = ((xl * nz + z) * nc + of_core) * per_tile + place % per_tile
    chosen = jnp.dot(
        x_ref[...].reshape(local * side, channels),
        jnp.where(line == wanted, 1.0, 0.0).astype(jnp.bfloat16),
        preferred_element_type=jnp.float32,
    ).astype(jnp.bfloat16)
    kept_ref[...] = chosen[:, :half]
    for face in range(local):
        for part in range(2):
            at = face * side + part * side // 2
            into = full + GAP + face * side // 2
            mine_ref[into : into + side // 2, part * half : (part + 1) * half] = chosen[at : at + side // 2, half:]


def copies_kernel(local, side, flags_ref, kept_ref, part_ref, out_ref, lines):
    pitch = side + 2 * GAP
    row = local * pitch
    half = kept_ref.shape[-1]
    start = local * side + GAP
    lines[...] = jnp.zeros_like(lines)
    for face in range(local):
        at = pl.multiple_of(flags_ref[0] * row + face * pitch + GAP, 16)
        lines[pl.ds(at, side), :] = kept_ref[face * side : (face + 1) * side].astype(jnp.float32)
        for part in range(2):
            at = pl.multiple_of((1 - flags_ref[0]) * row + face * pitch + GAP + part * side // 2, 16)
            lines[pl.ds(at, side // 2), :] = part_ref[
                start + face * side // 2 : start + (face + 1) * side // 2, part * half : (part + 1) * half
            ].astype(jnp.float32)
    for c in range(3):
        moved = lines[...] if c == 1 else pltpu.roll(lines[...], (1 - c) % (2 * row), 0)
        out_ref[:, c * half : (c + 1) * half] = moved.astype(jnp.bfloat16)


def send_kernel(local, side, blocks, flags_ref, own_ref, tails_ref, pieces_ref, near_ref, far_ref):
    px_blocks, ch_blocks = blocks
    px = side // px_blocks
    ch = own_ref.shape[-1] // ch_blocks
    count = px * 2 // ch_blocks
    full = local * side
    near, far = flags_ref[1], flags_ref[2]

    def put_wrap(out, start, of_g):
        for face in range(local):
            for b in range(px_blocks * ch_blocks):
                i, j = divmod(b, ch_blocks)
                piece = pieces_ref[b, face * count : (face + 1) * count]
                which = 0 if of_g else 1
                if ch_blocks == 1:
                    part = piece[which * px : (which + 1) * px]
                else:
                    part = piece[:, which * ch : (which + 1) * ch]
                at = start + face * side + i * px
                out[at : at + px, j * ch : (j + 1) * ch] = part
        tail = GAP if of_g else 0
        out[start + full : start + full + GAP, :] = tails_ref[tail : tail + GAP]

    @pl.when(near == 1)
    def _():
        put_wrap(near_ref, 0, False)
        put_wrap(near_ref, full + GAP, True)

    @pl.when(near == 0)
    def _():
        near_ref[...] = own_ref[...]

    @pl.when(far == 1)
    def _():
        put_wrap(far_ref, 0, True)

    @pl.when(far == 0)
    def _():
        far_ref[...] = own_ref[full + GAP :]


def put_row(pad, local, side, source, start, each):
    pitch = side + 2 * GAP
    full = local * side
    line = lax.broadcasted_iota(jnp.int32, (local * GAP, GAP), 0)
    lane = lax.broadcasted_iota(jnp.int32, (local * GAP, GAP), 1)
    spot, at_face = line % GAP, line // GAP
    n = each // 2
    k = jnp.where(spot < n, spot, jnp.where(spot >= GAP - n, spot - (GAP - each), GAP))
    spread = jnp.where(lane == k + each * at_face, 1.0, 0.0)
    spread = jnp.where(k < each, spread, 0.0).astype(jnp.bfloat16)
    tails = source[start + full : start + full + GAP, :]
    borders = jnp.dot(spread, tails, preferred_element_type=jnp.float32).astype(jnp.bfloat16)
    for face in range(local):
        at = face * pitch
        border = borders[face * GAP : (face + 1) * GAP]
        pad[at : at + GAP, :] = border
        pad[at + GAP : at + GAP + side, :] = source[start + face * side : start + (face + 1) * side, :]
        pad[at + GAP + side : at + pitch, :] = border


def row_taps(pairs, row):
    sums = []
    for c in range(3):
        total = None
        for rows, weight in pairs:
            term = lax.dot_general(
                rows, weight(c), (((1,), (1,)), ((), ())), preferred_element_type=jnp.float32
            )
            total = term if total is None else total + term
        sums.append(total)
    return pltpu.roll(sums[2], 1, 0) + sums[1] + pltpu.roll(sums[0], row - 1, 0)


def silu_slope(pre):
    pre = pre.astype(jnp.float32)
    logistic = jax.nn.sigmoid(pre)
    return logistic * (1.0 + pre * (1.0 - logistic))


def near_half_kernel(local, side, flags_ref, own_ref, part_ref, weight_ref, hidden_ref, slope_ref, own_pad, part_pad, pre_pad):
    row = own_pad.shape[0]
    toward = 2 * flags_ref[0]
    second = local * side + GAP
    put_row(own_pad, local, side, own_ref, second, 4)
    put_row(part_pad, local, side, part_ref, 0, 4)
    put_row(pre_pad, local, side, own_ref, 0, 2)
    own, part = own_pad[...], part_pad[...]
    hidden_ref[:row] = row_taps([(own, lambda c: weight_ref[toward, c])], row)
    hidden_ref[row:] = row_taps([(own, lambda c: weight_ref[1, c]), (part, lambda c: weight_ref[toward, c])], row)
    slope_ref[...] = silu_slope(pre_pad[...])


def grad_pre_kernel(local, side, flags_ref, near_ref, far_ref, hidden_ref, slope_ref, weight_ref, out_ref, near_pad, far_pad, pre_pad):
    row = near_pad.shape[0]
    core = flags_ref[0]
    away = 2 - 2 * core
    second = local * side + GAP
    put_row(near_pad, local, side, near_ref, second, 4)
    put_row(far_pad, local, side, far_ref, 0, 4)
    put_row(pre_pad, local, side, near_ref, 0, 2)
    near, far = near_pad[...], far_pad[...]
    outer = hidden_ref[:row] + row_taps(
        [(far, lambda c: weight_ref[away, c]), (near, lambda c: weight_ref[1, c])], row
    )
    inner = hidden_ref[row:] + row_taps([(near, lambda c: weight_ref[away, c])], row)
    outer = (outer * silu_slope(pre_pad[...])).astype(jnp.bfloat16)
    inner = (inner * slope_ref[...]).astype(jnp.bfloat16)
    out_ref[pl.ds(pl.multiple_of(core * row, 16), row), :] = outer
    out_ref[pl.ds(pl.multiple_of((1 - core) * row, 16), row), :] = inner


def conv_rows(pad, start, row, weight_ref):
    sums = []
    for c in range(3):
        total = None
        for r in range(3):
            at = start + (2 - r) * row
            rows = pad[pl.ds(at if isinstance(at, int) else pl.multiple_of(at, 16), row), :]
            term = lax.dot_general(
                rows, weight_ref[r, c], (((1,), (1,)), ((), ())), preferred_element_type=jnp.float32
            )
            total = term if total is None else total + term
        sums.append(total)
    return pltpu.roll(sums[2], 1, 0) + sums[1] + pltpu.roll(sums[0], row - 1, 0)


def four_rows(rows4, core, row, pre_ref, swapped_ref):
    rows4[pl.ds(pl.multiple_of(core * 2 * row, 16), 2 * row), :] = pre_ref[...]
    rows4[pl.ds(pl.multiple_of((1 - core) * 2 * row, 16), 2 * row), :] = swapped_ref[...]


def grad_input_kernel(local, side, flags_ref, pre_ref, swapped_ref, own_ref, weight_ref, out_ref, rows4):
    pitch = side + 2 * GAP
    row = local * pitch
    core = flags_ref[0]
    four_rows(rows4, core, row, pre_ref, swapped_ref)
    grad = conv_rows(rows4, core * row, row, weight_ref)
    for face in range(local):
        at = face * pitch + GAP
        own = own_ref[face].astype(jnp.float32)
        out_ref[face] = (own + grad[at : at + side, :]).astype(jnp.bfloat16)


def over_pixels(left, right):
    return lax.dot_general(left, right, (((0,), (0,)), ((), ())), preferred_element_type=jnp.float32)


def emit(out_ref, start, terms, nxl, per_tile):
    dests, half = out_ref.shape[0], out_ref.shape[2]
    lines = terms.shape[0] // dests
    for c in range(3):
        turned = terms[:, c * half : (c + 1) * half]
        at = pl.multiple_of(start + c * lines, 16)
        if nxl == 1:
            for d in range(dests):
                out_ref[d, pl.ds(at, lines)] = turned[d * lines : (d + 1) * lines, :].astype(jnp.bfloat16)
            continue
        split = turned.reshape(dests // 2, 2, lines, half)
        left = split[:, 0].reshape(-1, half)
        right = split[:, 1].reshape(-1, half)
        low = lax.broadcasted_iota(jnp.int32, left.shape, 1) % (2 * per_tile) < per_tile
        ones = (
            jnp.where(low, left, pltpu.roll(right, per_tile, 1)),
            jnp.where(low, pltpu.roll(left, half - per_tile, 1), right),
        )
        for xl, one in enumerate(ones):
            for d in range(dests // 2):
                out_ref[2 * d + xl, pl.ds(at, lines)] = one[d * lines : (d + 1) * lines, :].astype(jnp.bfloat16)


def first_half_kernel(row, nxl, per_tile, flags_ref, x_ref, pre_ref, out_ref, middle_ref):
    core = flags_ref[0]
    x_rows = pl.ds(pl.multiple_of(core * row, 16), row)
    rows = pl.ds(pl.multiple_of((1 - core) * row, 16), row)
    middle_ref[...] = over_pixels(pre_ref[rows, :], x_ref[x_rows, :])
    emit(out_ref, 0, over_pixels(pre_ref[...], x_ref[...]), nxl, per_tile)


def grad_first_kernel(row, nxl, per_tile, flags_ref, x_ref, swapped_ref, done_ref, middle_ref, out_ref):
    core = flags_ref[0]
    x_rows = pl.ds(pl.multiple_of((1 - core) * row, 16), row)
    rows = pl.ds(pl.multiple_of(core * row, 16), row)
    count = done_ref.shape[1]
    emit(
        out_ref,
        count,
        middle_ref[...] + over_pixels(swapped_ref[rows, :], x_ref[x_rows, :]),
        nxl,
        per_tile,
    )
    emit(out_ref, core * 2 * count, over_pixels(swapped_ref[...], x_ref[...]), nxl, per_tile)
    at = pl.multiple_of((1 - core) * 2 * count, 16)
    for d in range(done_ref.shape[0]):
        out_ref[d, pl.ds(at, count)] = done_ref[d]


def kernel(body, out_shape, inputs, smem=0, scratch=(), name=None, flops=0, nbytes=2**20, exps=0, hbm=0, vmem=VMEM, out_hbm=False):
    many = isinstance(out_shape, tuple)
    spots = [pl.BlockSpec(memory_space=pltpu.HBM)] * hbm + whole(len(inputs) - smem - hbm)
    return pl.pallas_call(
        body,
        out_shape=out_shape,
        in_specs=[pl.BlockSpec(memory_space=pltpu.SMEM)] * smem + spots,
        out_specs=tuple(whole(len(out_shape))) if many else pl.BlockSpec(memory_space=pltpu.HBM) if out_hbm else whole(1)[0],
        scratch_shapes=scratch,
        compiler_params=pltpu.CompilerParams(vmem_limit_bytes=vmem),
        cost_estimate=pl.CostEstimate(flops=flops, bytes_accessed=nbytes, transcendentals=exps),
        name=name,
    )(*inputs)


def on_device(sizes, saved_input, saved_pre, cotangent, first_weight, second_weight, seams, corners):
    nxh, ny, nxl, nz, nc = sizes
    nface, ntile, nchip = nxh * ny, nxl * nz * nc, nxl * nz
    x, p, g = saved_input[0, :, 0], saved_pre[0, :, 0], cotangent[0, :, 0]
    local, side, channels = x.shape
    faces = nface * local
    row = local * (side + 2 * GAP)
    bf = jnp.bfloat16
    shape = jax.ShapeDtypeStruct
    core = lax.axis_index("c")
    tile = lax.axis_index(TILE)
    top = tile >= ntile // 2
    near_wraps = (tile == 0) | (tile == ntile - 1)
    far_wraps = (tile == 1) | (tile == ntile - 2)
    flags = jnp.stack([core, *(flag.astype(jnp.int32) for flag in (near_wraps, far_wraps, ~top))])

    px_blocks = 4
    ch_blocks = nface // px_blocks
    px = side // px_blocks
    count = px * 2 // ch_blocks
    sent = kernel(
        functools.partial(pack_kernel, local, side, (px_blocks, ch_blocks)),
        shape((nface, local * (count + CELLS), channels), bf),
        (seams, g, p),
        1,
        (
            pltpu.VMEM((local, side, channels), bf),
            pltpu.VMEM((local, side, channels), bf),
            pltpu.VMEM((nface, local * (count + CELLS), channels), bf),
            pltpu.SemaphoreType.DMA((2,)),
            pltpu.SemaphoreType.DMA((nface,)),
        ),
        "pack",
        hbm=2,
        vmem=None,
        out_hbm=True,
    )
    swap = lambda a: lax.ppermute(a, "c", [(0, 1), (1, 0)])
    sent, flags, top = lax.optimization_barrier((sent, flags, top))
    table = lax.all_to_all(sent, FACE, 0, 0, tiled=True)

    cells = table[:, local * count :].reshape(faces, CELLS, channels)
    all_seams = cells[:, SEAM_AT, :4].astype(jnp.int32)
    want = jnp.where(top, all_seams[:, 0], all_seams[:, 2])
    picked = kernel(
        functools.partial(pick_kernel, faces, local, count),
        shape((nface, local * count, channels), bf),
        (want, table),
        1,
        (pltpu.VMEM((nface, local * count, channels), bf), pltpu.SemaphoreType.DMA((nface,))),
        "pick",
        out_hbm=True,
    )
    picked, table = lax.optimization_barrier((picked, table))
    wrapped = lax.all_to_all(picked, FACE, 0, 0, tiled=True)

    half = channels // nc
    per_tile = channels // ntile
    own, tails, mine, kept = kernel(
        functools.partial(border_kernel, local, side, (nxl, nz, nc, per_tile)),
        (
            shape((2 * (local * side + GAP), channels), bf),
            shape((2 * GAP, channels), bf),
            shape((local * side + GAP + local * side // 2, channels), bf),
            shape((local * side, half), bf),
        ),
        (flags, seams, corners, table, g, p, x),
        3,
        name="border",
    )
    wrapped, part = lax.optimization_barrier((wrapped, swap(mine)))
    near, far = kernel(
        functools.partial(send_kernel, local, side, (px_blocks, ch_blocks)),
        (shape(own.shape, bf), shape((own.shape[0] // 2, channels), bf)),
        (flags, own, tails, wrapped),
        1,
        name="send",
    )

    pairs = lambda step: [((t + step if t % 2 else t - step) % ntile, t) for t in range(ntile)]
    near = lax.ppermute(near, TILE, pairs(1))
    far = lax.ppermute(far, TILE, pairs(2))
    x_copies = kernel(
        functools.partial(copies_kernel, local, side),
        shape((2 * row, 3 * half), bf),
        (flags, kept, part),
        1,
        (pltpu.VMEM((2 * row, half), jnp.float32),),
        "copies",
    )

    pads = tuple(pltpu.VMEM((row, channels), bf) for _ in range(3))
    hidden, slope = kernel(
        functools.partial(near_half_kernel, local, side),
        (shape((2 * row, channels), jnp.float32), shape((row, channels), jnp.float32)),
        (flags, own, part, second_weight),
        1,
        pads,
        "near_half",
        2 * 9 * row * channels**2,
        2 * 2**20,
        row * channels,
    )
    near, far, x_copies, hidden, slope = lax.optimization_barrier((near, far, x_copies, hidden, slope))
    grad_pre = kernel(
        functools.partial(grad_pre_kernel, local, side),
        shape((2 * row, channels), bf),
        (flags, near, far, hidden, slope, second_weight),
        1,
        pads,
        "grad_pre",
        2 * 9 * row * channels**2,
        4 * 2**20,
        row * channels,
    )
    swapped = swap(grad_pre)

    rows4 = (pltpu.VMEM((4 * row, channels), bf),)
    width = channels // nface
    lines = width // nxl
    done, middle = kernel(
        functools.partial(first_half_kernel, row, nxl, per_tile),
        (shape((nface * nxl, 3 * lines, half), bf), shape((channels, 3 * half), jnp.float32)),
        (flags, x_copies, grad_pre),
        1,
        name="first_half",
    )
    swapped, done, middle = lax.optimization_barrier((swapped, done, middle))
    parts = kernel(
        functools.partial(grad_first_kernel, row, nxl, per_tile),
        shape((nface * nxl, 9 * lines, half), bf),
        (flags, x_copies, swapped, done, middle),
        1,
        name="grad_first",
        flops=2 * 9 * half * row * channels,
    )
    grad_input = kernel(
        functools.partial(grad_input_kernel, local, side),
        shape((local, side, channels), bf),
        (flags, grad_pre, swapped, g, first_weight),
        1,
        rows4,
        "grad_input",
        2 * 9 * row * channels**2,
        2 * 2**20,
    )
    scale_factor = 1.0 / math.sqrt(faces * ntile * side)
    got = lax.all_to_all(parts, FACE + ("xl",), 0, 0, tiled=True)
    total = kernel(
        functools.partial(first_sum_kernel, scale_factor),
        shape((nz, nxl * per_tile, 9 * lines), bf),
        (got,),
        name="first_sum",
    )
    got = lax.all_to_all(total, "z", 0, 0, tiled=True)
    first_out = kernel(second_sum_kernel, shape((3, 3, per_tile, width), jnp.float32), (got,), name="second_sum")
    return grad_input.reshape(saved_input.shape), first_out


def solution(mesh, sizes=(2, 4, 2, 16, 2)):
    fine = Mesh(mesh.devices.reshape(sizes), FACE + TILE)
    field = P(None, FACE, TILE, None, None)
    return jax.shard_map(
        functools.partial(on_device, sizes),
        mesh=fine,
        in_specs=(field, field, field, P(), P(), P(FACE, None), P(FACE, None)),
        out_specs=(field, P(None, None, TILE, FACE)),
        check_vma=False,
    )
```

```python
import functools
import math

import jax
import jax.numpy as jnp
import numpy as np
from jax import lax
from jax.experimental import pallas as pl
from jax.experimental.pallas import tpu as pltpu
from jax.sharding import Mesh
from jax.sharding import PartitionSpec as P

FACE = ("xh", "y")
TILE = ("xl", "z", "c")
CHIP = ("xl", "z")
GAP = 16
CELLS = 8
SEAM_AT = 6
VMEM = 40 * 2**20


def whole(n):
    return [pl.BlockSpec(memory_space=pltpu.VMEM)] * n


def leave(built, out_hbm, sems, b):
    return pltpu.make_async_copy(built.at[b], out_hbm.at[b], sems.at[b])


def pack_kernel(local, side, blocks, seams_ref, g_hbm, p_hbm, out_hbm, g_ref, p_ref, out_ref, sems, out_sems):
    fetches = [
        pltpu.make_async_copy(source.at[face], into.at[face], sems.at[which, face])
        for face in range(local)
        for which, (source, into) in enumerate(((g_hbm, g_ref), (p_hbm, p_ref)))
    ]
    for fetch in fetches:
        fetch.start()
    px_blocks, ch_blocks = blocks
    channels = g_ref.shape[-1]
    px, ch = side // px_blocks, channels // ch_blocks
    count = px * 2 // ch_blocks
    shape = (local * CELLS, local * side)
    line = lax.broadcasted_iota(jnp.int32, shape, 0)
    pixel = lax.broadcasted_iota(jnp.int32, shape, 1)
    cell, base = line % CELLS, line // CELLS * side
    of_g = jnp.where(cell < 2, base + cell, jnp.where(cell < 4, base + side - 4 + cell, -1))
    of_p = jnp.where(cell == 4, base, jnp.where(cell == 5, base + side - 1, -1))
    seams = jnp.zeros((local * CELLS, channels), jnp.float32)
    line = lax.broadcasted_iota(jnp.int32, seams.shape, 0)
    lane = lax.broadcasted_iota(jnp.int32, seams.shape, 1)
    for face in range(local):
        for i in range(4):
            here = (line == face * CELLS + SEAM_AT) & (lane == i)
            seams = jnp.where(here, seams_ref[face, i].astype(jnp.float32), seams)
    take = lambda at, ref: jnp.dot(
        jnp.where(at == pixel, 1.0, 0.0).astype(jnp.bfloat16),
        ref[...].reshape(local * side, channels),
        preferred_element_type=jnp.float32,
    )
    for fetch in fetches:
        fetch.wait()
    cells = (take(of_g, g_ref) + take(of_p, p_ref) + seams).astype(jnp.bfloat16)
    for b in range(px_blocks * ch_blocks):
        i, j = divmod(b, ch_blocks)
        for face in range(local):
            at = face * count
            for which, source in enumerate((g_ref, p_ref)):
                piece = source[face, i * px : (i + 1) * px, j * ch : (j + 1) * ch]
                if ch_blocks == 1:
                    out_ref[b, at + which * px : at + (which + 1) * px] = piece
                else:
                    out_ref[b, at : at + px, which * ch : (which + 1) * ch] = piece
        out_ref[b, local * count :] = cells
        leave(out_ref, out_hbm, out_sems, b).start()
    for b in range(px_blocks * ch_blocks):
        leave(out_ref, out_hbm, out_sems, b).wait()


def pick_kernel(faces, local, count, want_ref, table_ref, out_hbm, out_ref, sems):
    for i in range(faces):
        face = want_ref[i]
        at = pl.multiple_of(lax.rem(face, local) * count, 16)
        into, row = divmod(i, local)
        out_ref[into, row * count : (row + 1) * count] = table_ref[lax.div(face, local), pl.ds(at, count)]
        if row == local - 1:
            leave(out_ref, out_hbm, sems, into).start()
    for b in range(faces // local):
        leave(out_ref, out_hbm, sems, b).wait()


def first_sum_kernel(scale, got_ref, out_ref):
    total = got_ref[0].astype(jnp.float32)
    for i in range(1, got_ref.shape[0]):
        total = total + got_ref[i].astype(jnp.float32)
    turned = (total * scale).T
    out_ref[...] = turned.reshape(out_ref.shape).astype(jnp.bfloat16)


def second_sum_kernel(got_ref, out_ref):
    total = got_ref[0].astype(jnp.float32)
    for i in range(1, got_ref.shape[0]):
        total = total + got_ref[i].astype(jnp.float32)
    _, _, per_tile, width = out_ref.shape
    lines = total.shape[1] // 9
    for tap in range(9):
        r, c = divmod(tap, 3)
        for h in range(width // lines):
            out_ref[r, c, :, h * lines : (h + 1) * lines] = total[
                h * per_tile : (h + 1) * per_tile, tap * lines : (tap + 1) * lines
            ]


def border_kernel(
    local, side, tiles, flags_ref, seams_ref, corners_ref, table_ref, g_ref, p_ref, x_ref, own_ref, wrap_ref, mine_ref, kept_ref
):
    below = flags_ref[3]
    held = local * CELLS
    cells = table_ref[:, table_ref.shape[1] - held :].reshape(table_ref.shape[0] * held, -1)
    rows, width = 4 * GAP, cells.shape[0]
    row = lax.broadcasted_iota(jnp.int32, (rows, 1), 0)
    spot, block = row % GAP, row // GAP
    of_g = block % 2 == 1
    each = jnp.where(of_g, 4, 2)
    k = spot % each
    cell = jnp.where(of_g, k, jnp.where(spot < 2 * local, 4 + k, -1))
    is_left = k * 2 >= each
    face_at = jnp.zeros((rows, 1), jnp.int32)
    for face in range(local):
        for beyond in range(2):
            if beyond:
                left, right = corners_ref[face, 2 * below], corners_ref[face, 2 * below + 1]
            else:
                left, right = seams_ref[face, 3], seams_ref[face, 1]
            here = (spot // each == face) & (block // 2 == beyond)
            face_at = jnp.where(here, jnp.where(is_left, left, right), face_at)
    index = jnp.where(cell < 0, -1, face_at * CELLS + cell)
    where = lax.broadcasted_iota(jnp.int32, (rows, width), 1) == index
    tails = jnp.dot(
        jnp.where(where, 1.0, 0.0).astype(jnp.bfloat16), cells, preferred_element_type=jnp.float32
    ).astype(jnp.bfloat16)
    full = local * side
    for which, source in enumerate((p_ref, g_ref)):
        at = which * (full + GAP)
        own_ref[at : at + full] = source[...].reshape(full, -1)
        own_ref[at + full : at + full + GAP] = tails[which * GAP : (which + 1) * GAP]
    mine_ref[:full] = g_ref[...].reshape(full, -1)
    mine_ref[full : full + GAP] = tails[GAP : 2 * GAP]
    wrap_ref[...] = tails[2 * GAP :]
    nxl, nz, nc, per_tile = tiles
    channels, half = x_ref.shape[-1], kept_ref.shape[-1]
    line = lax.broadcasted_iota(jnp.int32, (channels, nc * half), 0)
    lane = lax.broadcasted_iota(jnp.int32, (channels, nc * half), 1)
    of_core = jnp.where(lane < half, flags_ref[0], 1 - flags_ref[0])
    place = lane % half
    xl, z = place // per_tile % nxl, place // (per_tile * nxl)
    wanted = ((xl * nz + z) * nc + of_core) * per_tile + place % per_tile
    chosen = jnp.dot(
        x_ref[...].reshape(local * side, channels),
        jnp.where(line == wanted, 1.0, 0.0).astype(jnp.bfloat16),
        preferred_element_type=jnp.float32,
    ).astype(jnp.bfloat16)
    kept_ref[...] = chosen[:, :half]
    for face in range(local):
        for part in range(2):
            at = face * side + part * side // 2
            into = full + GAP + face * side // 2
            mine_ref[into : into + side // 2, part * half : (part + 1) * half] = chosen[at : at + side // 2, half:]


def copies_kernel(local, side, flags_ref, kept_ref, part_ref, out_ref, lines):
    pitch = side + 2 * GAP
    row = local * pitch
    half = kept_ref.shape[-1]
    start = local * side + GAP
    lines[...] = jnp.zeros_like(lines)
    for face in range(local):
        at = pl.multiple_of(flags_ref[0] * row + face * pitch + GAP, 16)
        lines[pl.ds(at, side), :] = kept_ref[face * side : (face + 1) * side].astype(jnp.float32)
        for part in range(2):
            at = pl.multiple_of((1 - flags_ref[0]) * row + face * pitch + GAP + part * side // 2, 16)
            lines[pl.ds(at, side // 2), :] = part_ref[
                start + face * side // 2 : start + (face + 1) * side // 2, part * half : (part + 1) * half
            ].astype(jnp.float32)
    for c in range(3):
        moved = lines[...] if c == 1 else pltpu.roll(lines[...], (1 - c) % (2 * row), 0)
        out_ref[:, c * half : (c + 1) * half] = moved.astype(jnp.bfloat16)


def send_kernel(local, side, blocks, flags_ref, own_ref, tails_ref, pieces_ref, near_ref, far_ref):
    px_blocks, ch_blocks = blocks
    px = side // px_blocks
    ch = own_ref.shape[-1] // ch_blocks
    count = px * 2 // ch_blocks
    full = local * side
    near, far = flags_ref[1], flags_ref[2]

    def put_wrap(out, start, of_g):
        for face in range(local):
            for b in range(px_blocks * ch_blocks):
                i, j = divmod(b, ch_blocks)
                piece = pieces_ref[b, face * count : (face + 1) * count]
                which = 0 if of_g else 1
                if ch_blocks == 1:
                    part = piece[which * px : (which + 1) * px]
                else:
                    part = piece[:, which * ch : (which + 1) * ch]
                at = start + face * side + i * px
                out[at : at + px, j * ch : (j + 1) * ch] = part
        tail = GAP if of_g else 0
        out[start + full : start + full + GAP, :] = tails_ref[tail : tail + GAP]

    @pl.when(near == 1)
    def _():
        put_wrap(near_ref, 0, False)
        put_wrap(near_ref, full + GAP, True)

    @pl.when(near == 0)
    def _():
        near_ref[...] = own_ref[...]

    @pl.when(far == 1)
    def _():
        put_wrap(far_ref, 0, True)

    @pl.when(far == 0)
    def _():
        far_ref[...] = own_ref[full + GAP :]


def put_row(pad, local, side, source, start, each):
    pitch = side + 2 * GAP
    full = local * side
    line = lax.broadcasted_iota(jnp.int32, (local * GAP, GAP), 0)
    lane = lax.broadcasted_iota(jnp.int32, (local * GAP, GAP), 1)
    spot, at_face = line % GAP, line // GAP
    n = each // 2
    k = jnp.where(spot < n, spot, jnp.where(spot >= GAP - n, spot - (GAP - each), GAP))
    spread = jnp.where(lane == k + each * at_face, 1.0, 0.0)
    spread = jnp.where(k < each, spread, 0.0).astype(jnp.bfloat16)
    tails = source[start + full : start + full + GAP, :]
    borders = jnp.dot(spread, tails, preferred_element_type=jnp.float32).astype(jnp.bfloat16)
    for face in range(local):
        at = face * pitch
        border = borders[face * GAP : (face + 1) * GAP]
        pad[at : at + GAP, :] = border
        pad[at + GAP : at + GAP + side, :] = source[start + face * side : start + (face + 1) * side, :]
        pad[at + GAP + side : at + pitch, :] = border


def row_taps(pairs, row):
    sums = []
    for c in range(3):
        total = None
        for rows, weight in pairs:
            term = lax.dot_general(
                rows, weight(c), (((1,), (1,)), ((), ())), preferred_element_type=jnp.float32
            )
            total = term if total is None else total + term
        sums.append(total)
    return pltpu.roll(sums[2], 1, 0) + sums[1] + pltpu.roll(sums[0], row - 1, 0)


def silu_slope(pre):
    pre = pre.astype(jnp.float32)
    logistic = jax.nn.sigmoid(pre)
    return logistic * (1.0 + pre * (1.0 - logistic))


def near_half_kernel(local, side, flags_ref, own_ref, part_ref, weight_ref, hidden_ref, slope_ref, own_pad, part_pad, pre_pad):
    row = own_pad.shape[0]
    toward = 2 * flags_ref[0]
    second = local * side + GAP
    put_row(own_pad, local, side, own_ref, second, 4)
    put_row(part_pad, local, side, part_ref, 0, 4)
    put_row(pre_pad, local, side, own_ref, 0, 2)
    own, part = own_pad[...], part_pad[...]
    hidden_ref[:row] = row_taps([(own, lambda c: weight_ref[toward, c])], row)
    hidden_ref[row:] = row_taps([(own, lambda c: weight_ref[1, c]), (part, lambda c: weight_ref[toward, c])], row)
    slope_ref[...] = silu_slope(pre_pad[...])


def grad_pre_kernel(local, side, flags_ref, near_ref, far_ref, hidden_ref, slope_ref, weight_ref, out_ref, near_pad, far_pad, pre_pad):
    row = near_pad.shape[0]
    core = flags_ref[0]
    away = 2 - 2 * core
    second = local * side + GAP
    put_row(near_pad, local, side, near_ref, second, 4)
    put_row(far_pad, local, side, far_ref, 0, 4)
    put_row(pre_pad, local, side, near_ref, 0, 2)
    near, far = near_pad[...], far_pad[...]
    outer = hidden_ref[:row] + row_taps(
        [(far, lambda c: weight_ref[away, c]), (near, lambda c: weight_ref[1, c])], row
    )
    inner = hidden_ref[row:] + row_taps([(near, lambda c: weight_ref[away, c])], row)
    outer = (outer * silu_slope(pre_pad[...])).astype(jnp.bfloat16)
    inner = (inner * slope_ref[...]).astype(jnp.bfloat16)
    out_ref[pl.ds(pl.multiple_of(core * row, 16), row), :] = outer
    out_ref[pl.ds(pl.multiple_of((1 - core) * row, 16), row), :] = inner


def conv_rows(pad, start, row, weight_ref):
    sums = []
    for c in range(3):
        total = None
        for r in range(3):
            at = start + (2 - r) * row
            rows = pad[pl.ds(at if isinstance(at, int) else pl.multiple_of(at, 16), row), :]
            term = lax.dot_general(
                rows, weight_ref[r, c], (((1,), (1,)), ((), ())), preferred_element_type=jnp.float32
            )
            total = term if total is None else total + term
        sums.append(total)
    return pltpu.roll(sums[2], 1, 0) + sums[1] + pltpu.roll(sums[0], row - 1, 0)


def four_rows(rows4, core, row, pre_ref, swapped_ref):
    rows4[pl.ds(pl.multiple_of(core * 2 * row, 16), 2 * row), :] = pre_ref[...]
    rows4[pl.ds(pl.multiple_of((1 - core) * 2 * row, 16), 2 * row), :] = swapped_ref[...]


def grad_input_kernel(local, side, flags_ref, pre_ref, swapped_ref, own_ref, weight_ref, out_ref, rows4):
    pitch = side + 2 * GAP
    row = local * pitch
    core = flags_ref[0]
    four_rows(rows4, core, row, pre_ref, swapped_ref)
    grad = conv_rows(rows4, core * row, row, weight_ref)
    for face in range(local):
        at = face * pitch + GAP
        own = own_ref[face].astype(jnp.float32)
        out_ref[face] = (own + grad[at : at + side, :]).astype(jnp.bfloat16)


def over_pixels(left, right):
    return lax.dot_general(left, right, (((0,), (0,)), ((), ())), preferred_element_type=jnp.float32)


def emit(out_ref, start, terms, nxl, per_tile):
    dests, half = out_ref.shape[0], out_ref.shape[2]
    lines = terms.shape[0] // dests
    for c in range(3):
        turned = terms[:, c * half : (c + 1) * half]
        at = pl.multiple_of(start + c * lines, 16)
        if nxl == 1:
            for d in range(dests):
                out_ref[d, pl.ds(at, lines)] = turned[d * lines : (d + 1) * lines, :].astype(jnp.bfloat16)
            continue
        split = turned.reshape(dests // 2, 2, lines, half)
        left = split[:, 0].reshape(-1, half)
        right = split[:, 1].reshape(-1, half)
        low = lax.broadcasted_iota(jnp.int32, left.shape, 1) % (2 * per_tile) < per_tile
        ones = (
            jnp.where(low, left, pltpu.roll(right, per_tile, 1)),
            jnp.where(low, pltpu.roll(left, half - per_tile, 1), right),
        )
        for xl, one in enumerate(ones):
            for d in range(dests // 2):
                out_ref[2 * d + xl, pl.ds(at, lines)] = one[d * lines : (d + 1) * lines, :].astype(jnp.bfloat16)


def first_half_kernel(row, nxl, per_tile, flags_ref, x_ref, pre_ref, out_ref, middle_ref):
    core = flags_ref[0]
    x_rows = pl.ds(pl.multiple_of(core * row, 16), row)
    rows = pl.ds(pl.multiple_of((1 - core) * row, 16), row)
    middle_ref[...] = over_pixels(pre_ref[rows, :], x_ref[x_rows, :])
    emit(out_ref, 0, over_pixels(pre_ref[...], x_ref[...]), nxl, per_tile)


def grad_first_kernel(row, nxl, per_tile, flags_ref, x_ref, swapped_ref, done_ref, middle_ref, out_ref):
    core = flags_ref[0]
    x_rows = pl.ds(pl.multiple_of((1 - core) * row, 16), row)
    rows = pl.ds(pl.multiple_of(core * row, 16), row)
    count = done_ref.shape[1]
    emit(
        out_ref,
        count,
        middle_ref[...] + over_pixels(swapped_ref[rows, :], x_ref[x_rows, :]),
        nxl,
        per_tile,
    )
    emit(out_ref, core * 2 * count, over_pixels(swapped_ref[...], x_ref[...]), nxl, per_tile)
    at = pl.multiple_of((1 - core) * 2 * count, 16)
    for d in range(done_ref.shape[0]):
        out_ref[d, pl.ds(at, count)] = done_ref[d]


def kernel(body, out_shape, inputs, smem=0, scratch=(), name=None, flops=0, nbytes=2**20, exps=0, hbm=0, vmem=VMEM, out_hbm=False):
    many = isinstance(out_shape, tuple)
    spots = [pl.BlockSpec(memory_space=pltpu.HBM)] * hbm + whole(len(inputs) - smem - hbm)
    return pl.pallas_call(
        body,
        out_shape=out_shape,
        in_specs=[pl.BlockSpec(memory_space=pltpu.SMEM)] * smem + spots,
        out_specs=tuple(whole(len(out_shape))) if many else pl.BlockSpec(memory_space=pltpu.HBM) if out_hbm else whole(1)[0],
        scratch_shapes=scratch,
        compiler_params=pltpu.CompilerParams(vmem_limit_bytes=vmem),
        cost_estimate=pl.CostEstimate(flops=flops, bytes_accessed=nbytes, transcendentals=exps),
        name=name,
    )(*inputs)


def on_device(sizes, saved_input, saved_pre, cotangent, first_weight, second_weight, seams, corners):
    nxh, ny, nxl, nz, nc = sizes
    nface, ntile, nchip = nxh * ny, nxl * nz * nc, nxl * nz
    x, p, g = saved_input[0, :, 0], saved_pre[0, :, 0], cotangent[0, :, 0]
    local, side, channels = x.shape
    faces = nface * local
    row = local * (side + 2 * GAP)
    bf = jnp.bfloat16
    shape = jax.ShapeDtypeStruct
    core = lax.axis_index("c")
    tile = lax.axis_index(TILE)
    top = tile >= ntile // 2
    near_wraps = (tile == 0) | (tile == ntile - 1)
    far_wraps = (tile == 1) | (tile == ntile - 2)
    flags = jnp.stack([core, *(flag.astype(jnp.int32) for flag in (near_wraps, far_wraps, ~top))])

    px_blocks = 4
    ch_blocks = nface // px_blocks
    px = side // px_blocks
    count = px * 2 // ch_blocks
    sent = kernel(
        functools.partial(pack_kernel, local, side, (px_blocks, ch_blocks)),
        shape((nface, local * (count + CELLS), channels), bf),
        (seams, g, p),
        1,
        (
            pltpu.VMEM((local, side, channels), bf),
            pltpu.VMEM((local, side, channels), bf),
            pltpu.VMEM((nface, local * (count + CELLS), channels), bf),
            pltpu.SemaphoreType.DMA((2, local)),
            pltpu.SemaphoreType.DMA((nface,)),
        ),
        "pack",
        hbm=2,
        vmem=None,
        out_hbm=True,
    )
    swap = lambda a: lax.ppermute(a, "c", [(0, 1), (1, 0)])
    sent, flags, top = lax.optimization_barrier((sent, flags, top))
    table = lax.all_to_all(sent, FACE, 0, 0, tiled=True)

    cells = table[:, local * count :].reshape(faces, CELLS, channels)
    all_seams = cells[:, SEAM_AT, :4].astype(jnp.int32)
    want = jnp.where(top, all_seams[:, 0], all_seams[:, 2])
    picked = kernel(
        functools.partial(pick_kernel, faces, local, count),
        shape((nface, local * count, channels), bf),
        (want, table),
        1,
        (pltpu.VMEM((nface, local * count, channels), bf), pltpu.SemaphoreType.DMA((nface,))),
        "pick",
        out_hbm=True,
    )
    picked, table = lax.optimization_barrier((picked, table))
    wrapped = lax.all_to_all(picked, FACE, 0, 0, tiled=True)

    half = channels // nc
    per_tile = channels // ntile
    own, tails, mine, kept = kernel(
        functools.partial(border_kernel, local, side, (nxl, nz, nc, per_tile)),
        (
            shape((2 * (local * side + GAP), channels), bf),
            shape((2 * GAP, channels), bf),
            shape((local * side + GAP + local * side // 2, channels), bf),
            shape((local * side, half), bf),
        ),
        (flags, seams, corners, table, g, p, x),
        3,
        name="border",
    )
    wrapped, part = lax.optimization_barrier((wrapped, swap(mine)))
    near, far = kernel(
        functools.partial(send_kernel, local, side, (px_blocks, ch_blocks)),
        (shape(own.shape, bf), shape((own.shape[0] // 2, channels), bf)),
        (flags, own, tails, wrapped),
        1,
        name="send",
    )

    pairs = lambda step: [((t + step if t % 2 else t - step) % ntile, t) for t in range(ntile)]
    near = lax.ppermute(near, TILE, pairs(1))
    far = lax.ppermute(far, TILE, pairs(2))
    x_copies = kernel(
        functools.partial(copies_kernel, local, side),
        shape((2 * row, 3 * half), bf),
        (flags, kept, part),
        1,
        (pltpu.VMEM((2 * row, half), jnp.float32),),
        "copies",
    )

    pads = tuple(pltpu.VMEM((row, channels), bf) for _ in range(3))
    hidden, slope = kernel(
        functools.partial(near_half_kernel, local, side),
        (shape((2 * row, channels), jnp.float32), shape((row, channels), jnp.float32)),
        (flags, own, part, second_weight),
        1,
        pads,
        "near_half",
        2 * 9 * row * channels**2,
        2 * 2**20,
        row * channels,
    )
    near, far, x_copies, hidden, slope = lax.optimization_barrier((near, far, x_copies, hidden, slope))
    grad_pre = kernel(
        functools.partial(grad_pre_kernel, local, side),
        shape((2 * row, channels), bf),
        (flags, near, far, hidden, slope, second_weight),
        1,
        pads,
        "grad_pre",
        2 * 9 * row * channels**2,
        4 * 2**20,
        row * channels,
    )
    swapped = swap(grad_pre)

    rows4 = (pltpu.VMEM((4 * row, channels), bf),)
    width = channels // nface
    lines = width // nxl
    done, middle = kernel(
        functools.partial(first_half_kernel, row, nxl, per_tile),
        (shape((nface * nxl, 3 * lines, half), bf), shape((channels, 3 * half), jnp.float32)),
        (flags, x_copies, grad_pre),
        1,
        name="first_half",
    )
    swapped, done, middle = lax.optimization_barrier((swapped, done, middle))
    parts = kernel(
        functools.partial(grad_first_kernel, row, nxl, per_tile),
        shape((nface * nxl, 9 * lines, half), bf),
        (flags, x_copies, swapped, done, middle),
        1,
        name="grad_first",
        flops=2 * 9 * half * row * channels,
    )
    grad_input = kernel(
        functools.partial(grad_input_kernel, local, side),
        shape((local, side, channels), bf),
        (flags, grad_pre, swapped, g, first_weight),
        1,
        rows4,
        "grad_input",
        2 * 9 * row * channels**2,
        2 * 2**20,
    )
    scale_factor = 1.0 / math.sqrt(faces * ntile * side)
    got = lax.all_to_all(parts, FACE + ("xl",), 0, 0, tiled=True)
    total = kernel(
        functools.partial(first_sum_kernel, scale_factor),
        shape((nz, nxl * per_tile, 9 * lines), bf),
        (got,),
        name="first_sum",
    )
    got = lax.all_to_all(total, "z", 0, 0, tiled=True)
    first_out = kernel(second_sum_kernel, shape((3, 3, per_tile, width), jnp.float32), (got,), name="second_sum")
    return grad_input.reshape(saved_input.shape), first_out


def solution(mesh, sizes=(2, 4, 2, 16, 2)):
    fine = Mesh(mesh.devices.reshape(sizes), FACE + TILE)
    field = P(None, FACE, TILE, None, None)
    return jax.shard_map(
        functools.partial(on_device, sizes),
        mesh=fine,
        in_specs=(field, field, field, P(), P(), P(FACE, None), P(FACE, None)),
        out_specs=(field, P(None, None, TILE, FACE)),
        check_vma=False,
    )
```

```python
import functools
import math

import jax
import jax.numpy as jnp
import numpy as np
from jax import lax
from jax.experimental import pallas as pl
from jax.experimental.pallas import tpu as pltpu
from jax.sharding import Mesh
from jax.sharding import PartitionSpec as P

FACE = ("xh", "y")
TILE = ("xl", "z", "c")
CHIP = ("xl", "z")
GAP = 16
CELLS = 8
SEAM_AT = 6
VMEM = 40 * 2**20


def whole(n):
    return [pl.BlockSpec(memory_space=pltpu.VMEM)] * n


def leave(built, out_hbm, sems, b):
    return pltpu.make_async_copy(built.at[b], out_hbm.at[b], sems.at[b])


def pack_kernel(local, side, blocks, seams_ref, g_hbm, p_hbm, out_hbm, g_ref, p_ref, out_ref, sems, out_sems):
    fetches = [
        pltpu.make_async_copy(source.at[face], into.at[face], sems.at[which, face])
        for face in range(local)
        for which, (source, into) in enumerate(((g_hbm, g_ref), (p_hbm, p_ref)))
    ]
    for fetch in fetches:
        fetch.start()
    px_blocks, ch_blocks = blocks
    channels = g_ref.shape[-1]
    px, ch = side // px_blocks, channels // ch_blocks
    count = px * 2 // ch_blocks
    shape = (local * CELLS, local * side)
    line = lax.broadcasted_iota(jnp.int32, shape, 0)
    pixel = lax.broadcasted_iota(jnp.int32, shape, 1)
    cell, base = line % CELLS, line // CELLS * side
    of_g = jnp.where(cell < 2, base + cell, jnp.where(cell < 4, base + side - 4 + cell, -1))
    of_p = jnp.where(cell == 4, base, jnp.where(cell == 5, base + side - 1, -1))
    seams = jnp.zeros((local * CELLS, channels), jnp.float32)
    line = lax.broadcasted_iota(jnp.int32, seams.shape, 0)
    lane = lax.broadcasted_iota(jnp.int32, seams.shape, 1)
    for face in range(local):
        for i in range(4):
            here = (line == face * CELLS + SEAM_AT) & (lane == i)
            seams = jnp.where(here, seams_ref[face, i].astype(jnp.float32), seams)
    take = lambda at, ref: jnp.dot(
        jnp.where(at == pixel, 1.0, 0.0).astype(jnp.bfloat16),
        ref[...].reshape(local * side, channels),
        preferred_element_type=jnp.float32,
    )
    for fetch in fetches:
        fetch.wait()
    cells = (take(of_g, g_ref) + take(of_p, p_ref) + seams).astype(jnp.bfloat16)
    for b in range(px_blocks * ch_blocks):
        i, j = divmod(b, ch_blocks)
        for face in range(local):
            at = face * count
            for which, source in enumerate((g_ref, p_ref)):
                piece = source[face, i * px : (i + 1) * px, j * ch : (j + 1) * ch]
                if ch_blocks == 1:
                    out_ref[b, at + which * px : at + (which + 1) * px] = piece
                else:
                    out_ref[b, at : at + px, which * ch : (which + 1) * ch] = piece
        out_ref[b, local * count :] = cells
        leave(out_ref, out_hbm, out_sems, b).start()
    for b in range(px_blocks * ch_blocks):
        leave(out_ref, out_hbm, out_sems, b).wait()


def pick_kernel(faces, local, count, want_ref, table_ref, out_hbm, out_ref, sems):
    for i in range(faces):
        face = want_ref[i]
        at = pl.multiple_of(lax.rem(face, local) * count, 16)
        into, row = divmod(i, local)
        out_ref[into, row * count : (row + 1) * count] = table_ref[lax.div(face, local), pl.ds(at, count)]
        if row == local - 1:
            leave(out_ref, out_hbm, sems, into).start()
    for b in range(faces // local):
        leave(out_ref, out_hbm, sems, b).wait()


def first_sum_kernel(scale, got_ref, out_ref):
    total = got_ref[0].astype(jnp.float32)
    for i in range(1, got_ref.shape[0]):
        total = total + got_ref[i].astype(jnp.float32)
    turned = (total * scale).T
    out_ref[...] = turned.reshape(out_ref.shape).astype(jnp.bfloat16)


def second_sum_kernel(got_ref, out_ref):
    total = got_ref[0].astype(jnp.float32)
    for i in range(1, got_ref.shape[0]):
        total = total + got_ref[i].astype(jnp.float32)
    _, _, per_tile, width = out_ref.shape
    lines = total.shape[1] // 9
    for tap in range(9):
        r, c = divmod(tap, 3)
        for h in range(width // lines):
            out_ref[r, c, :, h * lines : (h + 1) * lines] = total[
                h * per_tile : (h + 1) * per_tile, tap * lines : (tap + 1) * lines
            ]


def border_kernel(
    local, side, tiles, flags_ref, seams_ref, corners_ref, table_ref, g_ref, p_ref, x_ref, own_ref, wrap_ref, mine_ref, kept_ref
):
    below = flags_ref[3]
    held = local * CELLS
    cells = table_ref[:, table_ref.shape[1] - held :].reshape(table_ref.shape[0] * held, -1)
    rows, width = 4 * GAP, cells.shape[0]
    row = lax.broadcasted_iota(jnp.int32, (rows, 1), 0)
    spot, block = row % GAP, row // GAP
    of_g = block % 2 == 1
    each = jnp.where(of_g, 4, 2)
    k = spot % each
    cell = jnp.where(of_g, k, jnp.where(spot < 2 * local, 4 + k, -1))
    is_left = k * 2 >= each
    face_at = jnp.zeros((rows, 1), jnp.int32)
    for face in range(local):
        for beyond in range(2):
            if beyond:
                left, right = corners_ref[face, 2 * below], corners_ref[face, 2 * below + 1]
            else:
                left, right = seams_ref[face, 3], seams_ref[face, 1]
            here = (spot // each == face) & (block // 2 == beyond)
            face_at = jnp.where(here, jnp.where(is_left, left, right), face_at)
    index = jnp.where(cell < 0, -1, face_at * CELLS + cell)
    where = lax.broadcasted_iota(jnp.int32, (rows, width), 1) == index
    tails = jnp.dot(
        jnp.where(where, 1.0, 0.0).astype(jnp.bfloat16), cells, preferred_element_type=jnp.float32
    ).astype(jnp.bfloat16)
    full = local * side
    for which, source in enumerate((p_ref, g_ref)):
        at = which * (full + GAP)
        own_ref[at : at + full] = source[...].reshape(full, -1)
        own_ref[at + full : at + full + GAP] = tails[which * GAP : (which + 1) * GAP]
    mine_ref[:full] = g_ref[...].reshape(full, -1)
    mine_ref[full : full + GAP] = tails[GAP : 2 * GAP]
    wrap_ref[...] = tails[2 * GAP :]
    nxl, nz, nc, per_tile = tiles
    channels, half = x_ref.shape[-1], kept_ref.shape[-1]
    line = lax.broadcasted_iota(jnp.int32, (channels, nc * half), 0)
    lane = lax.broadcasted_iota(jnp.int32, (channels, nc * half), 1)
    of_core = jnp.where(lane < half, flags_ref[0], 1 - flags_ref[0])
    place = lane % half
    xl, z = place // per_tile % nxl, place // (per_tile * nxl)
    wanted = ((xl * nz + z) * nc + of_core) * per_tile + place % per_tile
    chosen = jnp.dot(
        x_ref[...].reshape(local * side, channels),
        jnp.where(line == wanted, 1.0, 0.0).astype(jnp.bfloat16),
        preferred_element_type=jnp.float32,
    ).astype(jnp.bfloat16)
    kept_ref[...] = chosen[:, :half]
    for face in range(local):
        for part in range(2):
            at = face * side + part * side // 2
            into = full + GAP + face * side // 2
            mine_ref[into : into + side // 2, part * half : (part + 1) * half] = chosen[at : at + side // 2, half:]


def copies_kernel(local, side, flags_ref, kept_ref, part_ref, out_ref, lines):
    pitch = side + 2 * GAP
    row = local * pitch
    half = kept_ref.shape[-1]
    start = local * side + GAP
    lines[...] = jnp.zeros_like(lines)
    for face in range(local):
        at = pl.multiple_of(flags_ref[0] * row + face * pitch + GAP, 16)
        lines[pl.ds(at, side), :] = kept_ref[face * side : (face + 1) * side].astype(jnp.float32)
        for part in range(2):
            at = pl.multiple_of((1 - flags_ref[0]) * row + face * pitch + GAP + part * side // 2, 16)
            lines[pl.ds(at, side // 2), :] = part_ref[
                start + face * side // 2 : start + (face + 1) * side // 2, part * half : (part + 1) * half
            ].astype(jnp.float32)
    for c in range(3):
        moved = lines[...] if c == 1 else pltpu.roll(lines[...], (1 - c) % (2 * row), 0)
        out_ref[:, c * half : (c + 1) * half] = moved.astype(jnp.bfloat16)


def send_kernel(local, side, blocks, flags_ref, own_ref, tails_ref, pieces_ref, near_ref, far_ref):
    px_blocks, ch_blocks = blocks
    px = side // px_blocks
    ch = own_ref.shape[-1] // ch_blocks
    count = px * 2 // ch_blocks
    full = local * side
    near, far = flags_ref[1], flags_ref[2]

    def put_wrap(out, start, of_g):
        for face in range(local):
            for b in range(px_blocks * ch_blocks):
                i, j = divmod(b, ch_blocks)
                piece = pieces_ref[b, face * count : (face + 1) * count]
                which = 0 if of_g else 1
                if ch_blocks == 1:
                    part = piece[which * px : (which + 1) * px]
                else:
                    part = piece[:, which * ch : (which + 1) * ch]
                at = start + face * side + i * px
                out[at : at + px, j * ch : (j + 1) * ch] = part
        tail = GAP if of_g else 0
        out[start + full : start + full + GAP, :] = tails_ref[tail : tail + GAP]

    @pl.when(near == 1)
    def _():
        put_wrap(near_ref, 0, False)
        put_wrap(near_ref, full + GAP, True)

    @pl.when(near == 0)
    def _():
        near_ref[...] = own_ref[...]

    @pl.when(far == 1)
    def _():
        put_wrap(far_ref, 0, True)

    @pl.when(far == 0)
    def _():
        far_ref[...] = own_ref[full + GAP :]


def put_row(pad, local, side, source, start, each):
    pitch = side + 2 * GAP
    full = local * side
    line = lax.broadcasted_iota(jnp.int32, (local * GAP, GAP), 0)
    lane = lax.broadcasted_iota(jnp.int32, (local * GAP, GAP), 1)
    spot, at_face = line % GAP, line // GAP
    n = each // 2
    k = jnp.where(spot < n, spot, jnp.where(spot >= GAP - n, spot - (GAP - each), GAP))
    spread = jnp.where(lane == k + each * at_face, 1.0, 0.0)
    spread = jnp.where(k < each, spread, 0.0).astype(jnp.bfloat16)
    tails = source[start + full : start + full + GAP, :]
    borders = jnp.dot(spread, tails, preferred_element_type=jnp.float32).astype(jnp.bfloat16)
    for face in range(local):
        at = face * pitch
        border = borders[face * GAP : (face + 1) * GAP]
        pad[at : at + GAP, :] = border
        pad[at + GAP : at + GAP + side, :] = source[start + face * side : start + (face + 1) * side, :]
        pad[at + GAP + side : at + pitch, :] = border


def row_taps(pairs, row):
    sums = []
    for c in range(3):
        total = None
        for rows, weight in pairs:
            term = lax.dot_general(
                rows, weight(c), (((1,), (1,)), ((), ())), preferred_element_type=jnp.float32
            )
            total = term if total is None else total + term
        sums.append(total)
    return pltpu.roll(sums[2], 1, 0) + sums[1] + pltpu.roll(sums[0], row - 1, 0)


def silu_slope(pre):
    pre = pre.astype(jnp.float32)
    logistic = jax.nn.sigmoid(pre)
    return logistic * (1.0 + pre * (1.0 - logistic))


def near_half_kernel(local, side, flags_ref, own_ref, part_ref, weight_ref, hidden_ref, slope_ref, own_pad, part_pad, pre_pad):
    row = own_pad.shape[0]
    toward = 2 * flags_ref[0]
    second = local * side + GAP
    put_row(own_pad, local, side, own_ref, second, 4)
    put_row(part_pad, local, side, part_ref, 0, 4)
    put_row(pre_pad, local, side, own_ref, 0, 2)
    own, part = own_pad[...], part_pad[...]
    hidden_ref[:row] = row_taps([(own, lambda c: weight_ref[toward, c])], row)
    hidden_ref[row:] = row_taps([(own, lambda c: weight_ref[1, c]), (part, lambda c: weight_ref[toward, c])], row)
    slope_ref[...] = silu_slope(pre_pad[...])


def grad_pre_kernel(local, side, flags_ref, near_ref, far_ref, hidden_ref, slope_ref, weight_ref, out_ref, near_pad, far_pad, pre_pad):
    row = near_pad.shape[0]
    core = flags_ref[0]
    away = 2 - 2 * core
    second = local * side + GAP
    put_row(near_pad, local, side, near_ref, second, 4)
    put_row(far_pad, local, side, far_ref, 0, 4)
    put_row(pre_pad, local, side, near_ref, 0, 2)
    near, far = near_pad[...], far_pad[...]
    outer = hidden_ref[:row] + row_taps(
        [(far, lambda c: weight_ref[away, c]), (near, lambda c: weight_ref[1, c])], row
    )
    inner = hidden_ref[row:] + row_taps([(near, lambda c: weight_ref[away, c])], row)
    outer = (outer * silu_slope(pre_pad[...])).astype(jnp.bfloat16)
    inner = (inner * slope_ref[...]).astype(jnp.bfloat16)
    out_ref[pl.ds(pl.multiple_of(core * row, 16), row), :] = outer
    out_ref[pl.ds(pl.multiple_of((1 - core) * row, 16), row), :] = inner


def conv_rows(pad, start, row, weight_ref):
    sums = []
    for c in range(3):
        total = None
        for r in range(3):
            at = start + (2 - r) * row
            rows = pad[pl.ds(at if isinstance(at, int) else pl.multiple_of(at, 16), row), :]
            term = lax.dot_general(
                rows, weight_ref[r, c], (((1,), (1,)), ((), ())), preferred_element_type=jnp.float32
            )
            total = term if total is None else total + term
        sums.append(total)
    return pltpu.roll(sums[2], 1, 0) + sums[1] + pltpu.roll(sums[0], row - 1, 0)


def four_rows(rows4, core, row, pre_ref, swapped_ref):
    rows4[pl.ds(pl.multiple_of(core * 2 * row, 16), 2 * row), :] = pre_ref[...]
    rows4[pl.ds(pl.multiple_of((1 - core) * 2 * row, 16), 2 * row), :] = swapped_ref[...]


def grad_input_kernel(local, side, flags_ref, pre_ref, swapped_ref, own_ref, weight_ref, out_ref, rows4):
    pitch = side + 2 * GAP
    row = local * pitch
    core = flags_ref[0]
    four_rows(rows4, core, row, pre_ref, swapped_ref)
    grad = conv_rows(rows4, core * row, row, weight_ref)
    for face in range(local):
        at = face * pitch + GAP
        own = own_ref[face].astype(jnp.float32)
        out_ref[face] = (own + grad[at : at + side, :]).astype(jnp.bfloat16)


def over_pixels(left, right):
    return lax.dot_general(left, right, (((0,), (0,)), ((), ())), preferred_element_type=jnp.float32)


def emit(out_ref, start, terms, nxl, per_tile):
    dests, half = out_ref.shape[0], out_ref.shape[2]
    lines = terms.shape[0] // dests
    for c in range(3):
        turned = terms[:, c * half : (c + 1) * half]
        at = pl.multiple_of(start + c * lines, 16)
        if nxl == 1:
            for d in range(dests):
                out_ref[d, pl.ds(at, lines)] = turned[d * lines : (d + 1) * lines, :].astype(jnp.bfloat16)
            continue
        split = turned.reshape(dests // 2, 2, lines, half)
        left = split[:, 0].reshape(-1, half)
        right = split[:, 1].reshape(-1, half)
        low = lax.broadcasted_iota(jnp.int32, left.shape, 1) % (2 * per_tile) < per_tile
        ones = (
            jnp.where(low, left, pltpu.roll(right, per_tile, 1)),
            jnp.where(low, pltpu.roll(left, half - per_tile, 1), right),
        )
        for xl, one in enumerate(ones):
            for d in range(dests // 2):
                out_ref[2 * d + xl, pl.ds(at, lines)] = one[d * lines : (d + 1) * lines, :].astype(jnp.bfloat16)


def first_half_kernel(row, nxl, per_tile, flags_ref, x_ref, pre_ref, out_ref, middle_ref):
    core = flags_ref[0]
    x_rows = pl.ds(pl.multiple_of(core * row, 16), row)
    rows = pl.ds(pl.multiple_of((1 - core) * row, 16), row)
    middle_ref[...] = over_pixels(pre_ref[rows, :], x_ref[x_rows, :])
    emit(out_ref, 0, over_pixels(pre_ref[...], x_ref[...]), nxl, per_tile)


def grad_first_kernel(row, nxl, per_tile, flags_ref, x_ref, swapped_ref, done_ref, middle_ref, out_ref):
    core = flags_ref[0]
    x_rows = pl.ds(pl.multiple_of((1 - core) * row, 16), row)
    rows = pl.ds(pl.multiple_of(core * row, 16), row)
    count = done_ref.shape[1]
    emit(
        out_ref,
        count,
        middle_ref[...] + over_pixels(swapped_ref[rows, :], x_ref[x_rows, :]),
        nxl,
        per_tile,
    )
    emit(out_ref, core * 2 * count, over_pixels(swapped_ref[...], x_ref[...]), nxl, per_tile)
    at = pl.multiple_of((1 - core) * 2 * count, 16)
    for d in range(done_ref.shape[0]):
        out_ref[d, pl.ds(at, count)] = done_ref[d]


def kernel(body, out_shape, inputs, smem=0, scratch=(), name=None, flops=0, nbytes=2**20, exps=0, hbm=0, vmem=VMEM, out_hbm=False):
    many = isinstance(out_shape, tuple)
    spots = [pl.BlockSpec(memory_space=pltpu.HBM)] * hbm + whole(len(inputs) - smem - hbm)
    return pl.pallas_call(
        body,
        out_shape=out_shape,
        in_specs=[pl.BlockSpec(memory_space=pltpu.SMEM)] * smem + spots,
        out_specs=tuple(whole(len(out_shape))) if many else pl.BlockSpec(memory_space=pltpu.HBM) if out_hbm else whole(1)[0],
        scratch_shapes=scratch,
        compiler_params=pltpu.CompilerParams(vmem_limit_bytes=vmem),
        cost_estimate=pl.CostEstimate(flops=flops, bytes_accessed=nbytes, transcendentals=exps),
        name=name,
    )(*inputs)


def on_device(sizes, saved_input, saved_pre, cotangent, first_weight, second_weight, seams, corners):
    nxh, ny, nxl, nz, nc = sizes
    nface, ntile, nchip = nxh * ny, nxl * nz * nc, nxl * nz
    x, p, g = saved_input[0, :, 0], saved_pre[0, :, 0], cotangent[0, :, 0]
    local, side, channels = x.shape
    faces = nface * local
    row = local * (side + 2 * GAP)
    bf = jnp.bfloat16
    shape = jax.ShapeDtypeStruct
    core = lax.axis_index("c")
    tile = lax.axis_index(TILE)
    top = tile >= ntile // 2
    near_wraps = (tile == 0) | (tile == ntile - 1)
    far_wraps = (tile == 1) | (tile == ntile - 2)
    marks = [core, *(flag.astype(jnp.int32) for flag in (near_wraps, far_wraps, ~top))]

    px_blocks = 4
    ch_blocks = nface // px_blocks
    px = side // px_blocks
    count = px * 2 // ch_blocks
    sent = kernel(
        functools.partial(pack_kernel, local, side, (px_blocks, ch_blocks)),
        shape((nface, local * (count + CELLS), channels), bf),
        (seams, g, p),
        1,
        (
            pltpu.VMEM((local, side, channels), bf),
            pltpu.VMEM((local, side, channels), bf),
            pltpu.VMEM((nface, local * (count + CELLS), channels), bf),
            pltpu.SemaphoreType.DMA((2, local)),
            pltpu.SemaphoreType.DMA((nface,)),
        ),
        "pack",
        hbm=2,
        vmem=None,
        out_hbm=True,
    )
    swap = lambda a: lax.ppermute(a, "c", [(0, 1), (1, 0)])
    sent, marks, top = lax.optimization_barrier((sent, marks, top))
    table, marks = lax.optimization_barrier((lax.all_to_all(sent, FACE, 0, 0, tiled=True), marks))
    flags = jnp.stack(marks)

    cells = table[:, local * count :].reshape(faces, CELLS, channels)
    all_seams = cells[:, SEAM_AT, :4].astype(jnp.int32)
    want = jnp.where(top, all_seams[:, 0], all_seams[:, 2])
    picked = kernel(
        functools.partial(pick_kernel, faces, local, count),
        shape((nface, local * count, channels), bf),
        (want, table),
        1,
        (pltpu.VMEM((nface, local * count, channels), bf), pltpu.SemaphoreType.DMA((nface,))),
        "pick",
        out_hbm=True,
    )
    picked, table = lax.optimization_barrier((picked, table))
    wrapped = lax.all_to_all(picked, FACE, 0, 0, tiled=True)

    half = channels // nc
    per_tile = channels // ntile
    own, tails, mine, kept = kernel(
        functools.partial(border_kernel, local, side, (nxl, nz, nc, per_tile)),
        (
            shape((2 * (local * side + GAP), channels), bf),
            shape((2 * GAP, channels), bf),
            shape((local * side + GAP + local * side // 2, channels), bf),
            shape((local * side, half), bf),
        ),
        (flags, seams, corners, table, g, p, x),
        3,
        name="border",
    )
    wrapped, part = lax.optimization_barrier((wrapped, swap(mine)))
    near, far = kernel(
        functools.partial(send_kernel, local, side, (px_blocks, ch_blocks)),
        (shape(own.shape, bf), shape((own.shape[0] // 2, channels), bf)),
        (flags, own, tails, wrapped),
        1,
        name="send",
    )

    pairs = lambda step: [((t + step if t % 2 else t - step) % ntile, t) for t in range(ntile)]
    near = lax.ppermute(near, TILE, pairs(1))
    far = lax.ppermute(far, TILE, pairs(2))
    x_copies = kernel(
        functools.partial(copies_kernel, local, side),
        shape((2 * row, 3 * half), bf),
        (flags, kept, part),
        1,
        (pltpu.VMEM((2 * row, half), jnp.float32),),
        "copies",
    )

    pads = tuple(pltpu.VMEM((row, channels), bf) for _ in range(3))
    hidden, slope = kernel(
        functools.partial(near_half_kernel, local, side),
        (shape((2 * row, channels), jnp.float32), shape((row, channels), jnp.float32)),
        (flags, own, part, second_weight),
        1,
        pads,
        "near_half",
        2 * 9 * row * channels**2,
        2 * 2**20,
        row * channels,
    )
    near, far, x_copies, hidden, slope = lax.optimization_barrier((near, far, x_copies, hidden, slope))
    grad_pre = kernel(
        functools.partial(grad_pre_kernel, local, side),
        shape((2 * row, channels), bf),
        (flags, near, far, hidden, slope, second_weight),
        1,
        pads,
        "grad_pre",
        2 * 9 * row * channels**2,
        4 * 2**20,
        row * channels,
    )
    swapped = swap(grad_pre)

    rows4 = (pltpu.VMEM((4 * row, channels), bf),)
    width = channels // nface
    lines = width // nxl
    done, middle = kernel(
        functools.partial(first_half_kernel, row, nxl, per_tile),
        (shape((nface * nxl, 3 * lines, half), bf), shape((channels, 3 * half), jnp.float32)),
        (flags, x_copies, grad_pre),
        1,
        name="first_half",
    )
    swapped, done, middle = lax.optimization_barrier((swapped, done, middle))
    parts = kernel(
        functools.partial(grad_first_kernel, row, nxl, per_tile),
        shape((nface * nxl, 9 * lines, half), bf),
        (flags, x_copies, swapped, done, middle),
        1,
        name="grad_first",
        flops=2 * 9 * half * row * channels,
    )
    grad_input = kernel(
        functools.partial(grad_input_kernel, local, side),
        shape((local, side, channels), bf),
        (flags, grad_pre, swapped, g, first_weight),
        1,
        rows4,
        "grad_input",
        2 * 9 * row * channels**2,
        2 * 2**20,
    )
    scale_factor = 1.0 / math.sqrt(faces * ntile * side)
    got = lax.all_to_all(parts, FACE + ("xl",), 0, 0, tiled=True)
    total = kernel(
        functools.partial(first_sum_kernel, scale_factor),
        shape((nz, nxl * per_tile, 9 * lines), bf),
        (got,),
        name="first_sum",
    )
    got = lax.all_to_all(total, "z", 0, 0, tiled=True)
    first_out = kernel(second_sum_kernel, shape((3, 3, per_tile, width), jnp.float32), (got,), name="second_sum")
    return grad_input.reshape(saved_input.shape), first_out


def solution(mesh, sizes=(2, 4, 2, 16, 2)):
    fine = Mesh(mesh.devices.reshape(sizes), FACE + TILE)
    field = P(None, FACE, TILE, None, None)
    return jax.shard_map(
        functools.partial(on_device, sizes),
        mesh=fine,
        in_specs=(field, field, field, P(), P(), P(FACE, None), P(FACE, None)),
        out_specs=(field, P(None, None, TILE, FACE)),
        check_vma=False,
    )
```
